32 devices in a mesh: dp: 4 (over z), seq: 8 (over y, x, core).
Axes of the slice: x: 2, y: 2, z: 4, core: 2. Of those that a mesh axis runs over, the one named last changes fastest.
Arguments:
- layer_input: bfloat16 [4096, 2560], P(('dp', 'seq')), may hold values from -6 to 6
- positions: int32 [4096], P(('dp', 'seq')), may hold values from 0 to 1023, as said below
- attn_gain: bfloat16 [2560], P(('dp', 'seq')), may hold values from 0.5 to 1.5
- query_down: bfloat16 [2560, 768], P(('dp', 'seq')), may hold values from -0.125 to 0.125
- query_gain: bfloat16 [768], P(('dp', 'seq')), may hold values from 0.5 to 1.5
- query_up: bfloat16 [768, 3840], P(None, ('dp', 'seq')), may hold values from -0.4375 to 0.4375
- latent_down: bfloat16 [2560, 288], P(('dp', 'seq')), may hold values from -0.125 to 0.125
- latent_gain: bfloat16 [256], P(('dp', 'seq')), may hold values from 0.5 to 1.5
- latent_up: bfloat16 [256, 5120], P(None, ('dp', 'seq')), may hold values from -0.375 to 0.375
- output_proj: bfloat16 [2560, 2560], P(('dp', 'seq')), may hold values from -3 to 3
- ffn_gain: bfloat16 [2560], P(('dp', 'seq')), may hold values from 0.5 to 1.5
- ffn_gate: bfloat16 [2560, 6400], P(None, ('dp', 'seq')), may hold values from -0.125 to 0.125
- ffn_up: bfloat16 [2560, 6400], P(None, ('dp', 'seq')), may hold values from -0.125 to 0.125
- ffn_down: bfloat16 [6400, 2560], P(('dp', 'seq')), may hold values from -0.75 to 0.75
- cotangent: bfloat16 [4096, 2560], P(('dp', 'seq')), may hold values from -6 to 6
Outputs:
- layer_output: bfloat16 [4096, 2560], P(('dp', 'seq'))
- input_grad: float32 [4096, 2560], P(('dp', 'seq'))
- grad_attn_gain: float32 [2560], P(('dp', 'seq'))
- grad_query_down: float32 [2560, 768], P(('dp', 'seq'))
- grad_query_gain: float32 [768], P(('dp', 'seq'))
- grad_query_up: float32 [768, 3840], P(None, ('dp', 'seq'))
- grad_latent_down: float32 [2560, 288], P(('dp', 'seq'))
- grad_latent_gain: float32 [256], P(('dp', 'seq'))
- grad_latent_up: float32 [256, 5120], P(None, ('dp', 'seq'))
- grad_output_proj: float32 [2560, 2560], P(('dp', 'seq'))
- grad_ffn_gain: float32 [2560], P(('dp', 'seq'))
- grad_ffn_gate: float32 [2560, 6400], P(None, ('dp', 'seq'))
- grad_ffn_up: float32 [2560, 6400], P(None, ('dp', 'seq'))
- grad_ffn_down: float32 [6400, 2560], P(('dp', 'seq'))
The draws below stay inside these ranges and needn't reach their ends.
Inputs may be any that keep to these rules, and one draw needn't show every extreme that they name: Each sequence of 1024 tokens is a pack of documents: positions count 0, 1, 2, ... from each document's first token, the first token of every sequence starts a document, and one sequence, drawn from the seed, is a single document.
All inputs are finite; a program needn't handle non-finite values.
Results may differ from the reference program's by a relative error of at most 0.02.
Values may be sent and summed in bfloat16 or wider, within the bound.
No kernel may reach another device: no remote copies, remote signals or barrier semaphores. Data moves between devices by JAX's collectives and lax.ppermute only.
A program may use at most 768 MiB of HBM per device.

```python
import math
from functools import partial
import jax
import jax.numpy as jnp
from jax import lax

D = 2560
Q_RANK = 768
KV_RANK = 256
HEADS = 40
NOPE = 64
ROPE = 32
VDIM = 64
FF = 6400
TOK_DEV = 128
LENGTH = 1024
SEQS = 4
TOKENS = 4096
N_SEQ = 8


def draw_positions(key, part):
    key = jax.random.fold_in(key, 7)
    first_key, second_key = jax.random.split(key)
    doc_marks = jax.random.randint(first_key, (SEQS, LENGTH), 0, max(LENGTH // 8, 2)) == 0
    whole_row = jax.random.randint(second_key, (), 0, SEQS)
    token_index = jnp.arange(LENGTH, dtype=jnp.int32)
    seq_rows = jnp.arange(SEQS, dtype=jnp.int32)
    doc_marks = doc_marks & (seq_rows[:, None] != whole_row) | (token_index[None, :] == 0)
    starts = lax.cummax(jnp.where(doc_marks, token_index[None, :], 0), axis=1)
    return (token_index[None, :] - starts).reshape(TOKENS).astype(jnp.int32)


def block_scale(rng, extent, cuts, least, largest):
    level = 1.0
    for dim, parts in cuts:
        heights = jax.random.uniform(jax.random.fold_in(jax.random.fold_in(rng, 6), dim), (parts,), jnp.float32, least / len(cuts), largest / len(cuts))
        level = level * jnp.repeat(jnp.exp(heights), extent[dim] // parts).reshape((-1,) + (1,) * (len(extent) - 1 - dim))
    return level


def noise(stream_key, extent, scale, bound, shards=(), kind=jnp.bfloat16):
    loudness = block_scale(stream_key, extent, shards, -0.22, 0.18) if shards else 1.0
    array = jax.random.normal(stream_key, extent, jnp.float32) * scale * loudness
    return jnp.minimum(jnp.maximum(array, -bound), bound).astype(kind)


def setup_inputs(seed: int = 0) -> dict:
    streams_of = jax.random.split(jax.random.key(seed), 16)
    return {
        "layer_input": noise(streams_of[0], (TOKENS, D), 1.0, 6.0, ((0, 32),)),
        "positions": draw_positions(jax.random.fold_in(streams_of[15], 71), 0),
        "attn_gain": jnp.clip(1.0 + 0.1 * jax.random.normal(streams_of[2], (D,), jnp.float32), 0.5, 1.5).astype(jnp.bfloat16),
        "query_down": noise(streams_of[3], (D, Q_RANK), D ** -0.5, 0.125, ((0, 32),)),
        "query_gain": jnp.clip(1.0 + 0.1 * jax.random.normal(streams_of[4], (Q_RANK,), jnp.float32), 0.5, 1.5).astype(jnp.bfloat16),
        "query_up": noise(streams_of[5], (Q_RANK, HEADS * (NOPE + ROPE)), (Q_RANK // 4) ** -0.5, 0.4375, ((1, 32),)),
        "latent_down": noise(streams_of[6], (D, KV_RANK + ROPE), D ** -0.5, 0.125, ((0, 32),)),
        "latent_gain": jnp.clip(1.0 + 0.1 * jax.random.normal(streams_of[7], (KV_RANK,), jnp.float32), 0.5, 1.5).astype(jnp.bfloat16),
        "latent_up": noise(streams_of[8], (KV_RANK, HEADS * (NOPE + VDIM)), KV_RANK ** -0.5, 0.375, ((1, 32),)),
        "output_proj": noise(streams_of[9], (HEADS * VDIM, D), 4 ** -0.5, 3.0, ((0, 32),)),
        "ffn_gain": jnp.clip(1.0 + 0.1 * jax.random.normal(streams_of[10], (D,), jnp.float32), 0.5, 1.5).astype(jnp.bfloat16),
        "ffn_gate": noise(streams_of[11], (D, FF), D ** -0.5, 0.125, ((1, 32),)),
        "ffn_up": noise(streams_of[12], (D, FF), D ** -0.5, 0.125, ((1, 32),)),
        "ffn_down": noise(streams_of[13], (FF, D), 64 ** -0.5, 0.75, ((0, 32),)),
        "cotangent": noise(streams_of[14], (TOKENS, D), 1.0, 6.0, ((0, 32),)),
    }


EPSILON = 1e-05
RESIDUAL_SCALE = 1.4 / math.sqrt(62.0)
HIGHEST = lax.Precision.HIGHEST

@jax.custom_vjp
def low(v):
    return lax.optimization_barrier(v.astype(jnp.bfloat16)).astype(jnp.float32)

@jax.custom_vjp
def low_back(v):
    return v

def low_keep(v):
    return (low(v), None)

def low_pass(kept, grad):
    return (grad,)

def back_keep(v):
    return (v, None)

def back_low(kept, grad):
    return (low(grad),)
low.defvjp(low_keep, low_pass)
low_back.defvjp(back_keep, back_low)

def matmul(left, right):
    return jnp.dot(left, right, precision=HIGHEST)

def rms_scaled(values, scale_gain):
    return values * lax.rsqrt(lax.optimization_barrier(jnp.mean(values * values, axis=-1, keepdims=True)) + EPSILON) * scale_gain

def rotary_tables(positions):
    half_width = ROPE // 2
    inverse = 10000.0 ** (-2.0 * jnp.arange(half_width, dtype=jnp.float32) / ROPE)
    angles = positions.astype(jnp.float32)[:, None] * inverse[None, :]
    cos_table = jnp.cos(angles)
    sin_table = jnp.sin(angles)
    return (jnp.concatenate([cos_table, cos_table], -1), jnp.concatenate([sin_table, sin_table], -1))

def rotate(values, cos_table, sin_table):
    half_width = values.shape[-1] // 2
    turned = jnp.concatenate([-values[..., half_width:], values[..., :half_width]], -1)
    return values * cos_table + turned * sin_table

def attend(block_index, query_block, latent_keys, rotary_keys, latent_up):
    key_count = latent_keys.shape[0]
    score_scale = (NOPE + ROPE) ** (-0.5)
    keys_values = low(low_back(matmul(latent_keys, latent_up))).reshape(key_count, HEADS, NOPE + VDIM)
    scores = jnp.einsum('thd,lhd->htl', query_block[..., :NOPE], keys_values[..., :NOPE], precision=HIGHEST)
    scores = scores + jnp.einsum('thr,lr->htl', query_block[..., NOPE:], rotary_keys, precision=HIGHEST)
    scores = low_back(scores * score_scale)
    query_rows = block_index * TOK_DEV + jnp.arange(TOK_DEV)
    allowed = query_rows[:, None] >= jnp.arange(key_count)[None, :]
    scores = jnp.where(allowed[None], scores, -1e+30)
    row_peak = lax.optimization_barrier(jnp.max(scores, axis=-1, keepdims=True))
    exponent_terms = jnp.exp(scores - row_peak)
    probabilities = low(exponent_terms / lax.optimization_barrier(jnp.sum(exponent_terms, axis=-1, keepdims=True)))
    attended = jnp.einsum('htl,lhv->thv', probabilities, keys_values[..., NOPE:], precision=HIGHEST)
    return low(low_back(attended)).reshape(TOK_DEV, HEADS * VDIM)

def layer_forward(inputs, weights, cos_table, sin_table):
    attn_gain, query_down, query_gain, query_up, latent_down, latent_gain, latent_up, output_proj, ffn_gain, ffn_gate, ffn_up, ffn_down = weights
    normed = low(rms_scaled(inputs, attn_gain))
    query_latent = low_back(matmul(normed, query_down))
    query_normed = low(rms_scaled(query_latent, query_gain))
    projected = low_back(matmul(query_normed, query_up)).reshape(LENGTH, HEADS, NOPE + ROPE)
    queries = low(jnp.concatenate([projected[..., :NOPE], rotate(projected[..., NOPE:], cos_table[:, None, :], sin_table[:, None, :])], -1))
    compressed = low_back(matmul(normed, latent_down))
    latent = low(rms_scaled(compressed[:, :KV_RANK], latent_gain))
    rotary_keys = low(rotate(compressed[:, KV_RANK:], cos_table, sin_table))
    pieces = []
    for block_index in range(N_SEQ):
        stop_row = (block_index + 1) * TOK_DEV
        pieces.append(jax.checkpoint(partial(attend, block_index))(queries[block_index * TOK_DEV:stop_row], latent[:stop_row], rotary_keys[:stop_row], latent_up))
    attended = jnp.concatenate(pieces, 0)
    branch = low_back(matmul(attended, output_proj))
    middle = inputs + RESIDUAL_SCALE * branch
    normed_two = low(rms_scaled(middle, ffn_gain))
    gate_values = low_back(matmul(normed_two, ffn_gate))
    upward = low_back(matmul(normed_two, ffn_up))
    activated = low(gate_values * jax.nn.sigmoid(gate_values) * upward)
    return middle + RESIDUAL_SCALE * low_back(matmul(activated, ffn_down))

def reference(layer_input, positions, attn_gain, query_down, query_gain, query_up, latent_down, latent_gain, latent_up, output_proj, ffn_gain, ffn_gate, ffn_up, ffn_down, cotangent):
    weights = tuple((matrix.astype(jnp.float32) for matrix in (attn_gain, query_down, query_gain, query_up, latent_down, latent_gain, latent_up, output_proj, ffn_gain, ffn_gate, ffn_up, ffn_down)))
    inputs = layer_input.astype(jnp.float32).reshape(SEQS, LENGTH, D)
    seq_positions = positions.reshape(SEQS, LENGTH)
    seq_cotangent = cotangent.astype(jnp.float32).reshape(SEQS, LENGTH, D)

    def one_sequence(totals, sliced):
        seq_input, seq_place, seq_grad = sliced
        cos_table, sin_table = rotary_tables(seq_place)
        result, pullback = jax.vjp(lambda values, params: layer_forward(values, params, cos_table, sin_table), seq_input, weights)
        input_grads, weight_grads = pullback(seq_grad)
        return (jax.tree.map(jnp.add, totals, weight_grads), (result, input_grads))
    zero_grads = tuple((jnp.zeros_like(matrix) for matrix in weights))
    totals, (results, input_grads) = lax.scan(one_sequence, zero_grads, (inputs, seq_positions, seq_cotangent))
    return (results.reshape(TOKENS, D).astype(jnp.bfloat16), input_grads.reshape(TOKENS, D), totals[0], totals[1], totals[2], totals[3], totals[4], totals[5], totals[6], totals[7], totals[8], totals[9], totals[10], totals[11])
```

```python
import math

import jax
import jax.numpy as jnp
from jax import lax
from jax.experimental import pallas as pl
from jax.experimental.pallas import tpu as pltpu
from jax.sharding import PartitionSpec as P

KV_RANK = 256
HEADS = 40
NOPE = 64
ROPE = 32
VDIM = 64


EPSILON = 1e-05
RESIDUAL_SCALE = 1.4 / math.sqrt(62.0)
F32 = jnp.float32
BF16 = jnp.bfloat16


def norm_parts(values):
    inverse = lax.rsqrt(jnp.mean(values * values, axis=-1, keepdims=True) + EPSILON)
    return (values * inverse, inverse)


def norm_back(grad_scaled, normalized, inverse, scale_gain):
    gain_grad = jnp.sum(grad_scaled * normalized, axis=0)
    grad_normal = grad_scaled * scale_gain
    values_grad = inverse * (
        grad_normal - normalized * jnp.mean(grad_normal * normalized, axis=-1, keepdims=True)
    )
    return (values_grad, gain_grad)


def rotary_tables(positions):
    half_width = ROPE // 2
    inverse = 10000.0 ** (-2.0 * jnp.arange(half_width, dtype=F32) / ROPE)
    angles = positions.astype(F32)[:, None] * inverse[None, :]
    cos_table = jnp.cos(angles)
    sin_table = jnp.sin(angles)
    return (
        jnp.concatenate([cos_table, cos_table], -1),
        jnp.concatenate([sin_table, sin_table], -1),
    )


def rotate(values, cos_table, sin_table):
    half_width = values.shape[-1] // 2
    turned = jnp.concatenate([-values[..., half_width:], values[..., :half_width]], -1)
    return values * cos_table + turned * sin_table


def rotate_back(grads, cos_table, sin_table):
    half_width = grads.shape[-1] // 2
    scaled = grads * sin_table
    return grads * cos_table + jnp.concatenate(
        [scaled[..., half_width:], -scaled[..., :half_width]], -1
    )


def score_block(query_block, keys_values, rotary_all, allowed):
    score_scale = (NOPE + ROPE) ** (-0.5)
    scores = jnp.einsum(
        "thd,lhd->htl",
        query_block[..., :NOPE],
        keys_values[..., :NOPE],
        preferred_element_type=F32,
    )
    scores = scores + jnp.einsum(
        "thr,lr->htl", query_block[..., NOPE:], rotary_all, preferred_element_type=F32
    )
    return jnp.where(allowed[None], scores * score_scale, -1e30)


def dot(spec, left, right):
    return jnp.einsum(spec, left, right, preferred_element_type=F32)


def shift(value, axis, count, step):
    return lax.ppermute(value, axis, [(i, (i + step) % count) for i in range(count)])


def gather_dp(value, count):
    return [value] + [shift(value, "dp", count, k) for k in range(1, count)]


def scatter_dp(parts, count):
    total = parts[0].astype(F32)
    for k in range(1, count):
        total = total + shift(parts[k].astype(BF16), "dp", count, -k).astype(F32)
    return total


def gather_all(rows, dp_count):
    by_place = jnp.stack(gather_dp(rows, dp_count))
    place = lax.axis_index("dp")
    order = (place - jnp.arange(dp_count)) % dp_count
    absolute = jnp.take(by_place, order, axis=0)
    whole = lax.all_gather(absolute, "seq", axis=1, tiled=True)
    return whole.reshape(-1, rows.shape[1])


def scatter_all(grads, dp_count):
    blocks = grads.astype(BF16).reshape(dp_count, -1, grads.shape[1])
    own_seq = lax.psum_scatter(blocks, "seq", scatter_dimension=1, tiled=True)
    place = lax.axis_index("dp")
    parts = [
        lax.dynamic_index_in_dim(own_seq, (place - k) % dp_count, 0, keepdims=False)
        for k in range(dp_count)
    ]
    return scatter_dp(parts, dp_count)


def per_device_general(
    dp_count,
    layer_input,
    positions,
    attn_gain,
    query_down,
    query_gain,
    query_up,
    latent_down,
    latent_gain,
    latent_up,
    output_proj,
    ffn_gain,
    ffn_gate,
    ffn_up,
    ffn_down,
    cotangent,
):
    token_count, width = layer_input.shape
    query_rank = query_down.shape[1]
    own_rows = query_down.shape[0]
    score_scale = (NOPE + ROPE) ** (-0.5)

    def column(gain):
        return jnp.pad(gain, (0, own_rows - gain.shape[0]))[:, None]

    down_width = query_rank + KV_RANK + ROPE
    pad_width = -(down_width + 4) % 128
    packed = jnp.concatenate(
        [
            query_down,
            latent_down,
            column(attn_gain),
            column(ffn_gain),
            column(query_gain),
            column(latent_gain),
            jnp.zeros((own_rows, pad_width), BF16),
        ],
        1,
    )
    packed_full = gather_all(packed, dp_count)
    down_full = packed_full[:, :down_width]
    gains = packed_full[:, down_width : down_width + 4].T.astype(F32)
    attn_gain_full = gains[0]
    ffn_gain_full = gains[1]

    def short_gain(row, own):
        return row.reshape(-1, own_rows)[:, : own.shape[0]].reshape(-1)

    query_gain_full = short_gain(gains[2], query_gain)
    latent_gain_full = short_gain(gains[3], latent_gain)

    query_up_full = gather_all(query_up.T, dp_count)
    latent_up_full = gather_all(latent_up.T, dp_count)
    proj_full = gather_all(output_proj, dp_count)
    gate_full = lax.all_gather(ffn_gate.T, "seq", axis=0, tiled=True)
    upward_full = lax.all_gather(ffn_up.T, "seq", axis=0, tiled=True)
    ffn_down_full = lax.all_gather(ffn_down, "seq", axis=0, tiled=True)

    grad_out = cotangent.astype(F32)
    grad_two = (RESIDUAL_SCALE * grad_out).astype(BF16)
    grad_rows = jnp.concatenate(gather_dp(grad_two, dp_count))

    inputs = layer_input.astype(F32)
    cos_table, sin_table = rotary_tables(positions)
    normal_one, inverse_one = norm_parts(inputs)
    normed = (normal_one * attn_gain_full).astype(BF16)
    down_out = jnp.dot(normed, down_full, preferred_element_type=F32)
    query_latent = down_out[:, :query_rank]
    compressed = down_out[:, query_rank:]
    normal_latent, inverse_latent = norm_parts(compressed[:, :KV_RANK])
    latent = (normal_latent * latent_gain_full).astype(BF16)
    rotary_keys = rotate(compressed[:, KV_RANK:], cos_table, sin_table).astype(BF16)
    keys_all = lax.all_gather(
        jnp.concatenate([latent, rotary_keys], -1), "seq", axis=0, tiled=True
    )
    latent_all = keys_all[:, :KV_RANK]
    rotary_all = keys_all[:, KV_RANK:]
    normal_query, inverse_query = norm_parts(query_latent)
    query_normed = (normal_query * query_gain_full).astype(BF16)
    projected = dot("tq,kq->tk", query_normed, query_up_full).reshape(
        token_count, HEADS, NOPE + ROPE
    )
    queries = jnp.concatenate(
        [
            projected[..., :NOPE],
            rotate(projected[..., NOPE:], cos_table[:, None, :], sin_table[:, None, :]),
        ],
        -1,
    ).astype(BF16)
    key_count = latent_all.shape[0]
    head_group = math.gcd(HEADS, 8)
    group_count = HEADS // head_group
    first_row = lax.axis_index("seq") * token_count
    allowed = (first_row + jnp.arange(token_count))[:, None] >= jnp.arange(key_count)[None, :]
    up_grouped = latent_up_full.reshape(group_count, head_group * (NOPE + VDIM), KV_RANK)
    query_grouped = queries.reshape(token_count, group_count, head_group, NOPE + ROPE).transpose(
        1, 0, 2, 3
    )

    def forward_group(operands):
        query_block, up_block = operands
        keys_values = dot("lc,kc->lk", latent_all, up_block).astype(BF16)
        keys_values = keys_values.reshape(key_count, head_group, NOPE + VDIM)
        scores = score_block(query_block, keys_values, rotary_all, allowed)
        row_peak = jnp.max(scores, axis=-1, keepdims=True)
        exponent_terms = jnp.exp(scores - row_peak)
        row_totals = jnp.sum(exponent_terms, axis=-1, keepdims=True)
        probabilities = (exponent_terms / row_totals).astype(BF16)
        attended_block = dot("htl,lhv->thv", probabilities, keys_values[..., NOPE:])
        return (keys_values, attended_block, (row_peak + jnp.log(row_totals))[..., 0])

    kept_values, attended_grouped, log_totals = lax.map(forward_group, (query_grouped, up_grouped))
    attended_low = (
        attended_grouped.transpose(1, 0, 2, 3).reshape(token_count, HEADS * VDIM).astype(BF16)
    )
    branch = jnp.dot(attended_low, proj_full, preferred_element_type=F32)
    middle = inputs + RESIDUAL_SCALE * branch
    normal_two, inverse_two = norm_parts(middle)
    normed_two = (normal_two * ffn_gain_full).astype(BF16)

    normed_rows = jnp.concatenate(gather_dp(normed_two, dp_count))
    gate_values = dot("td,fd->tf", normed_rows, gate_full)
    upward = dot("td,fd->tf", normed_rows, upward_full)
    grad_activated = dot("td,fd->tf", grad_rows, ffn_down_full)
    sigmoid_gate = jax.nn.sigmoid(gate_values)
    activated = (gate_values * sigmoid_gate * upward).astype(BF16)
    grad_upward = (grad_activated * gate_values * sigmoid_gate).astype(BF16)
    grad_gate = (
        grad_activated * upward * sigmoid_gate * (1.0 + gate_values * (1.0 - sigmoid_gate))
    ).astype(BF16)
    grad_normed_part = dot("tf,fd->td", grad_gate, gate_full) + dot(
        "tf,fd->td", grad_upward, upward_full
    )
    grad_normed_two = scatter_dp(jnp.split(grad_normed_part, dp_count), dp_count)
    down_part = dot("tf,fd->td", activated, ffn_down_full)
    layer_output = (
        middle + RESIDUAL_SCALE * scatter_dp(jnp.split(down_part, dp_count), dp_count)
    ).astype(BF16)

    def scatter_seq(grads):
        return lax.psum_scatter(
            grads.astype(BF16), "seq", scatter_dimension=0, tiled=True
        ).astype(F32)

    sum_down = scatter_seq(dot("tf,td->fd", activated, grad_rows))
    sum_gate = scatter_seq(dot("tf,td->fd", grad_gate, normed_rows)).T
    sum_up = scatter_seq(dot("tf,td->fd", grad_upward, normed_rows)).T

    grad_middle_norm, grad_ffn_gain_part = norm_back(
        grad_normed_two, normal_two, inverse_two, ffn_gain_full
    )
    grad_middle = grad_out + grad_middle_norm
    grad_branch = (RESIDUAL_SCALE * grad_middle).astype(BF16)
    sum_out = scatter_all(dot("tk,td->kd", attended_low, grad_branch), dp_count)
    grad_attended = dot("td,kd->tk", grad_branch, proj_full).astype(BF16)
    grad_att_grouped = grad_attended.reshape(token_count, group_count, head_group, VDIM).transpose(
        1, 0, 2, 3
    )

    def backward_group(carried, operands):
        latent_sum, rotary_sum = carried
        query_block, keys_values, log_block, grad_att, attended_block, up_block = operands
        scores = score_block(query_block, keys_values, rotary_all, allowed)
        probabilities = jnp.exp(scores - log_block[..., None])
        grad_probs = dot("thv,lhv->htl", grad_att, keys_values[..., NOPE:])
        row_delta = jnp.sum(grad_att.astype(F32) * attended_block, axis=-1)
        grad_scores = (probabilities * (grad_probs - jnp.transpose(row_delta)[..., None])).astype(
            BF16
        )
        grad_query_nope = dot("htl,lhd->thd", grad_scores, keys_values[..., :NOPE]) * score_scale
        grad_query_rot = dot("htl,lr->thr", grad_scores, rotary_all) * score_scale
        grad_keys = dot("htl,thd->lhd", grad_scores, query_block[..., :NOPE]) * score_scale
        grad_rotary_part = dot("htl,thr->lr", grad_scores, query_block[..., NOPE:]) * score_scale
        grad_values = dot("htl,thv->lhv", probabilities.astype(BF16), grad_att)
        grad_pairs = (
            jnp.concatenate([grad_keys, grad_values], -1)
            .astype(BF16)
            .reshape(key_count, head_group * (NOPE + VDIM))
        )
        grad_up_block = dot("lk,lc->kc", grad_pairs, latent_all)
        latent_sum = latent_sum + dot("lk,kc->lc", grad_pairs, up_block)
        return (
            (latent_sum, rotary_sum + grad_rotary_part),
            (jnp.concatenate([grad_query_nope, grad_query_rot], -1), grad_up_block),
        )

    start_sums = (
        jnp.zeros((key_count, KV_RANK), F32),
        jnp.zeros((key_count, ROPE), F32),
    )
    (grad_latent_all, grad_rotary_all), (grad_query_grouped, grad_up_grouped) = lax.scan(
        backward_group,
        start_sums,
        (query_grouped, kept_values, log_totals, grad_att_grouped, attended_grouped, up_grouped),
    )
    sum_latent_up = scatter_all(
        grad_up_grouped.reshape(HEADS * (NOPE + VDIM), KV_RANK), dp_count
    ).T
    grad_keys_own = lax.psum_scatter(
        jnp.concatenate([grad_latent_all, grad_rotary_all], -1).astype(BF16),
        "seq",
        scatter_dimension=0,
        tiled=True,
    ).astype(F32)
    grad_latent_own = grad_keys_own[:, :KV_RANK]
    grad_rotary_own = grad_keys_own[:, KV_RANK:]
    grad_queries = grad_query_grouped.transpose(1, 0, 2, 3).reshape(token_count, HEADS, NOPE + ROPE)
    grad_projected = jnp.concatenate(
        [
            grad_queries[..., :NOPE],
            rotate_back(grad_queries[..., NOPE:], cos_table[:, None, :], sin_table[:, None, :]),
        ],
        -1,
    )
    grad_projected = grad_projected.astype(BF16).reshape(token_count, HEADS * (NOPE + ROPE))
    sum_query_up = scatter_all(dot("tk,tq->kq", grad_projected, query_normed), dp_count).T
    grad_query_normed = dot("tk,kq->tq", grad_projected, query_up_full)
    grad_query_latent, grad_query_gain_part = norm_back(
        grad_query_normed, normal_query, inverse_query, query_gain_full
    )
    grad_latent_norm, grad_latent_gain_part = norm_back(
        grad_latent_own, normal_latent, inverse_latent, latent_gain_full
    )
    grad_down_out = jnp.concatenate(
        [
            grad_query_latent,
            grad_latent_norm,
            rotate_back(grad_rotary_own, cos_table, sin_table),
        ],
        -1,
    ).astype(BF16)
    grad_down_part = dot("td,tc->dc", normed, grad_down_out)
    grad_normed = dot("tc,dc->td", grad_down_out, down_full)
    grad_input_norm, grad_attn_gain_part = norm_back(
        grad_normed, normal_one, inverse_one, attn_gain_full
    )
    input_grad = grad_middle + grad_input_norm

    def short_column(grads, own):
        blocks = grads.reshape(-1, own.shape[0])
        return jnp.pad(blocks, ((0, 0), (0, own_rows - own.shape[0]))).reshape(-1)

    gain_columns = jnp.stack(
        [
            grad_attn_gain_part,
            grad_ffn_gain_part,
            short_column(grad_query_gain_part, query_gain),
            short_column(grad_latent_gain_part, latent_gain),
        ],
        1,
    )
    sum_packed = scatter_all(
        jnp.concatenate([grad_down_part, gain_columns, jnp.zeros((width, pad_width), F32)], 1),
        dp_count,
    )
    sum_gains = sum_packed[:, down_width : down_width + 4].T
    return (
        layer_output,
        input_grad,
        sum_gains[0],
        sum_packed[:, :query_rank],
        sum_gains[2][: query_gain.shape[0]],
        sum_query_up,
        sum_packed[:, query_rank:down_width],
        sum_gains[3][: latent_gain.shape[0]],
        sum_latent_up,
        sum_out,
        sum_gains[1],
        sum_gate,
        sum_up,
        sum_down,
    )


HEAD_LANES = 128
SCORE_SCALE = (NOPE + ROPE) ** (-0.5)
QUERY_BLOCK = 256


def head_keys(pairs, rotary):
    lane = lax.broadcasted_iota(jnp.int32, pairs.shape, 1)
    return jnp.where(lane < NOPE, pairs, rotary)


def block_scores(query, keys, start):
    scores = lax.dot_general(
        query, keys, (((1,), (1,)), ((), ())), preferred_element_type=F32
    )
    row = start + lax.broadcasted_iota(jnp.int32, scores.shape, 0)
    column = lax.broadcasted_iota(jnp.int32, scores.shape, 1)
    return jnp.where(row >= column, scores * SCORE_SCALE, -1e30)


def turn(values, cos_ref, left_ref, right_ref, sign):
    half = ROPE // 2
    return (
        values * cos_ref
        + sign * (pltpu.roll(values, HEAD_LANES - half, 1) * left_ref)
        + sign * (pltpu.roll(values, half, 1) * right_ref)
    )


def attend_kernel(
    projected_ref, pairs_ref, rotary_ref, cos_ref, left_ref, right_ref,
    query_ref, attended_ref, log_ref, keys_ref,
):
    length = projected_ref.shape[0]
    block = min(QUERY_BLOCK, length)
    keys_ref[...] = head_keys(pairs_ref[...], rotary_ref[...])
    for start in range(0, length, block):
        rows = pl.ds(start, block)
        stop = start + block
        query = turn(
            projected_ref[rows, :], cos_ref[rows, :], left_ref[rows, :], right_ref[rows, :], 1.0
        ).astype(BF16)
        query_ref[rows, :] = query
        scores = block_scores(query, keys_ref[0:stop, :], start)
        peak = jnp.max(scores, axis=-1, keepdims=True)
        terms = jnp.exp(scores - peak)
        totals = jnp.sum(terms, axis=-1, keepdims=True)
        probs = (terms / totals).astype(BF16)
        mixed = jnp.dot(probs, pairs_ref[0:stop, :], preferred_element_type=F32)
        lane = lax.broadcasted_iota(jnp.int32, mixed.shape, 1)
        attended_ref[rows, :] = jnp.where(lane >= NOPE, mixed, 0.0).astype(BF16)
        log_ref[rows, :] = jnp.broadcast_to(peak + jnp.log(totals), mixed.shape)


def attend(projected, pairs, rotary, tables):
    length, lanes = projected.shape
    own = pl.BlockSpec((length, HEAD_LANES), lambda h: (0, h))
    shared = pl.BlockSpec((length, HEAD_LANES), lambda h: (0, 0))
    return pl.pallas_call(
        attend_kernel,
        grid=(lanes // HEAD_LANES,),
        in_specs=[own, own, shared, shared, shared, shared],
        out_specs=[own, own, own],
        out_shape=[
            jax.ShapeDtypeStruct((length, lanes), BF16),
            jax.ShapeDtypeStruct((length, lanes), BF16),
            jax.ShapeDtypeStruct((length, lanes), F32),
        ],
        scratch_shapes=[pltpu.VMEM((length, HEAD_LANES), BF16)],
        compiler_params=pltpu.CompilerParams(vmem_limit_bytes=40 * 1024 * 1024),
        cost_estimate=pl.CostEstimate(
            flops=3 * lanes * length * length, bytes_accessed=12 * lanes * length,
            transcendentals=length * length * lanes // HEAD_LANES,
        ),
        name="attend",
    )(projected, pairs, rotary, *tables)


def attend_back_kernel(
    query_ref, pairs_ref, rotary_ref, log_ref, grad_ref, cos_ref, left_ref, right_ref,
    grad_query_ref, grad_pairs_ref, grad_rotary_ref, keys_ref, grad_keys_ref, grad_values_ref,
):
    length = query_ref.shape[0]
    block = min(QUERY_BLOCK, length)
    keys_ref[...] = head_keys(pairs_ref[...], rotary_ref[...])
    grad_keys_ref[...] = jnp.zeros_like(grad_keys_ref)
    grad_values_ref[...] = jnp.zeros_like(grad_values_ref)
    for start in range(0, length, block):
        rows = pl.ds(start, block)
        stop = start + block
        query = query_ref[rows, :]
        grad = grad_ref[rows, :]
        scores = block_scores(query, keys_ref[0:stop, :], start)
        probs = jnp.exp(scores - log_ref[rows, 0:1])
        grad_probs = lax.dot_general(
            grad, pairs_ref[0:stop, :], (((1,), (1,)), ((), ())), preferred_element_type=F32
        )
        delta = jnp.sum(probs * grad_probs, axis=-1, keepdims=True)
        grad_scores = (probs * (grad_probs - delta)).astype(BF16)
        grad_query = (
            jnp.dot(grad_scores, keys_ref[0:stop, :], preferred_element_type=F32) * SCORE_SCALE
        )
        grad_query_ref[rows, :] = turn(
            grad_query, cos_ref[rows, :], left_ref[rows, :], right_ref[rows, :], -1.0
        ).astype(BF16)
        grad_keys_ref[:, 0:stop] += jnp.dot(
            query.T, grad_scores, preferred_element_type=F32
        )
        grad_values_ref[:, 0:stop] += jnp.dot(
            grad.T, probs.astype(BF16), preferred_element_type=F32
        )
    grad_keys = grad_keys_ref[...].T * SCORE_SCALE
    lane = lax.broadcasted_iota(jnp.int32, grad_keys.shape, 1)
    grad_pairs_ref[...] = jnp.where(lane < NOPE, grad_keys, grad_values_ref[...].T).astype(BF16)

    @pl.when(pl.program_id(0) == 0)
    def _():
        grad_rotary_ref[...] = jnp.zeros_like(grad_rotary_ref)

    grad_rotary_ref[...] += grad_keys


def attend_back(query, pairs, rotary, logs, grad, tables):
    length, lanes = query.shape
    own = pl.BlockSpec((length, HEAD_LANES), lambda h: (0, h))
    shared = pl.BlockSpec((length, HEAD_LANES), lambda h: (0, 0))
    return pl.pallas_call(
        attend_back_kernel,
        grid=(lanes // HEAD_LANES,),
        in_specs=[own, own, shared, own, own, shared, shared, shared],
        out_specs=[own, own, shared],
        out_shape=[
            jax.ShapeDtypeStruct((length, lanes), BF16),
            jax.ShapeDtypeStruct((length, lanes), BF16),
            jax.ShapeDtypeStruct((length, HEAD_LANES), F32),
        ],
        scratch_shapes=[
            pltpu.VMEM((length, HEAD_LANES), BF16),
            pltpu.VMEM((HEAD_LANES, length), F32),
            pltpu.VMEM((HEAD_LANES, length), F32),
        ],
        compiler_params=pltpu.CompilerParams(vmem_limit_bytes=48 * 1024 * 1024),
        cost_estimate=pl.CostEstimate(
            flops=8 * lanes * length * length, bytes_accessed=14 * lanes * length,
            transcendentals=length * length * lanes // HEAD_LANES,
        ),
        name="attend_back",
    )(query, pairs, rotary, logs, grad, *tables)


def ffn_kernel(
    weights_ref, rows_ref, grads_ref,
    hidden_ref, grad_rows_ref, out_rows_ref, grad_sum_ref, out_sum_ref,
):
    step = pl.program_id(0)
    hidden = weights_ref.shape[1] // 3

    def against(rows, start):
        return lax.dot_general(
            rows[...], weights_ref[0, start : start + hidden, :], (((1,), (1,)), ((), ())),
            preferred_element_type=F32,
        )

    gate_values = against(rows_ref, 0)
    upward = against(rows_ref, hidden)
    grad_activated = against(grads_ref, 2 * hidden)
    sigmoid_gate = jax.nn.sigmoid(gate_values)
    activated = gate_values * sigmoid_gate * upward
    grad_upward = grad_activated * gate_values * sigmoid_gate
    grad_gate = (
        grad_activated * upward * sigmoid_gate * (1.0 + gate_values * (1.0 - sigmoid_gate))
    )
    hidden_ref[0, 0:hidden, :] = grad_gate.T.astype(BF16)
    hidden_ref[0, hidden : 2 * hidden, :] = grad_upward.T.astype(BF16)
    hidden_ref[0, 2 * hidden : 3 * hidden, :] = activated.T.astype(BF16)

    def through(values, start):
        return jnp.dot(
            values.astype(BF16), weights_ref[0, start : start + hidden, :],
            preferred_element_type=F32,
        )

    grad_part = through(grad_gate, 0) + through(grad_upward, hidden)
    out_part = through(activated, 2 * hidden)

    @pl.when(step == 0)
    def _():
        grad_sum_ref[...] = grad_part
        out_sum_ref[...] = out_part

    @pl.when(step > 0)
    def _():
        grad_sum_ref[...] += grad_part
        out_sum_ref[...] += out_part

    @pl.when(step == pl.num_programs(0) - 1)
    def _():
        grad_rows_ref[...] = grad_sum_ref[...].astype(BF16)
        out_rows_ref[...] = out_sum_ref[...].astype(BF16)


def feed_forward(weights, rows, grads):
    steps, triple, width = weights.shape
    count = rows.shape[0]
    whole = pl.BlockSpec(memory_space=pltpu.VMEM)
    return pl.pallas_call(
        ffn_kernel,
        grid=(steps,),
        in_specs=[pl.BlockSpec((1, triple, width), lambda i: (i, 0, 0)), whole, whole],
        out_specs=[pl.BlockSpec((1, triple, count), lambda i: (i, 0, 0)), whole, whole],
        out_shape=[
            jax.ShapeDtypeStruct((steps, triple, count), BF16),
            jax.ShapeDtypeStruct((count, width), BF16),
            jax.ShapeDtypeStruct((count, width), BF16),
        ],
        scratch_shapes=[pltpu.VMEM((count, width), F32), pltpu.VMEM((count, width), F32)],
        compiler_params=pltpu.CompilerParams(vmem_limit_bytes=56 * 1024 * 1024),
        cost_estimate=pl.CostEstimate(
            flops=4 * steps * triple * width * count,
            bytes_accessed=2 * steps * triple * (width + count) + 8 * count * width,
            transcendentals=steps * triple * count // 3,
        ),
        name="feed_forward",
    )(weights, rows, grads)


def ffn_grads_kernel(hidden_ref, rows_ref, grads_ref, out_ref):
    hidden = hidden_ref.shape[1] // 3
    for start, source in ((0, rows_ref), (hidden, rows_ref), (2 * hidden, grads_ref)):
        out_ref[0, start : start + hidden, :] = jnp.dot(
            hidden_ref[0, start : start + hidden, :], source[...], preferred_element_type=F32
        ).astype(BF16)


def ffn_grads(hidden, rows, grads):
    steps, triple, count = hidden.shape
    width = rows.shape[1]
    whole = pl.BlockSpec(memory_space=pltpu.VMEM)
    return pl.pallas_call(
        ffn_grads_kernel,
        grid=(steps,),
        in_specs=[pl.BlockSpec((1, triple, count), lambda i: (i, 0, 0)), whole, whole],
        out_specs=pl.BlockSpec((1, triple, width), lambda i: (i, 0, 0)),
        out_shape=jax.ShapeDtypeStruct((steps, triple, width), BF16),
        compiler_params=pltpu.CompilerParams(vmem_limit_bytes=48 * 1024 * 1024),
        cost_estimate=pl.CostEstimate(
            flops=2 * steps * triple * width * count,
            bytes_accessed=2 * steps * triple * (width + count) + 4 * count * width,
            transcendentals=0,
        ),
        name="ffn_grads",
    )(hidden, rows, grads)


def after(value, *others):
    return lax.optimization_barrier((value,) + others)[0]


def flip(value, count, bits):
    return lax.ppermute(value, "seq", [(i, i ^ bits) for i in range(count)])


def gather_seq(value, count, chip, core, axis=0):
    even = [value] + [flip(value, count, 2 * m) for m in range(1, count // 2)]
    odd = [flip(piece, count, 1) for piece in even]
    shape = value.shape[:axis] + (count // 2, 2) + value.shape[axis:]
    whole = jnp.zeros(shape, value.dtype)
    for pieces, side in ((even, core), (odd, 1 - core)):
        for m, piece in enumerate(pieces):
            start = [0] * len(shape)
            start[axis] = chip ^ m
            start[axis + 1] = side
            whole = lax.dynamic_update_slice(
                whole, jnp.expand_dims(piece, (axis, axis + 1)), start
            )
    return whole


def choose(value, index, axis):
    return lax.dynamic_index_in_dim(value, index, axis, keepdims=False)


def scatter_seq(mine, theirs, count, chip, axis=0):
    half = mine.astype(F32) + flip(theirs.astype(BF16), count, 1).astype(F32)
    total = choose(half, chip, axis)
    half_low = half.astype(BF16)
    for m in range(1, count // 2):
        total = total + flip(choose(half_low, chip ^ m, axis), count, 2 * m).astype(F32)
    return total


def per_device_heads(
    dp_count,
    seq_count,
    layer_input,
    positions,
    attn_gain,
    query_down,
    query_gain,
    query_up,
    latent_down,
    latent_gain,
    latent_up,
    output_proj,
    ffn_gain,
    ffn_gate,
    ffn_up,
    ffn_down,
    cotangent,
):
    tokens, width = layer_input.shape
    query_rank = query_down.shape[1]
    own_rows = query_down.shape[0]
    down_width = query_rank + KV_RANK + ROPE
    heads = HEADS // seq_count
    place = lax.axis_index("dp")
    spot = lax.axis_index("seq")
    chip, core = spot // 2, spot % 2
    chips = seq_count // 2
    both = ("dp", "seq")
    devices = dp_count * seq_count
    length = seq_count * tokens

    def by_core(value):
        value = value.reshape(chips, 2, tokens, value.shape[1])
        return choose(value, core, 1), choose(value, 1 - core, 1)

    def gather_dp_ordered(value):
        whole = jnp.zeros((dp_count,) + value.shape, value.dtype)
        for k, piece in enumerate(gather_dp(value, dp_count)):
            whole = lax.dynamic_update_index_in_dim(whole, piece, (place - k) % dp_count, 0)
        return whole

    def scatter_dp_ordered(blocks):
        return scatter_dp(
            [choose(blocks, (place - k) % dp_count, 0) for k in range(dp_count)], dp_count
        )

    padded_width = down_width + 4 + -(down_width + 4) % HEAD_LANES

    def column(gain):
        return jnp.pad(gain, (0, own_rows - gain.shape[0]))[:, None]

    down_own = jnp.concatenate(
        [
            query_down,
            latent_down,
            column(attn_gain),
            column(ffn_gain),
            column(query_gain),
            column(latent_gain),
            jnp.zeros((own_rows, padded_width - down_width - 4), BF16),
        ],
        1,
    )
    down_plane = gather_dp_ordered(down_own)
    down_full = gather_seq(down_plane, seq_count, chip, core, 1).reshape(width, padded_width)
    gains = down_full[:, down_width : down_width + 4].T.astype(F32)
    attn_gain_full = gains[0]
    ffn_gain_full = gains[1]

    def short_gain(row, own):
        return row.reshape(devices, own_rows)[:, : own.shape[0]].reshape(-1)

    query_gain_full = short_gain(gains[2], query_gain)
    latent_gain_full = short_gain(gains[3], latent_gain)

    def group_rows(rows):
        whole = jnp.zeros((dp_count,) + rows.shape, rows.dtype)
        for k in range(dp_count):
            pairs = [
                (s * dp_count + (z + k) % dp_count, z * seq_count + s)
                for z in range(dp_count)
                for s in range(seq_count)
            ]
            whole = lax.dynamic_update_index_in_dim(
                whole, lax.ppermute(rows, both, pairs), (place + k) % dp_count, 0
            )
        return whole

    to_owner = [
        (z * seq_count + s, s * dp_count + z) for z in range(dp_count) for s in range(seq_count)
    ]

    def group_home(blocks):
        return lax.ppermute(scatter_dp_ordered(blocks).astype(BF16), both, to_owner).astype(F32)

    up_rows = max(query_up.shape[1], latent_up.shape[1])
    up_packed = jnp.concatenate(
        [
            jnp.pad(query_up.T, ((0, up_rows - query_up.shape[1]), (0, 0))),
            jnp.pad(latent_up.T, ((0, up_rows - latent_up.shape[1]), (0, 0))),
        ],
        1,
    )
    up_group = group_rows(after(up_packed, down_plane))
    query_up_padded = jnp.pad(
        up_group[:, : query_up.shape[1], :query_rank].reshape(heads, NOPE + ROPE, query_rank),
        ((0, 0), (0, HEAD_LANES - NOPE - ROPE), (0, 0)),
    ).reshape(heads * HEAD_LANES, query_rank)
    latent_up_group = up_group[:, : latent_up.shape[1], query_rank:].reshape(-1, KV_RANK)

    inputs = layer_input.astype(F32)
    normal_one, inverse_one = norm_parts(inputs)
    normed = (normal_one * attn_gain_full).astype(BF16)
    normed = after(normed, query_up_padded, latent_up_group)
    down_out = jnp.dot(normed, down_full, preferred_element_type=F32)
    normal_query, inverse_query = norm_parts(down_out[:, :query_rank])
    query_normed = (normal_query * query_gain_full).astype(BF16)
    normal_latent, inverse_latent = norm_parts(down_out[:, query_rank : query_rank + KV_RANK])
    latent = (normal_latent * latent_gain_full).astype(BF16)
    cos_table, sin_table = rotary_tables(positions)
    rotary_keys = rotate(
        down_out[:, query_rank + KV_RANK : down_width], cos_table, sin_table
    ).astype(BF16)
    half = ROPE // 2

    def two_parts(table):
        high = table.astype(BF16)
        return [high, (table - high.astype(F32)).astype(BF16)]

    token_message = jnp.concatenate(
        [query_normed, latent, rotary_keys]
        + two_parts(cos_table[:, :half])
        + two_parts(sin_table[:, :half]),
        1,
    )
    token_all = gather_seq(token_message, seq_count, chip, core).reshape(
        length, token_message.shape[1]
    )
    proj_group = group_rows(after(output_proj, down_full)).reshape(-1, width)
    grad_out = cotangent.astype(F32)
    grad_two = (RESIDUAL_SCALE * grad_out).astype(BF16)
    grad_rows = jnp.concatenate(gather_dp(after(grad_two, proj_group), dp_count))
    proj_padded = jnp.pad(
        proj_group.reshape(heads, VDIM, width), ((0, 0), (HEAD_LANES - VDIM, 0), (0, 0))
    ).reshape(heads * HEAD_LANES, width)
    ffn_own = after(jnp.concatenate([ffn_gate.T, ffn_up.T, ffn_down], 0), down_full)
    ffn_full = lax.all_gather(ffn_own, "seq", axis=0)

    query_normed_all = token_all[:, :query_rank]
    latent_all = token_all[:, query_rank : query_rank + KV_RANK]
    rotary_all = token_all[:, query_rank + KV_RANK : down_width]
    angles = token_all[:, down_width:].astype(F32)
    cos_all = angles[:, :half] + angles[:, half : 2 * half]
    sin_all = angles[:, 2 * half : 3 * half] + angles[:, 3 * half :]

    def lanes(start, values):
        return jnp.pad(values, ((0, 0), (start, HEAD_LANES - start - values.shape[1])))

    tables = (
        jnp.concatenate(
            [
                jnp.ones((length, NOPE), F32),
                cos_all,
                cos_all,
                jnp.zeros((length, HEAD_LANES - NOPE - ROPE), F32),
            ],
            1,
        ),
        lanes(NOPE, -sin_all),
        lanes(NOPE + half, sin_all),
    )
    rotary_lanes = lanes(NOPE, rotary_all)
    projected = dot("tq,kq->tk", query_normed_all, query_up_padded)
    pairs = dot("tc,kc->tk", latent_all, latent_up_group).astype(BF16)
    query, attended, logs = attend(projected, pairs, rotary_lanes, tables)

    attended_mine, attended_theirs = by_core(attended)
    branch = scatter_seq(
        dot("mtk,kd->mtd", attended_mine, proj_padded),
        dot("mtk,kd->mtd", attended_theirs, proj_padded),
        seq_count,
        chip,
    )
    middle = inputs + RESIDUAL_SCALE * branch
    normal_two, inverse_two = norm_parts(middle)
    normed_two = (normal_two * ffn_gain_full).astype(BF16)
    normed_two = after(normed_two, grad_rows)

    normed_rows = jnp.concatenate(gather_dp(normed_two, dp_count))
    proj_full = lax.all_gather(after(proj_group, normed_two), "seq", axis=0, tiled=True)
    hidden, grad_part, out_part = feed_forward(ffn_full, normed_rows, grad_rows)
    grad_parts = jnp.split(grad_part, dp_count)
    returned = [
        shift(grad_parts[k], "dp", dp_count, -k).astype(F32) for k in range(1, dp_count)
    ]
    grad_normed_two = sum(returned, grad_parts[0].astype(F32))
    hidden = after(hidden, returned[0])
    ffn_sums = lax.psum_scatter(
        ffn_grads(hidden, normed_rows, grad_rows), "seq", scatter_dimension=0
    ).astype(F32)
    out_part = after(out_part, grad_normed_two)
    layer_output = (
        middle + RESIDUAL_SCALE * scatter_dp(jnp.split(out_part, dp_count), dp_count)
    ).astype(BF16)

    grad_middle_norm, grad_ffn_gain_part = norm_back(
        grad_normed_two, normal_two, inverse_two, ffn_gain_full
    )
    grad_middle = grad_out + grad_middle_norm
    grad_branch = (RESIDUAL_SCALE * grad_middle).astype(BF16)
    grad_attended = dot("td,kd->tk", grad_branch, proj_full).astype(BF16)
    grad_attended = lax.all_to_all(
        grad_attended.reshape(tokens, seq_count, heads * VDIM).transpose(1, 0, 2),
        "seq",
        split_axis=0,
        concat_axis=0,
        tiled=True,
    ).reshape(length, heads, VDIM)
    grad_attended = jnp.pad(
        grad_attended, ((0, 0), (0, 0), (HEAD_LANES - VDIM, 0))
    ).reshape(length, heads * HEAD_LANES)
    grad_projected, grad_pairs, grad_rotary = attend_back(
        query, pairs, rotary_lanes, logs, grad_attended, tables
    )
    token_grads = []
    for projected_part, pairs_part, rotary_part in zip(
        by_core(grad_projected), by_core(grad_pairs), by_core(grad_rotary)
    ):
        token_grads.append(
            jnp.concatenate(
                [
                    dot("mtk,kq->mtq", projected_part, query_up_padded).astype(BF16),
                    dot("mtk,kc->mtc", pairs_part, latent_up_group).astype(BF16),
                    rotary_part[:, :, NOPE : NOPE + ROPE].astype(BF16),
                ],
                2,
            )
        )
    grad_own = scatter_seq(token_grads[0], token_grads[1], seq_count, chip)

    query_up_grads = dot("tk,tq->kq", grad_projected, query_normed_all).astype(BF16)
    query_up_grads = query_up_grads.reshape(heads, HEAD_LANES, query_rank)[:, : NOPE + ROPE]
    query_up_grads = query_up_grads.reshape(dp_count, -1, query_rank)
    latent_up_grads = dot("tk,tc->kc", grad_pairs, latent_all).astype(BF16)
    latent_up_grads = latent_up_grads.reshape(dp_count, -1, KV_RANK)
    up_grads = jnp.concatenate(
        [
            jnp.pad(
                query_up_grads, ((0, 0), (0, up_rows - query_up_grads.shape[1]), (0, 0))
            ),
            jnp.pad(
                latent_up_grads, ((0, 0), (0, up_rows - latent_up_grads.shape[1]), (0, 0))
            ),
        ],
        2,
    )
    sum_up = group_home(up_grads)
    sum_query_up = sum_up[: query_up.shape[1], :query_rank].T
    sum_latent_up = sum_up[: latent_up.shape[1], query_rank:].T

    branch_all = gather_seq(after(grad_branch, grad_attended), seq_count, chip, core)
    proj_grads = dot("tk,td->kd", attended, branch_all.reshape(length, width)).astype(BF16)
    proj_grads = proj_grads.reshape(heads, HEAD_LANES, width)[:, HEAD_LANES - VDIM :]
    sum_out = group_home(proj_grads.reshape(dp_count, -1, width))

    grad_query_latent, grad_query_gain_part = norm_back(
        grad_own[:, :query_rank], normal_query, inverse_query, query_gain_full
    )
    grad_latent_norm, grad_latent_gain_part = norm_back(
        grad_own[:, query_rank : query_rank + KV_RANK],
        normal_latent,
        inverse_latent,
        latent_gain_full,
    )
    grad_down_out = jnp.concatenate(
        [
            grad_query_latent,
            grad_latent_norm,
            rotate_back(grad_own[:, query_rank + KV_RANK :], cos_table, sin_table),
            jnp.zeros((tokens, padded_width - down_width), F32),
        ],
        -1,
    ).astype(BF16)
    grad_normed = dot("tc,dc->td", grad_down_out, down_full)
    grad_input_norm, grad_attn_gain_part = norm_back(
        grad_normed, normal_one, inverse_one, attn_gain_full
    )
    input_grad = grad_middle + grad_input_norm

    def short_column(grads, own):
        blocks = grads.reshape(devices, own.shape[0])
        return jnp.pad(blocks, ((0, 0), (0, own_rows - own.shape[0]))).reshape(-1)

    gain_columns = jnp.stack(
        [
            grad_attn_gain_part,
            grad_ffn_gain_part,
            short_column(grad_query_gain_part, query_gain),
            short_column(grad_latent_gain_part, latent_gain),
        ],
        1,
    )
    down_sums = dot("td,tc->dc", normed, grad_down_out) + jnp.pad(
        gain_columns, ((0, 0), (down_width, padded_width - down_width - 4))
    )
    down_sums = down_sums.astype(BF16).reshape(dp_count, chips, 2, own_rows, padded_width)
    sum_down = scatter_dp_ordered(
        scatter_seq(
            choose(down_sums, core, 2), choose(down_sums, 1 - core, 2), seq_count, chip, 1
        )
    )
    sum_gains = sum_down[:, down_width : down_width + 4].T
    own_hidden = ffn_down.shape[0]
    return (
        layer_output,
        input_grad,
        sum_gains[0],
        sum_down[:, :query_rank],
        sum_gains[2][: query_gain.shape[0]],
        sum_query_up,
        sum_down[:, query_rank:down_width],
        sum_gains[3][: latent_gain.shape[0]],
        sum_latent_up,
        sum_out,
        sum_gains[1],
        ffn_sums[:own_hidden].T,
        ffn_sums[own_hidden : 2 * own_hidden].T,
        ffn_sums[2 * own_hidden :],
    )


def solution(mesh):
    both = ("dp", "seq")
    dp_count = mesh.shape["dp"]

    seq_count = mesh.shape["seq"]
    by_heads = HEADS % seq_count == 0 and seq_count & (seq_count - 1) == 0

    def run(*arrays):
        if by_heads:
            return per_device_heads(dp_count, seq_count, *arrays)
        return per_device_general(dp_count, *arrays)

    in_specs = (
        P(both, None),
        P(both),
        P(both),
        P(both, None),
        P(both),
        P(None, both),
        P(both, None),
        P(both),
        P(None, both),
        P(both, None),
        P(both),
        P(None, both),
        P(None, both),
        P(both, None),
        P(both, None),
    )
    out_specs = (
        P(both, None),
        P(both, None),
        P(both),
        P(both, None),
        P(both),
        P(None, both),
        P(both, None),
        P(both),
        P(None, both),
        P(both, None),
        P(both),
        P(None, both),
        P(None, both),
        P(both, None),
    )
    return jax.shard_map(run, mesh=mesh, in_specs=in_specs, out_specs=out_specs, check_vma=False)
```

```python
import math

import jax
import jax.numpy as jnp
from jax import lax
from jax.experimental import pallas as pl
from jax.experimental.pallas import tpu as pltpu
from jax.sharding import PartitionSpec as P

KV_RANK = 256
HEADS = 40
NOPE = 64
ROPE = 32
VDIM = 64


EPSILON = 1e-05
RESIDUAL_SCALE = 1.4 / math.sqrt(62.0)
F32 = jnp.float32
BF16 = jnp.bfloat16


def norm_parts(values):
    inverse = lax.rsqrt(jnp.mean(values * values, axis=-1, keepdims=True) + EPSILON)
    return (values * inverse, inverse)


def norm_back(grad_scaled, normalized, inverse, scale_gain):
    gain_grad = jnp.sum(grad_scaled * normalized, axis=0)
    grad_normal = grad_scaled * scale_gain
    values_grad = inverse * (
        grad_normal - normalized * jnp.mean(grad_normal * normalized, axis=-1, keepdims=True)
    )
    return (values_grad, gain_grad)


def rotary_tables(positions):
    half_width = ROPE // 2
    inverse = 10000.0 ** (-2.0 * jnp.arange(half_width, dtype=F32) / ROPE)
    angles = positions.astype(F32)[:, None] * inverse[None, :]
    cos_table = jnp.cos(angles)
    sin_table = jnp.sin(angles)
    return (
        jnp.concatenate([cos_table, cos_table], -1),
        jnp.concatenate([sin_table, sin_table], -1),
    )


def rotate(values, cos_table, sin_table):
    half_width = values.shape[-1] // 2
    turned = jnp.concatenate([-values[..., half_width:], values[..., :half_width]], -1)
    return values * cos_table + turned * sin_table


def rotate_back(grads, cos_table, sin_table):
    half_width = grads.shape[-1] // 2
    scaled = grads * sin_table
    return grads * cos_table + jnp.concatenate(
        [scaled[..., half_width:], -scaled[..., :half_width]], -1
    )


def score_block(query_block, keys_values, rotary_all, allowed):
    score_scale = (NOPE + ROPE) ** (-0.5)
    scores = jnp.einsum(
        "thd,lhd->htl",
        query_block[..., :NOPE],
        keys_values[..., :NOPE],
        preferred_element_type=F32,
    )
    scores = scores + jnp.einsum(
        "thr,lr->htl", query_block[..., NOPE:], rotary_all, preferred_element_type=F32
    )
    return jnp.where(allowed[None], scores * score_scale, -1e30)


def dot(spec, left, right):
    return jnp.einsum(spec, left, right, preferred_element_type=F32)


def shift(value, axis, count, step):
    return lax.ppermute(value, axis, [(i, (i + step) % count) for i in range(count)])


def gather_dp(value, count):
    return [value] + [shift(value, "dp", count, k) for k in range(1, count)]


def scatter_dp(parts, count):
    total = parts[0].astype(F32)
    for k in range(1, count):
        total = total + shift(parts[k].astype(BF16), "dp", count, -k).astype(F32)
    return total


def gather_all(rows, dp_count):
    by_place = jnp.stack(gather_dp(rows, dp_count))
    place = lax.axis_index("dp")
    order = (place - jnp.arange(dp_count)) % dp_count
    absolute = jnp.take(by_place, order, axis=0)
    whole = lax.all_gather(absolute, "seq", axis=1, tiled=True)
    return whole.reshape(-1, rows.shape[1])


def scatter_all(grads, dp_count):
    blocks = grads.astype(BF16).reshape(dp_count, -1, grads.shape[1])
    own_seq = lax.psum_scatter(blocks, "seq", scatter_dimension=1, tiled=True)
    place = lax.axis_index("dp")
    parts = [
        lax.dynamic_index_in_dim(own_seq, (place - k) % dp_count, 0, keepdims=False)
        for k in range(dp_count)
    ]
    return scatter_dp(parts, dp_count)


def per_device_general(
    dp_count,
    layer_input,
    positions,
    attn_gain,
    query_down,
    query_gain,
    query_up,
    latent_down,
    latent_gain,
    latent_up,
    output_proj,
    ffn_gain,
    ffn_gate,
    ffn_up,
    ffn_down,
    cotangent,
):
    token_count, width = layer_input.shape
    query_rank = query_down.shape[1]
    own_rows = query_down.shape[0]
    score_scale = (NOPE + ROPE) ** (-0.5)

    def column(gain):
        return jnp.pad(gain, (0, own_rows - gain.shape[0]))[:, None]

    down_width = query_rank + KV_RANK + ROPE
    pad_width = -(down_width + 4) % 128
    packed = jnp.concatenate(
        [
            query_down,
            latent_down,
            column(attn_gain),
            column(ffn_gain),
            column(query_gain),
            column(latent_gain),
            jnp.zeros((own_rows, pad_width), BF16),
        ],
        1,
    )
    packed_full = gather_all(packed, dp_count)
    down_full = packed_full[:, :down_width]
    gains = packed_full[:, down_width : down_width + 4].T.astype(F32)
    attn_gain_full = gains[0]
    ffn_gain_full = gains[1]

    def short_gain(row, own):
        return row.reshape(-1, own_rows)[:, : own.shape[0]].reshape(-1)

    query_gain_full = short_gain(gains[2], query_gain)
    latent_gain_full = short_gain(gains[3], latent_gain)

    query_up_full = gather_all(query_up.T, dp_count)
    latent_up_full = gather_all(latent_up.T, dp_count)
    proj_full = gather_all(output_proj, dp_count)
    gate_full = lax.all_gather(ffn_gate.T, "seq", axis=0, tiled=True)
    upward_full = lax.all_gather(ffn_up.T, "seq", axis=0, tiled=True)
    ffn_down_full = lax.all_gather(ffn_down, "seq", axis=0, tiled=True)

    grad_out = cotangent.astype(F32)
    grad_two = (RESIDUAL_SCALE * grad_out).astype(BF16)
    grad_rows = jnp.concatenate(gather_dp(grad_two, dp_count))

    inputs = layer_input.astype(F32)
    cos_table, sin_table = rotary_tables(positions)
    normal_one, inverse_one = norm_parts(inputs)
    normed = (normal_one * attn_gain_full).astype(BF16)
    down_out = jnp.dot(normed, down_full, preferred_element_type=F32)
    query_latent = down_out[:, :query_rank]
    compressed = down_out[:, query_rank:]
    normal_latent, inverse_latent = norm_parts(compressed[:, :KV_RANK])
    latent = (normal_latent * latent_gain_full).astype(BF16)
    rotary_keys = rotate(compressed[:, KV_RANK:], cos_table, sin_table).astype(BF16)
    keys_all = lax.all_gather(
        jnp.concatenate([latent, rotary_keys], -1), "seq", axis=0, tiled=True
    )
    latent_all = keys_all[:, :KV_RANK]
    rotary_all = keys_all[:, KV_RANK:]
    normal_query, inverse_query = norm_parts(query_latent)
    query_normed = (normal_query * query_gain_full).astype(BF16)
    projected = dot("tq,kq->tk", query_normed, query_up_full).reshape(
        token_count, HEADS, NOPE + ROPE
    )
    queries = jnp.concatenate(
        [
            projected[..., :NOPE],
            rotate(projected[..., NOPE:], cos_table[:, None, :], sin_table[:, None, :]),
        ],
        -1,
    ).astype(BF16)
    key_count = latent_all.shape[0]
    head_group = math.gcd(HEADS, 8)
    group_count = HEADS // head_group
    first_row = lax.axis_index("seq") * token_count
    allowed = (first_row + jnp.arange(token_count))[:, None] >= jnp.arange(key_count)[None, :]
    up_grouped = latent_up_full.reshape(group_count, head_group * (NOPE + VDIM), KV_RANK)
    query_grouped = queries.reshape(token_count, group_count, head_group, NOPE + ROPE).transpose(
        1, 0, 2, 3
    )

    def forward_group(operands):
        query_block, up_block = operands
        keys_values = dot("lc,kc->lk", latent_all, up_block).astype(BF16)
        keys_values = keys_values.reshape(key_count, head_group, NOPE + VDIM)
        scores = score_block(query_block, keys_values, rotary_all, allowed)
        row_peak = jnp.max(scores, axis=-1, keepdims=True)
        exponent_terms = jnp.exp(scores - row_peak)
        row_totals = jnp.sum(exponent_terms, axis=-1, keepdims=True)
        probabilities = (exponent_terms / row_totals).astype(BF16)
        attended_block = dot("htl,lhv->thv", probabilities, keys_values[..., NOPE:])
        return (keys_values, attended_block, (row_peak + jnp.log(row_totals))[..., 0])

    kept_values, attended_grouped, log_totals = lax.map(forward_group, (query_grouped, up_grouped))
    attended_low = (
        attended_grouped.transpose(1, 0, 2, 3).reshape(token_count, HEADS * VDIM).astype(BF16)
    )
    branch = jnp.dot(attended_low, proj_full, preferred_element_type=F32)
    middle = inputs + RESIDUAL_SCALE * branch
    normal_two, inverse_two = norm_parts(middle)
    normed_two = (normal_two * ffn_gain_full).astype(BF16)

    normed_rows = jnp.concatenate(gather_dp(normed_two, dp_count))
    gate_values = dot("td,fd->tf", normed_rows, gate_full)
    upward = dot("td,fd->tf", normed_rows, upward_full)
    grad_activated = dot("td,fd->tf", grad_rows, ffn_down_full)
    sigmoid_gate = jax.nn.sigmoid(gate_values)
    activated = (gate_values * sigmoid_gate * upward).astype(BF16)
    grad_upward = (grad_activated * gate_values * sigmoid_gate).astype(BF16)
    grad_gate = (
        grad_activated * upward * sigmoid_gate * (1.0 + gate_values * (1.0 - sigmoid_gate))
    ).astype(BF16)
    grad_normed_part = dot("tf,fd->td", grad_gate, gate_full) + dot(
        "tf,fd->td", grad_upward, upward_full
    )
    grad_normed_two = scatter_dp(jnp.split(grad_normed_part, dp_count), dp_count)
    down_part = dot("tf,fd->td", activated, ffn_down_full)
    layer_output = (
        middle + RESIDUAL_SCALE * scatter_dp(jnp.split(down_part, dp_count), dp_count)
    ).astype(BF16)

    def scatter_seq(grads):
        return lax.psum_scatter(
            grads.astype(BF16), "seq", scatter_dimension=0, tiled=True
        ).astype(F32)

    sum_down = scatter_seq(dot("tf,td->fd", activated, grad_rows))
    sum_gate = scatter_seq(dot("tf,td->fd", grad_gate, normed_rows)).T
    sum_up = scatter_seq(dot("tf,td->fd", grad_upward, normed_rows)).T

    grad_middle_norm, grad_ffn_gain_part = norm_back(
        grad_normed_two, normal_two, inverse_two, ffn_gain_full
    )
    grad_middle = grad_out + grad_middle_norm
    grad_branch = (RESIDUAL_SCALE * grad_middle).astype(BF16)
    sum_out = scatter_all(dot("tk,td->kd", attended_low, grad_branch), dp_count)
    grad_attended = dot("td,kd->tk", grad_branch, proj_full).astype(BF16)
    grad_att_grouped = grad_attended.reshape(token_count, group_count, head_group, VDIM).transpose(
        1, 0, 2, 3
    )

    def backward_group(carried, operands):
        latent_sum, rotary_sum = carried
        query_block, keys_values, log_block, grad_att, attended_block, up_block = operands
        scores = score_block(query_block, keys_values, rotary_all, allowed)
        probabilities = jnp.exp(scores - log_block[..., None])
        grad_probs = dot("thv,lhv->htl", grad_att, keys_values[..., NOPE:])
        row_delta = jnp.sum(grad_att.astype(F32) * attended_block, axis=-1)
        grad_scores = (probabilities * (grad_probs - jnp.transpose(row_delta)[..., None])).astype(
            BF16
        )
        grad_query_nope = dot("htl,lhd->thd", grad_scores, keys_values[..., :NOPE]) * score_scale
        grad_query_rot = dot("htl,lr->thr", grad_scores, rotary_all) * score_scale
        grad_keys = dot("htl,thd->lhd", grad_scores, query_block[..., :NOPE]) * score_scale
        grad_rotary_part = dot("htl,thr->lr", grad_scores, query_block[..., NOPE:]) * score_scale
        grad_values = dot("htl,thv->lhv", probabilities.astype(BF16), grad_att)
        grad_pairs = (
            jnp.concatenate([grad_keys, grad_values], -1)
            .astype(BF16)
            .reshape(key_count, head_group * (NOPE + VDIM))
        )
        grad_up_block = dot("lk,lc->kc", grad_pairs, latent_all)
        latent_sum = latent_sum + dot("lk,kc->lc", grad_pairs, up_block)
        return (
            (latent_sum, rotary_sum + grad_rotary_part),
            (jnp.concatenate([grad_query_nope, grad_query_rot], -1), grad_up_block),
        )

    start_sums = (
        jnp.zeros((key_count, KV_RANK), F32),
        jnp.zeros((key_count, ROPE), F32),
    )
    (grad_latent_all, grad_rotary_all), (grad_query_grouped, grad_up_grouped) = lax.scan(
        backward_group,
        start_sums,
        (query_grouped, kept_values, log_totals, grad_att_grouped, attended_grouped, up_grouped),
    )
    sum_latent_up = scatter_all(
        grad_up_grouped.reshape(HEADS * (NOPE + VDIM), KV_RANK), dp_count
    ).T
    grad_keys_own = lax.psum_scatter(
        jnp.concatenate([grad_latent_all, grad_rotary_all], -1).astype(BF16),
        "seq",
        scatter_dimension=0,
        tiled=True,
    ).astype(F32)
    grad_latent_own = grad_keys_own[:, :KV_RANK]
    grad_rotary_own = grad_keys_own[:, KV_RANK:]
    grad_queries = grad_query_grouped.transpose(1, 0, 2, 3).reshape(token_count, HEADS, NOPE + ROPE)
    grad_projected = jnp.concatenate(
        [
            grad_queries[..., :NOPE],
            rotate_back(grad_queries[..., NOPE:], cos_table[:, None, :], sin_table[:, None, :]),
        ],
        -1,
    )
    grad_projected = grad_projected.astype(BF16).reshape(token_count, HEADS * (NOPE + ROPE))
    sum_query_up = scatter_all(dot("tk,tq->kq", grad_projected, query_normed), dp_count).T
    grad_query_normed = dot("tk,kq->tq", grad_projected, query_up_full)
    grad_query_latent, grad_query_gain_part = norm_back(
        grad_query_normed, normal_query, inverse_query, query_gain_full
    )
    grad_latent_norm, grad_latent_gain_part = norm_back(
        grad_latent_own, normal_latent, inverse_latent, latent_gain_full
    )
    grad_down_out = jnp.concatenate(
        [
            grad_query_latent,
            grad_latent_norm,
            rotate_back(grad_rotary_own, cos_table, sin_table),
        ],
        -1,
    ).astype(BF16)
    grad_down_part = dot("td,tc->dc", normed, grad_down_out)
    grad_normed = dot("tc,dc->td", grad_down_out, down_full)
    grad_input_norm, grad_attn_gain_part = norm_back(
        grad_normed, normal_one, inverse_one, attn_gain_full
    )
    input_grad = grad_middle + grad_input_norm

    def short_column(grads, own):
        blocks = grads.reshape(-1, own.shape[0])
        return jnp.pad(blocks, ((0, 0), (0, own_rows - own.shape[0]))).reshape(-1)

    gain_columns = jnp.stack(
        [
            grad_attn_gain_part,
            grad_ffn_gain_part,
            short_column(grad_query_gain_part, query_gain),
            short_column(grad_latent_gain_part, latent_gain),
        ],
        1,
    )
    sum_packed = scatter_all(
        jnp.concatenate([grad_down_part, gain_columns, jnp.zeros((width, pad_width), F32)], 1),
        dp_count,
    )
    sum_gains = sum_packed[:, down_width : down_width + 4].T
    return (
        layer_output,
        input_grad,
        sum_gains[0],
        sum_packed[:, :query_rank],
        sum_gains[2][: query_gain.shape[0]],
        sum_query_up,
        sum_packed[:, query_rank:down_width],
        sum_gains[3][: latent_gain.shape[0]],
        sum_latent_up,
        sum_out,
        sum_gains[1],
        sum_gate,
        sum_up,
        sum_down,
    )


HEAD_LANES = 128
SCORE_SCALE = (NOPE + ROPE) ** (-0.5)
QUERY_BLOCK = 256


def head_keys(pairs, rotary):
    lane = lax.broadcasted_iota(jnp.int32, pairs.shape, 1)
    return jnp.where(lane < NOPE, pairs, rotary)


def block_scores(query, keys, start):
    scores = lax.dot_general(
        query, keys, (((1,), (1,)), ((), ())), preferred_element_type=F32
    )
    row = start + lax.broadcasted_iota(jnp.int32, scores.shape, 0)
    column = lax.broadcasted_iota(jnp.int32, scores.shape, 1)
    return jnp.where(row >= column, scores * SCORE_SCALE, -1e30)


def turn(values, cos_ref, left_ref, right_ref, sign):
    half = ROPE // 2
    return (
        values * cos_ref
        + sign * (pltpu.roll(values, HEAD_LANES - half, 1) * left_ref)
        + sign * (pltpu.roll(values, half, 1) * right_ref)
    )


def attend_kernel(
    projected_ref, pairs_ref, rotary_ref, cos_ref, left_ref, right_ref,
    query_ref, attended_ref, log_ref, keys_ref,
):
    length = projected_ref.shape[0]
    block = min(QUERY_BLOCK, length)
    keys_ref[...] = head_keys(pairs_ref[...], rotary_ref[...])
    for start in range(0, length, block):
        rows = pl.ds(start, block)
        stop = start + block
        query = turn(
            projected_ref[rows, :], cos_ref[rows, :], left_ref[rows, :], right_ref[rows, :], 1.0
        ).astype(BF16)
        query_ref[rows, :] = query
        scores = block_scores(query, keys_ref[0:stop, :], start)
        peak = jnp.max(scores, axis=-1, keepdims=True)
        terms = jnp.exp(scores - peak)
        totals = jnp.sum(terms, axis=-1, keepdims=True)
        probs = (terms / totals).astype(BF16)
        mixed = jnp.dot(probs, pairs_ref[0:stop, :], preferred_element_type=F32)
        lane = lax.broadcasted_iota(jnp.int32, mixed.shape, 1)
        attended_ref[rows, :] = jnp.where(lane >= NOPE, mixed, 0.0).astype(BF16)
        log_ref[rows, :] = jnp.broadcast_to(peak + jnp.log(totals), mixed.shape)


def attend(projected, pairs, rotary, tables):
    length, lanes = projected.shape
    own = pl.BlockSpec((length, HEAD_LANES), lambda h: (0, h))
    shared = pl.BlockSpec((length, HEAD_LANES), lambda h: (0, 0))
    return pl.pallas_call(
        attend_kernel,
        grid=(lanes // HEAD_LANES,),
        in_specs=[own, own, shared, shared, shared, shared],
        out_specs=[own, own, own],
        out_shape=[
            jax.ShapeDtypeStruct((length, lanes), BF16),
            jax.ShapeDtypeStruct((length, lanes), BF16),
            jax.ShapeDtypeStruct((length, lanes), F32),
        ],
        scratch_shapes=[pltpu.VMEM((length, HEAD_LANES), BF16)],
        compiler_params=pltpu.CompilerParams(vmem_limit_bytes=40 * 1024 * 1024),
        cost_estimate=pl.CostEstimate(
            flops=3 * lanes * length * length, bytes_accessed=12 * lanes * length,
            transcendentals=length * length * lanes // HEAD_LANES,
        ),
        name="attend",
    )(projected, pairs, rotary, *tables)


def attend_back_kernel(
    query_ref, pairs_ref, rotary_ref, log_ref, grad_ref, cos_ref, left_ref, right_ref,
    grad_query_ref, grad_pairs_ref, grad_rotary_ref, keys_ref, grad_keys_ref, grad_values_ref,
):
    length = query_ref.shape[0]
    block = min(QUERY_BLOCK, length)
    keys_ref[...] = head_keys(pairs_ref[...], rotary_ref[...])
    grad_keys_ref[...] = jnp.zeros_like(grad_keys_ref)
    grad_values_ref[...] = jnp.zeros_like(grad_values_ref)
    for start in range(0, length, block):
        rows = pl.ds(start, block)
        stop = start + block
        query = query_ref[rows, :]
        grad = grad_ref[rows, :]
        scores = block_scores(query, keys_ref[0:stop, :], start)
        probs = jnp.exp(scores - log_ref[rows, 0:1])
        grad_probs = lax.dot_general(
            grad, pairs_ref[0:stop, :], (((1,), (1,)), ((), ())), preferred_element_type=F32
        )
        delta = jnp.sum(probs * grad_probs, axis=-1, keepdims=True)
        grad_scores = (probs * (grad_probs - delta)).astype(BF16)
        grad_query = (
            jnp.dot(grad_scores, keys_ref[0:stop, :], preferred_element_type=F32) * SCORE_SCALE
        )
        grad_query_ref[rows, :] = turn(
            grad_query, cos_ref[rows, :], left_ref[rows, :], right_ref[rows, :], -1.0
        ).astype(BF16)
        grad_keys_ref[:, 0:stop] += jnp.dot(
            query.T, grad_scores, preferred_element_type=F32
        )
        grad_values_ref[:, 0:stop] += jnp.dot(
            grad.T, probs.astype(BF16), preferred_element_type=F32
        )
    grad_keys = grad_keys_ref[...].T * SCORE_SCALE
    lane = lax.broadcasted_iota(jnp.int32, grad_keys.shape, 1)
    grad_pairs_ref[...] = jnp.where(lane < NOPE, grad_keys, grad_values_ref[...].T).astype(BF16)

    @pl.when(pl.program_id(0) == 0)
    def _():
        grad_rotary_ref[...] = jnp.zeros_like(grad_rotary_ref)

    grad_rotary_ref[...] += grad_keys


def attend_back(query, pairs, rotary, logs, grad, tables):
    length, lanes = query.shape
    own = pl.BlockSpec((length, HEAD_LANES), lambda h: (0, h))
    shared = pl.BlockSpec((length, HEAD_LANES), lambda h: (0, 0))
    return pl.pallas_call(
        attend_back_kernel,
        grid=(lanes // HEAD_LANES,),
        in_specs=[own, own, shared, own, own, shared, shared, shared],
        out_specs=[own, own, shared],
        out_shape=[
            jax.ShapeDtypeStruct((length, lanes), BF16),
            jax.ShapeDtypeStruct((length, lanes), BF16),
            jax.ShapeDtypeStruct((length, HEAD_LANES), F32),
        ],
        scratch_shapes=[
            pltpu.VMEM((length, HEAD_LANES), BF16),
            pltpu.VMEM((HEAD_LANES, length), F32),
            pltpu.VMEM((HEAD_LANES, length), F32),
        ],
        compiler_params=pltpu.CompilerParams(vmem_limit_bytes=48 * 1024 * 1024),
        cost_estimate=pl.CostEstimate(
            flops=8 * lanes * length * length, bytes_accessed=14 * lanes * length,
            transcendentals=length * length * lanes // HEAD_LANES,
        ),
        name="attend_back",
    )(query, pairs, rotary, logs, grad, *tables)


def ffn_kernel(weights_ref, rows_ref, grads_ref, both_ref, act_ref):
    def against(index, rows):
        return lax.dot_general(
            weights_ref[index], rows[...], (((1,), (1,)), ((), ())), preferred_element_type=F32
        )

    gate_values = against(0, rows_ref)
    upward = against(1, rows_ref)
    grad_activated = against(2, grads_ref)
    sigmoid_gate = jax.nn.sigmoid(gate_values)
    swish = gate_values * sigmoid_gate
    act_ref[...] = (swish * upward).astype(BF16)
    both_ref[1] = (grad_activated * swish).astype(BF16)
    both_ref[0] = (
        grad_activated * upward * sigmoid_gate * (1.0 + gate_values * (1.0 - sigmoid_gate))
    ).astype(BF16)


def ffn_hidden(weights, rows, grads):
    _, hidden, width = weights.shape
    count = rows.shape[0]
    block = hidden // 4
    whole = pl.BlockSpec(memory_space=pltpu.VMEM)
    own = pl.BlockSpec((block, count), lambda i: (i, 0))
    return pl.pallas_call(
        ffn_kernel,
        grid=(hidden // block,),
        in_specs=[pl.BlockSpec((3, block, width), lambda i: (0, i, 0)), whole, whole],
        out_specs=[pl.BlockSpec((2, block, count), lambda i: (0, i, 0)), own],
        out_shape=[
            jax.ShapeDtypeStruct((2, hidden, count), BF16),
            jax.ShapeDtypeStruct((hidden, count), BF16),
        ],
        compiler_params=pltpu.CompilerParams(vmem_limit_bytes=48 * 1024 * 1024),
        cost_estimate=pl.CostEstimate(
            flops=6 * hidden * width * count,
            bytes_accessed=6 * hidden * (width + count) + 4 * count * width,
            transcendentals=hidden * count,
        ),
        name="ffn_hidden",
    )(weights, rows, grads)


def ffn_grads_kernel(both_ref, act_ref, rows_ref, grads_ref, earlier_ref, out_ref):
    hidden = act_ref.shape[1]
    parts = ((both_ref[0, 0], rows_ref), (both_ref[1, 0], rows_ref), (act_ref[0], grads_ref))
    for place, (left, right) in enumerate(parts):
        out_ref[0, place * hidden : (place + 1) * hidden, :] = jnp.dot(
            left, right[...], preferred_element_type=F32
        ).astype(BF16)


def ffn_grads(grad_both, activated, rows, grads, earlier):
    steps, hidden, count = activated.shape
    width = rows.shape[1]
    whole = pl.BlockSpec(memory_space=pltpu.VMEM)
    own = pl.BlockSpec((1, hidden, count), lambda i: (i, 0, 0))
    return pl.pallas_call(
        ffn_grads_kernel,
        grid=(steps,),
        in_specs=[
            pl.BlockSpec((2, 1, hidden, count), lambda i: (0, i, 0, 0)),
            own,
            whole,
            whole,
            pl.BlockSpec(memory_space=pl.ANY),
        ],
        out_specs=pl.BlockSpec((1, 3 * hidden, width), lambda i: (i, 0, 0)),
        out_shape=jax.ShapeDtypeStruct((steps, 3 * hidden, width), BF16),
        compiler_params=pltpu.CompilerParams(vmem_limit_bytes=48 * 1024 * 1024),
        cost_estimate=pl.CostEstimate(
            flops=6 * steps * hidden * width * count,
            bytes_accessed=6 * steps * hidden * (width + count) + 4 * count * width,
            transcendentals=0,
        ),
        name="ffn_grads",
    )(grad_both, activated, rows, grads, earlier)


def done(value):
    first = value[(0,) * value.ndim].astype(F32)
    return (first != first).astype(jnp.int32)


def hold(value, token):
    return jnp.where(token == 0, value, jnp.zeros_like(value))


def flip(value):
    count = lax.axis_size("seq")
    return lax.ppermute(value, "seq", [(i, i ^ 1) for i in range(count)])


def exchange(blocks, axis, groups=None):
    return lax.all_to_all(
        blocks, axis, split_axis=0, concat_axis=0, axis_index_groups=groups, tiled=True
    )


def repeat(value, count):
    return jnp.broadcast_to(value[None], (count,) + value.shape)


def choose(value, index, axis):
    return lax.dynamic_index_in_dim(value, index, axis, keepdims=False)


def per_device_heads(
    dp_count,
    seq_count,
    layer_input,
    positions,
    attn_gain,
    query_down,
    query_gain,
    query_up,
    latent_down,
    latent_gain,
    latent_up,
    output_proj,
    ffn_gain,
    ffn_gate,
    ffn_up,
    ffn_down,
    cotangent,
):
    tokens, width = layer_input.shape
    query_rank = query_down.shape[1]
    own_rows = query_down.shape[0]
    down_width = query_rank + KV_RANK + ROPE
    heads = HEADS // seq_count
    core = lax.axis_index("seq") % 2
    chips = seq_count // 2
    both = ("dp", "seq")
    devices = dp_count * seq_count
    length = seq_count * tokens
    place = lax.axis_index("dp")
    chip = lax.axis_index("seq") // 2
    same_core = [[2 * j + c for j in range(chips)] for c in range(2)]

    def across(value, steps):
        return lax.ppermute(value, "seq", [(i, i ^ (2 * steps)) for i in range(seq_count)])

    def place_in(whole, piece, index, axis):
        return lax.dynamic_update_slice_in_dim(whole, jnp.expand_dims(piece, axis), index, axis)

    def gather_plane(value, token=0, axis=0):
        shape = value.shape[:axis] + (chips,) + value.shape[axis:]
        whole = jnp.zeros(shape, value.dtype)
        for m in range(chips):
            piece = across(value, m) if m else value
            index = chip ^ m if m < chips - 1 else (chip ^ m) + token
            whole = place_in(whole, piece, index, axis)
        return whole

    def with_other_core(mine, axis=1):
        shape = mine.shape[:axis] + (2,) + mine.shape[axis:]
        whole = place_in(jnp.zeros(shape, mine.dtype), mine, core, axis)
        return place_in(whole, flip(mine), 1 - core, axis)

    def gather_seq(value, token=0, axis=0):
        return with_other_core(gather_plane(value, token, axis), axis + 1)

    def scatter_seq(mine, theirs, token=0):
        half = mine.astype(F32) + flip(theirs.astype(BF16)).astype(F32)
        half = half.astype(BF16)
        total = choose(half, chip, 0).astype(F32)
        for m in range(1, chips):
            total = total + across(choose(half, (chip ^ m) + token, 0), m).astype(F32)
        return total

    def gather_z(value):
        whole = jnp.zeros((dp_count,) + value.shape, value.dtype)
        for k, piece in enumerate(gather_dp(value, dp_count)):
            whole = lax.dynamic_update_index_in_dim(whole, piece, (place - k) % dp_count, 0)
        return whole

    def scatter_z(blocks):
        blocks = blocks.astype(BF16)
        total = choose(blocks, place, 0).astype(F32)
        for k in range(1, dp_count):
            block = choose(blocks, (place - k) % dp_count, 0)
            total = total + shift(block, "dp", dp_count, -k).astype(F32)
        return total

    def by_core(value, token=0):
        value = value.reshape(chips, 2, tokens, value.shape[1])
        return choose(value, core, 1), choose(value, 1 - core + token, 1)

    padded_width = down_width + 4 + -(down_width + 4) % HEAD_LANES

    def column(gain):
        return jnp.pad(gain, (0, own_rows - gain.shape[0]))[:, None]

    down_own = jnp.concatenate(
        [
            query_down,
            latent_down,
            column(attn_gain),
            column(ffn_gain),
            column(query_gain),
            column(latent_gain),
            jnp.zeros((own_rows, padded_width - down_width - 4), BF16),
        ],
        1,
    )
    down_plane = gather_z(down_own)
    to_owner = [
        (z * seq_count + s, s * dp_count + z) for z in range(dp_count) for s in range(seq_count)
    ]
    to_group = [(owner, holder) for holder, owner in to_owner]
    up_rows = max(query_up.shape[1], latent_up.shape[1])
    up_packed = jnp.concatenate(
        [
            jnp.pad(query_up.T, ((0, up_rows - query_up.shape[1]), (0, 0))),
            jnp.pad(latent_up.T, ((0, up_rows - latent_up.shape[1]), (0, 0))),
        ],
        1,
    )
    up_moved = lax.ppermute(up_packed, both, to_group)
    up_group = gather_z(hold(up_moved, done(down_plane)))
    proj_moved = lax.ppermute(output_proj, both, to_group)
    proj_group = gather_z(hold(proj_moved, done(up_group))).reshape(-1, width)
    down_full = gather_seq(down_plane, done(up_group), 1).reshape(width, padded_width)
    gains = down_full[:, down_width : down_width + 4].T.astype(F32)
    attn_gain_full = gains[0]
    ffn_gain_full = gains[1]

    def short_gain(row, own):
        return row.reshape(devices, own_rows)[:, : own.shape[0]].reshape(-1)

    query_gain_full = short_gain(gains[2], query_gain)
    latent_gain_full = short_gain(gains[3], latent_gain)

    query_up_padded = jnp.pad(
        up_group[:, : query_up.shape[1], :query_rank].reshape(heads, NOPE + ROPE, query_rank),
        ((0, 0), (0, HEAD_LANES - NOPE - ROPE), (0, 0)),
    ).reshape(heads * HEAD_LANES, query_rank)
    latent_up_group = up_group[:, : latent_up.shape[1], query_rank:].reshape(-1, KV_RANK)

    inputs = layer_input.astype(F32)
    normal_one, inverse_one = norm_parts(inputs)
    normed = (normal_one * attn_gain_full).astype(BF16)
    down_out = jnp.dot(normed, down_full, preferred_element_type=F32)
    normal_query, inverse_query = norm_parts(down_out[:, :query_rank])
    query_normed = (normal_query * query_gain_full).astype(BF16)
    normal_latent, inverse_latent = norm_parts(down_out[:, query_rank : query_rank + KV_RANK])
    latent = (normal_latent * latent_gain_full).astype(BF16)
    cos_table, sin_table = rotary_tables(positions)
    rotary_keys = rotate(
        down_out[:, query_rank + KV_RANK : down_width], cos_table, sin_table
    ).astype(BF16)
    half = ROPE // 2

    def two_parts(table):
        high = table.astype(BF16)
        return [high, (table - high.astype(F32)).astype(BF16)]

    token_message = jnp.concatenate(
        [query_normed, latent, rotary_keys]
        + two_parts(cos_table[:, :half])
        + two_parts(sin_table[:, :half]),
        1,
    )
    token_all = gather_seq(token_message, done(proj_group)).reshape(
        length, token_message.shape[1]
    )
    grad_out = cotangent.astype(F32)
    grad_two = (RESIDUAL_SCALE * grad_out).astype(BF16)
    grad_rows = gather_z(hold(grad_two, done(proj_group))).reshape(-1, width)
    proj_padded = jnp.pad(
        proj_group.reshape(heads, VDIM, width), ((0, 0), (HEAD_LANES - VDIM, 0), (0, 0))
    ).reshape(heads * HEAD_LANES, width)
    ffn_own = hold(jnp.stack([ffn_gate.T, ffn_up.T, ffn_down]), done(down_full))
    ffn_full = lax.all_gather(ffn_own, "seq", axis=1, tiled=True)

    query_normed_all = token_all[:, :query_rank]
    latent_all = token_all[:, query_rank : query_rank + KV_RANK]
    rotary_all = token_all[:, query_rank + KV_RANK : down_width]
    angles = token_all[:, down_width:].astype(F32)
    cos_all = angles[:, :half] + angles[:, half : 2 * half]
    sin_all = angles[:, 2 * half : 3 * half] + angles[:, 3 * half :]

    def lanes(start, values):
        return jnp.pad(values, ((0, 0), (start, HEAD_LANES - start - values.shape[1])))

    tables = (
        jnp.concatenate(
            [
                jnp.ones((length, NOPE), F32),
                cos_all,
                cos_all,
                jnp.zeros((length, HEAD_LANES - NOPE - ROPE), F32),
            ],
            1,
        ),
        lanes(NOPE, -sin_all),
        lanes(NOPE + half, sin_all),
    )
    rotary_lanes = lanes(NOPE, rotary_all)
    projected = dot("tq,kq->tk", query_normed_all, query_up_padded)
    pairs = dot("tc,kc->tk", latent_all, latent_up_group).astype(BF16)
    query, attended, logs = attend(projected, pairs, rotary_lanes, tables)

    attended_mine, attended_theirs = by_core(attended, done(grad_rows))
    branch = scatter_seq(
        dot("mtk,kd->mtd", attended_mine, proj_padded),
        dot("mtk,kd->mtd", attended_theirs, proj_padded),
    )
    middle = inputs + RESIDUAL_SCALE * branch
    normal_two, inverse_two = norm_parts(middle)
    normed_two = (normal_two * ffn_gain_full).astype(BF16)

    normed_rows = gather_z(normed_two).reshape(-1, width)
    proj_full = lax.all_gather(hold(proj_group, done(normed_two)), "seq", axis=0, tiled=True)
    own_hidden = ffn_down.shape[0]
    count = dp_count * tokens
    grad_both, activated = ffn_hidden(ffn_full, normed_rows, grad_rows)
    grad_part = dot("gft,gfd->td", grad_both, ffn_full[:2])
    grad_parts = grad_part.astype(BF16).reshape(dp_count, tokens, width)
    returned = [
        shift(choose(grad_parts, (place - k) % dp_count, 0), "dp", dp_count, -k)
        for k in range(1, dp_count)
    ]
    grad_normed_two = choose(grad_parts, place, 0).astype(F32)
    for piece in returned:
        grad_normed_two = grad_normed_two + piece.astype(F32)
    ffn_sums = lax.psum_scatter(
        ffn_grads(
            grad_both.reshape(2, seq_count, own_hidden, count),
            activated.reshape(seq_count, own_hidden, count),
            normed_rows,
            grad_rows,
            returned[0],
        ),
        "seq",
        scatter_dimension=0,
    ).astype(F32)
    out_part = dot("ft,fd->td", activated, ffn_full[2]).astype(BF16)

    grad_middle_norm, grad_ffn_gain_part = norm_back(
        grad_normed_two, normal_two, inverse_two, ffn_gain_full
    )
    grad_middle = grad_out + grad_middle_norm
    grad_branch = (RESIDUAL_SCALE * grad_middle).astype(BF16)
    grad_attended = dot("td,kd->tk", grad_branch, proj_full).astype(BF16)
    grad_attended = exchange(
        grad_attended.reshape(tokens, seq_count, heads * VDIM).transpose(1, 0, 2), "seq"
    ).reshape(length, heads, VDIM)
    grad_attended = jnp.pad(
        grad_attended, ((0, 0), (0, 0), (HEAD_LANES - VDIM, 0))
    ).reshape(length, heads * HEAD_LANES)
    grad_projected, grad_pairs, grad_rotary = attend_back(
        query, pairs, rotary_lanes, logs, grad_attended, tables
    )
    token_grads = []
    for projected_part, pairs_part, rotary_part in zip(
        by_core(grad_projected), by_core(grad_pairs), by_core(grad_rotary)
    ):
        token_grads.append(
            jnp.concatenate(
                [
                    dot("mtk,kq->mtq", projected_part, query_up_padded).astype(BF16),
                    dot("mtk,kc->mtc", pairs_part, latent_up_group).astype(BF16),
                    rotary_part[:, :, NOPE : NOPE + ROPE].astype(BF16),
                ],
                2,
            )
        )
    branch_plane = gather_plane(grad_branch)
    grad_own = scatter_seq(token_grads[0], token_grads[1], done(branch_plane))
    out_parts = hold(out_part.reshape(dp_count, tokens, width), done(grad_attended))
    out_sum = jnp.sum(exchange(out_parts, "dp").astype(F32), 0)
    layer_output = (middle + RESIDUAL_SCALE * out_sum).astype(BF16)

    query_up_grads = dot("tk,tq->kq", grad_projected, query_normed_all).astype(BF16)
    query_up_grads = query_up_grads.reshape(heads, HEAD_LANES, query_rank)[:, : NOPE + ROPE]
    query_up_grads = query_up_grads.reshape(dp_count, -1, query_rank)
    latent_up_grads = dot("tk,tc->kc", grad_pairs, latent_all).astype(BF16)
    latent_up_grads = latent_up_grads.reshape(dp_count, -1, KV_RANK)
    up_grads = jnp.concatenate(
        [
            jnp.pad(
                query_up_grads, ((0, 0), (0, up_rows - query_up_grads.shape[1]), (0, 0))
            ),
            jnp.pad(
                latent_up_grads, ((0, 0), (0, up_rows - latent_up_grads.shape[1]), (0, 0))
            ),
        ],
        2,
    )
    branch_all = with_other_core(branch_plane)
    proj_grads = dot("tk,td->kd", attended, branch_all.reshape(length, width)).astype(BF16)
    proj_grads = proj_grads.reshape(heads, HEAD_LANES, width)[:, HEAD_LANES - VDIM :]
    group_grads = jnp.concatenate(
        [up_grads, proj_grads.reshape(dp_count, -1, up_grads.shape[2])], 1
    )
    group_sums = jnp.sum(exchange(hold(group_grads, done(grad_own)), "dp").astype(F32), 0)
    group_sums = lax.ppermute(group_sums.astype(BF16), both, to_owner).astype(F32)
    sum_query_up = group_sums[: query_up.shape[1], :query_rank].T
    sum_latent_up = group_sums[: latent_up.shape[1], query_rank:].T
    sum_out = group_sums[up_rows:].reshape(-1, width)

    grad_query_latent, grad_query_gain_part = norm_back(
        grad_own[:, :query_rank], normal_query, inverse_query, query_gain_full
    )
    grad_latent_norm, grad_latent_gain_part = norm_back(
        grad_own[:, query_rank : query_rank + KV_RANK],
        normal_latent,
        inverse_latent,
        latent_gain_full,
    )
    grad_down_out = jnp.concatenate(
        [
            grad_query_latent,
            grad_latent_norm,
            rotate_back(grad_own[:, query_rank + KV_RANK :], cos_table, sin_table),
            jnp.zeros((tokens, padded_width - down_width), F32),
        ],
        -1,
    ).astype(BF16)
    grad_normed = dot("tc,dc->td", grad_down_out, down_full)
    grad_input_norm, grad_attn_gain_part = norm_back(
        grad_normed, normal_one, inverse_one, attn_gain_full
    )
    input_grad = grad_middle + grad_input_norm

    def short_column(grads, own):
        blocks = grads.reshape(devices, own.shape[0])
        return jnp.pad(blocks, ((0, 0), (0, own_rows - own.shape[0]))).reshape(-1)

    gain_columns = jnp.stack(
        [
            grad_attn_gain_part,
            grad_ffn_gain_part,
            short_column(grad_query_gain_part, query_gain),
            short_column(grad_latent_gain_part, latent_gain),
        ],
        1,
    )
    down_sums = dot("td,tc->dc", normed, grad_down_out) + jnp.pad(
        gain_columns, ((0, 0), (down_width, padded_width - down_width - 4))
    )
    down_sums = down_sums.astype(BF16).reshape(dp_count, chips, 2, own_rows, padded_width)
    down_sums = down_sums.transpose(1, 2, 0, 3, 4)
    sum_down = scatter_z(
        scatter_seq(choose(down_sums, core, 1), choose(down_sums, 1 - core, 1))
    )
    sum_gains = sum_down[:, down_width : down_width + 4].T
    return (
        layer_output,
        input_grad,
        sum_gains[0],
        sum_down[:, :query_rank],
        sum_gains[2][: query_gain.shape[0]],
        sum_query_up,
        sum_down[:, query_rank:down_width],
        sum_gains[3][: latent_gain.shape[0]],
        sum_latent_up,
        sum_out,
        sum_gains[1],
        ffn_sums[:own_hidden].T,
        ffn_sums[own_hidden : 2 * own_hidden].T,
        ffn_sums[2 * own_hidden :],
    )


def solution(mesh):
    both = ("dp", "seq")
    dp_count = mesh.shape["dp"]

    seq_count = mesh.shape["seq"]
    by_heads = HEADS % seq_count == 0 and seq_count & (seq_count - 1) == 0

    def run(*arrays):
        if by_heads:
            return per_device_heads(dp_count, seq_count, *arrays)
        return per_device_general(dp_count, *arrays)

    in_specs = (
        P(both, None),
        P(both),
        P(both),
        P(both, None),
        P(both),
        P(None, both),
        P(both, None),
        P(both),
        P(None, both),
        P(both, None),
        P(both),
        P(None, both),
        P(None, both),
        P(both, None),
        P(both, None),
    )
    out_specs = (
        P(both, None),
        P(both, None),
        P(both),
        P(both, None),
        P(both),
        P(None, both),
        P(both, None),
        P(both),
        P(None, both),
        P(both, None),
        P(both),
        P(None, both),
        P(None, both),
        P(both, None),
    )
    return jax.shard_map(run, mesh=mesh, in_specs=in_specs, out_specs=out_specs, check_vma=False)
```

```python
import math

import jax
import jax.numpy as jnp
from jax import lax
from jax.experimental import pallas as pl
from jax.experimental.pallas import tpu as pltpu
from jax.sharding import PartitionSpec as P

KV_RANK = 256
HEADS = 40
NOPE = 64
ROPE = 32
VDIM = 64


EPSILON = 1e-05
RESIDUAL_SCALE = 1.4 / math.sqrt(62.0)
F32 = jnp.float32
BF16 = jnp.bfloat16


def norm_parts(values):
    inverse = lax.rsqrt(jnp.mean(values * values, axis=-1, keepdims=True) + EPSILON)
    return (values * inverse, inverse)


def norm_back(grad_scaled, normalized, inverse, scale_gain):
    gain_grad = jnp.sum(grad_scaled * normalized, axis=0)
    grad_normal = grad_scaled * scale_gain
    values_grad = inverse * (
        grad_normal - normalized * jnp.mean(grad_normal * normalized, axis=-1, keepdims=True)
    )
    return (values_grad, gain_grad)


def rotary_tables(positions):
    half_width = ROPE // 2
    inverse = 10000.0 ** (-2.0 * jnp.arange(half_width, dtype=F32) / ROPE)
    angles = positions.astype(F32)[:, None] * inverse[None, :]
    cos_table = jnp.cos(angles)
    sin_table = jnp.sin(angles)
    return (
        jnp.concatenate([cos_table, cos_table], -1),
        jnp.concatenate([sin_table, sin_table], -1),
    )


def rotate(values, cos_table, sin_table):
    half_width = values.shape[-1] // 2
    turned = jnp.concatenate([-values[..., half_width:], values[..., :half_width]], -1)
    return values * cos_table + turned * sin_table


def rotate_back(grads, cos_table, sin_table):
    half_width = grads.shape[-1] // 2
    scaled = grads * sin_table
    return grads * cos_table + jnp.concatenate(
        [scaled[..., half_width:], -scaled[..., :half_width]], -1
    )


def score_block(query_block, keys_values, rotary_all, allowed):
    score_scale = (NOPE + ROPE) ** (-0.5)
    scores = jnp.einsum(
        "thd,lhd->htl",
        query_block[..., :NOPE],
        keys_values[..., :NOPE],
        preferred_element_type=F32,
    )
    scores = scores + jnp.einsum(
        "thr,lr->htl", query_block[..., NOPE:], rotary_all, preferred_element_type=F32
    )
    return jnp.where(allowed[None], scores * score_scale, -1e30)


def dot(spec, left, right):
    return jnp.einsum(spec, left, right, preferred_element_type=F32)


def shift(value, axis, count, step):
    return lax.ppermute(value, axis, [(i, (i + step) % count) for i in range(count)])


def gather_dp(value, count):
    return [value] + [shift(value, "dp", count, k) for k in range(1, count)]


def scatter_dp(parts, count):
    total = parts[0].astype(F32)
    for k in range(1, count):
        total = total + shift(parts[k].astype(BF16), "dp", count, -k).astype(F32)
    return total


def gather_all(rows, dp_count):
    by_place = jnp.stack(gather_dp(rows, dp_count))
    place = lax.axis_index("dp")
    order = (place - jnp.arange(dp_count)) % dp_count
    absolute = jnp.take(by_place, order, axis=0)
    whole = lax.all_gather(absolute, "seq", axis=1, tiled=True)
    return whole.reshape(-1, rows.shape[1])


def scatter_all(grads, dp_count):
    blocks = grads.astype(BF16).reshape(dp_count, -1, grads.shape[1])
    own_seq = lax.psum_scatter(blocks, "seq", scatter_dimension=1, tiled=True)
    place = lax.axis_index("dp")
    parts = [
        lax.dynamic_index_in_dim(own_seq, (place - k) % dp_count, 0, keepdims=False)
        for k in range(dp_count)
    ]
    return scatter_dp(parts, dp_count)


def per_device_general(
    dp_count,
    layer_input,
    positions,
    attn_gain,
    query_down,
    query_gain,
    query_up,
    latent_down,
    latent_gain,
    latent_up,
    output_proj,
    ffn_gain,
    ffn_gate,
    ffn_up,
    ffn_down,
    cotangent,
):
    token_count, width = layer_input.shape
    query_rank = query_down.shape[1]
    own_rows = query_down.shape[0]
    score_scale = (NOPE + ROPE) ** (-0.5)

    def column(gain):
        return jnp.pad(gain, (0, own_rows - gain.shape[0]))[:, None]

    down_width = query_rank + KV_RANK + ROPE
    pad_width = -(down_width + 4) % 128
    packed = jnp.concatenate(
        [
            query_down,
            latent_down,
            column(attn_gain),
            column(ffn_gain),
            column(query_gain),
            column(latent_gain),
            jnp.zeros((own_rows, pad_width), BF16),
        ],
        1,
    )
    packed_full = gather_all(packed, dp_count)
    down_full = packed_full[:, :down_width]
    gains = packed_full[:, down_width : down_width + 4].T.astype(F32)
    attn_gain_full = gains[0]
    ffn_gain_full = gains[1]

    def short_gain(row, own):
        return row.reshape(-1, own_rows)[:, : own.shape[0]].reshape(-1)

    query_gain_full = short_gain(gains[2], query_gain)
    latent_gain_full = short_gain(gains[3], latent_gain)

    query_up_full = gather_all(query_up.T, dp_count)
    latent_up_full = gather_all(latent_up.T, dp_count)
    proj_full = gather_all(output_proj, dp_count)
    gate_full = lax.all_gather(ffn_gate.T, "seq", axis=0, tiled=True)
    upward_full = lax.all_gather(ffn_up.T, "seq", axis=0, tiled=True)
    ffn_down_full = lax.all_gather(ffn_down, "seq", axis=0, tiled=True)

    grad_out = cotangent.astype(F32)
    grad_two = (RESIDUAL_SCALE * grad_out).astype(BF16)
    grad_rows = jnp.concatenate(gather_dp(grad_two, dp_count))

    inputs = layer_input.astype(F32)
    cos_table, sin_table = rotary_tables(positions)
    normal_one, inverse_one = norm_parts(inputs)
    normed = (normal_one * attn_gain_full).astype(BF16)
    down_out = jnp.dot(normed, down_full, preferred_element_type=F32)
    query_latent = down_out[:, :query_rank]
    compressed = down_out[:, query_rank:]
    normal_latent, inverse_latent = norm_parts(compressed[:, :KV_RANK])
    latent = (normal_latent * latent_gain_full).astype(BF16)
    rotary_keys = rotate(compressed[:, KV_RANK:], cos_table, sin_table).astype(BF16)
    keys_all = lax.all_gather(
        jnp.concatenate([latent, rotary_keys], -1), "seq", axis=0, tiled=True
    )
    latent_all = keys_all[:, :KV_RANK]
    rotary_all = keys_all[:, KV_RANK:]
    normal_query, inverse_query = norm_parts(query_latent)
    query_normed = (normal_query * query_gain_full).astype(BF16)
    projected = dot("tq,kq->tk", query_normed, query_up_full).reshape(
        token_count, HEADS, NOPE + ROPE
    )
    queries = jnp.concatenate(
        [
            projected[..., :NOPE],
            rotate(projected[..., NOPE:], cos_table[:, None, :], sin_table[:, None, :]),
        ],
        -1,
    ).astype(BF16)
    key_count = latent_all.shape[0]
    head_group = math.gcd(HEADS, 8)
    group_count = HEADS // head_group
    first_row = lax.axis_index("seq") * token_count
    allowed = (first_row + jnp.arange(token_count))[:, None] >= jnp.arange(key_count)[None, :]
    up_grouped = latent_up_full.reshape(group_count, head_group * (NOPE + VDIM), KV_RANK)
    query_grouped = queries.reshape(token_count, group_count, head_group, NOPE + ROPE).transpose(
        1, 0, 2, 3
    )

    def forward_group(operands):
        query_block, up_block = operands
        keys_values = dot("lc,kc->lk", latent_all, up_block).astype(BF16)
        keys_values = keys_values.reshape(key_count, head_group, NOPE + VDIM)
        scores = score_block(query_block, keys_values, rotary_all, allowed)
        row_peak = jnp.max(scores, axis=-1, keepdims=True)
        exponent_terms = jnp.exp(scores - row_peak)
        row_totals = jnp.sum(exponent_terms, axis=-1, keepdims=True)
        probabilities = (exponent_terms / row_totals).astype(BF16)
        attended_block = dot("htl,lhv->thv", probabilities, keys_values[..., NOPE:])
        return (keys_values, attended_block, (row_peak + jnp.log(row_totals))[..., 0])

    kept_values, attended_grouped, log_totals = lax.map(forward_group, (query_grouped, up_grouped))
    attended_low = (
        attended_grouped.transpose(1, 0, 2, 3).reshape(token_count, HEADS * VDIM).astype(BF16)
    )
    branch = jnp.dot(attended_low, proj_full, preferred_element_type=F32)
    middle = inputs + RESIDUAL_SCALE * branch
    normal_two, inverse_two = norm_parts(middle)
    normed_two = (normal_two * ffn_gain_full).astype(BF16)

    normed_rows = jnp.concatenate(gather_dp(normed_two, dp_count))
    gate_values = dot("td,fd->tf", normed_rows, gate_full)
    upward = dot("td,fd->tf", normed_rows, upward_full)
    grad_activated = dot("td,fd->tf", grad_rows, ffn_down_full)
    sigmoid_gate = jax.nn.sigmoid(gate_values)
    activated = (gate_values * sigmoid_gate * upward).astype(BF16)
    grad_upward = (grad_activated * gate_values * sigmoid_gate).astype(BF16)
    grad_gate = (
        grad_activated * upward * sigmoid_gate * (1.0 + gate_values * (1.0 - sigmoid_gate))
    ).astype(BF16)
    grad_normed_part = dot("tf,fd->td", grad_gate, gate_full) + dot(
        "tf,fd->td", grad_upward, upward_full
    )
    grad_normed_two = scatter_dp(jnp.split(grad_normed_part, dp_count), dp_count)
    down_part = dot("tf,fd->td", activated, ffn_down_full)
    layer_output = (
        middle + RESIDUAL_SCALE * scatter_dp(jnp.split(down_part, dp_count), dp_count)
    ).astype(BF16)

    def scatter_seq(grads):
        return lax.psum_scatter(
            grads.astype(BF16), "seq", scatter_dimension=0, tiled=True
        ).astype(F32)

    sum_down = scatter_seq(dot("tf,td->fd", activated, grad_rows))
    sum_gate = scatter_seq(dot("tf,td->fd", grad_gate, normed_rows)).T
    sum_up = scatter_seq(dot("tf,td->fd", grad_upward, normed_rows)).T

    grad_middle_norm, grad_ffn_gain_part = norm_back(
        grad_normed_two, normal_two, inverse_two, ffn_gain_full
    )
    grad_middle = grad_out + grad_middle_norm
    grad_branch = (RESIDUAL_SCALE * grad_middle).astype(BF16)
    sum_out = scatter_all(dot("tk,td->kd", attended_low, grad_branch), dp_count)
    grad_attended = dot("td,kd->tk", grad_branch, proj_full).astype(BF16)
    grad_att_grouped = grad_attended.reshape(token_count, group_count, head_group, VDIM).transpose(
        1, 0, 2, 3
    )

    def backward_group(carried, operands):
        latent_sum, rotary_sum = carried
        query_block, keys_values, log_block, grad_att, attended_block, up_block = operands
        scores = score_block(query_block, keys_values, rotary_all, allowed)
        probabilities = jnp.exp(scores - log_block[..., None])
        grad_probs = dot("thv,lhv->htl", grad_att, keys_values[..., NOPE:])
        row_delta = jnp.sum(grad_att.astype(F32) * attended_block, axis=-1)
        grad_scores = (probabilities * (grad_probs - jnp.transpose(row_delta)[..., None])).astype(
            BF16
        )
        grad_query_nope = dot("htl,lhd->thd", grad_scores, keys_values[..., :NOPE]) * score_scale
        grad_query_rot = dot("htl,lr->thr", grad_scores, rotary_all) * score_scale
        grad_keys = dot("htl,thd->lhd", grad_scores, query_block[..., :NOPE]) * score_scale
        grad_rotary_part = dot("htl,thr->lr", grad_scores, query_block[..., NOPE:]) * score_scale
        grad_values = dot("htl,thv->lhv", probabilities.astype(BF16), grad_att)
        grad_pairs = (
            jnp.concatenate([grad_keys, grad_values], -1)
            .astype(BF16)
            .reshape(key_count, head_group * (NOPE + VDIM))
        )
        grad_up_block = dot("lk,lc->kc", grad_pairs, latent_all)
        latent_sum = latent_sum + dot("lk,kc->lc", grad_pairs, up_block)
        return (
            (latent_sum, rotary_sum + grad_rotary_part),
            (jnp.concatenate([grad_query_nope, grad_query_rot], -1), grad_up_block),
        )

    start_sums = (
        jnp.zeros((key_count, KV_RANK), F32),
        jnp.zeros((key_count, ROPE), F32),
    )
    (grad_latent_all, grad_rotary_all), (grad_query_grouped, grad_up_grouped) = lax.scan(
        backward_group,
        start_sums,
        (query_grouped, kept_values, log_totals, grad_att_grouped, attended_grouped, up_grouped),
    )
    sum_latent_up = scatter_all(
        grad_up_grouped.reshape(HEADS * (NOPE + VDIM), KV_RANK), dp_count
    ).T
    grad_keys_own = lax.psum_scatter(
        jnp.concatenate([grad_latent_all, grad_rotary_all], -1).astype(BF16),
        "seq",
        scatter_dimension=0,
        tiled=True,
    ).astype(F32)
    grad_latent_own = grad_keys_own[:, :KV_RANK]
    grad_rotary_own = grad_keys_own[:, KV_RANK:]
    grad_queries = grad_query_grouped.transpose(1, 0, 2, 3).reshape(token_count, HEADS, NOPE + ROPE)
    grad_projected = jnp.concatenate(
        [
            grad_queries[..., :NOPE],
            rotate_back(grad_queries[..., NOPE:], cos_table[:, None, :], sin_table[:, None, :]),
        ],
        -1,
    )
    grad_projected = grad_projected.astype(BF16).reshape(token_count, HEADS * (NOPE + ROPE))
    sum_query_up = scatter_all(dot("tk,tq->kq", grad_projected, query_normed), dp_count).T
    grad_query_normed = dot("tk,kq->tq", grad_projected, query_up_full)
    grad_query_latent, grad_query_gain_part = norm_back(
        grad_query_normed, normal_query, inverse_query, query_gain_full
    )
    grad_latent_norm, grad_latent_gain_part = norm_back(
        grad_latent_own, normal_latent, inverse_latent, latent_gain_full
    )
    grad_down_out = jnp.concatenate(
        [
            grad_query_latent,
            grad_latent_norm,
            rotate_back(grad_rotary_own, cos_table, sin_table),
        ],
        -1,
    ).astype(BF16)
    grad_down_part = dot("td,tc->dc", normed, grad_down_out)
    grad_normed = dot("tc,dc->td", grad_down_out, down_full)
    grad_input_norm, grad_attn_gain_part = norm_back(
        grad_normed, normal_one, inverse_one, attn_gain_full
    )
    input_grad = grad_middle + grad_input_norm

    def short_column(grads, own):
        blocks = grads.reshape(-1, own.shape[0])
        return jnp.pad(blocks, ((0, 0), (0, own_rows - own.shape[0]))).reshape(-1)

    gain_columns = jnp.stack(
        [
            grad_attn_gain_part,
            grad_ffn_gain_part,
            short_column(grad_query_gain_part, query_gain),
            short_column(grad_latent_gain_part, latent_gain),
        ],
        1,
    )
    sum_packed = scatter_all(
        jnp.concatenate([grad_down_part, gain_columns, jnp.zeros((width, pad_width), F32)], 1),
        dp_count,
    )
    sum_gains = sum_packed[:, down_width : down_width + 4].T
    return (
        layer_output,
        input_grad,
        sum_gains[0],
        sum_packed[:, :query_rank],
        sum_gains[2][: query_gain.shape[0]],
        sum_query_up,
        sum_packed[:, query_rank:down_width],
        sum_gains[3][: latent_gain.shape[0]],
        sum_latent_up,
        sum_out,
        sum_gains[1],
        sum_gate,
        sum_up,
        sum_down,
    )


HEAD_LANES = 128
SCORE_SCALE = (NOPE + ROPE) ** (-0.5)
QUERY_BLOCK = 256


def head_keys(pairs, rotary):
    lane = lax.broadcasted_iota(jnp.int32, pairs.shape, 1)
    return jnp.where(lane < NOPE, pairs, rotary)


def block_scores(query, keys, start):
    scores = lax.dot_general(
        query, keys, (((1,), (1,)), ((), ())), preferred_element_type=F32
    )
    row = start + lax.broadcasted_iota(jnp.int32, scores.shape, 0)
    column = lax.broadcasted_iota(jnp.int32, scores.shape, 1)
    return jnp.where(row >= column, scores * SCORE_SCALE, -1e30)


def turn(values, cos_ref, left_ref, right_ref, sign):
    half = ROPE // 2
    return (
        values * cos_ref
        + sign * (pltpu.roll(values, HEAD_LANES - half, 1) * left_ref)
        + sign * (pltpu.roll(values, half, 1) * right_ref)
    )


def attend_kernel(
    projected_ref, pairs_ref, rotary_ref, cos_ref, left_ref, right_ref,
    query_ref, attended_ref, log_ref, keys_ref,
):
    length = projected_ref.shape[0]
    block = min(QUERY_BLOCK, length)
    keys_ref[...] = head_keys(pairs_ref[...], rotary_ref[...])
    for start in range(0, length, block):
        rows = pl.ds(start, block)
        stop = start + block
        query = turn(
            projected_ref[rows, :], cos_ref[rows, :], left_ref[rows, :], right_ref[rows, :], 1.0
        ).astype(BF16)
        query_ref[rows, :] = query
        scores = block_scores(query, keys_ref[0:stop, :], start)
        peak = jnp.max(scores, axis=-1, keepdims=True)
        terms = jnp.exp(scores - peak)
        totals = jnp.sum(terms, axis=-1, keepdims=True)
        probs = (terms / totals).astype(BF16)
        mixed = jnp.dot(probs, pairs_ref[0:stop, :], preferred_element_type=F32)
        lane = lax.broadcasted_iota(jnp.int32, mixed.shape, 1)
        attended_ref[rows, :] = jnp.where(lane >= NOPE, mixed, 0.0).astype(BF16)
        log_ref[rows, :] = jnp.broadcast_to(peak + jnp.log(totals), mixed.shape)


def attend(projected, pairs, rotary, tables):
    length, lanes = projected.shape
    own = pl.BlockSpec((length, HEAD_LANES), lambda h: (0, h))
    shared = pl.BlockSpec((length, HEAD_LANES), lambda h: (0, 0))
    return pl.pallas_call(
        attend_kernel,
        grid=(lanes // HEAD_LANES,),
        in_specs=[own, own, shared, shared, shared, shared],
        out_specs=[own, own, own],
        out_shape=[
            jax.ShapeDtypeStruct((length, lanes), BF16),
            jax.ShapeDtypeStruct((length, lanes), BF16),
            jax.ShapeDtypeStruct((length, lanes), F32),
        ],
        scratch_shapes=[pltpu.VMEM((length, HEAD_LANES), BF16)],
        compiler_params=pltpu.CompilerParams(vmem_limit_bytes=40 * 1024 * 1024),
        cost_estimate=pl.CostEstimate(
            flops=3 * lanes * length * length, bytes_accessed=12 * lanes * length,
            transcendentals=length * length * lanes // HEAD_LANES,
        ),
        name="attend",
    )(projected, pairs, rotary, *tables)


def attend_back_kernel(
    query_ref, pairs_ref, rotary_ref, log_ref, grad_ref, cos_ref, left_ref, right_ref,
    earlier_ref, grad_query_ref, grad_pairs_ref, grad_rotary_ref, keys_ref, grad_keys_ref, grad_values_ref,
):
    length = query_ref.shape[0]
    block = min(QUERY_BLOCK, length)
    keys_ref[...] = head_keys(pairs_ref[...], rotary_ref[...])
    grad_keys_ref[...] = jnp.zeros_like(grad_keys_ref)
    grad_values_ref[...] = jnp.zeros_like(grad_values_ref)
    for start in range(0, length, block):
        rows = pl.ds(start, block)
        stop = start + block
        query = query_ref[rows, :]
        grad = grad_ref[rows, :]
        scores = block_scores(query, keys_ref[0:stop, :], start)
        probs = jnp.exp(scores - log_ref[rows, 0:1])
        grad_probs = lax.dot_general(
            grad, pairs_ref[0:stop, :], (((1,), (1,)), ((), ())), preferred_element_type=F32
        )
        delta = jnp.sum(probs * grad_probs, axis=-1, keepdims=True)
        grad_scores = (probs * (grad_probs - delta)).astype(BF16)
        grad_query = (
            jnp.dot(grad_scores, keys_ref[0:stop, :], preferred_element_type=F32) * SCORE_SCALE
        )
        grad_query_ref[rows, :] = turn(
            grad_query, cos_ref[rows, :], left_ref[rows, :], right_ref[rows, :], -1.0
        ).astype(BF16)
        grad_keys_ref[:, 0:stop] += jnp.dot(
            query.T, grad_scores, preferred_element_type=F32
        )
        grad_values_ref[:, 0:stop] += jnp.dot(
            grad.T, probs.astype(BF16), preferred_element_type=F32
        )
    grad_keys = grad_keys_ref[...].T * SCORE_SCALE
    lane = lax.broadcasted_iota(jnp.int32, grad_keys.shape, 1)
    grad_pairs_ref[...] = jnp.where(lane < NOPE, grad_keys, grad_values_ref[...].T).astype(BF16)

    @pl.when(pl.program_id(0) == 0)
    def _():
        grad_rotary_ref[...] = jnp.zeros_like(grad_rotary_ref)

    grad_rotary_ref[...] += grad_keys


def attend_back(query, pairs, rotary, logs, grad, tables, earlier):
    length, lanes = query.shape
    own = pl.BlockSpec((length, HEAD_LANES), lambda h: (0, h))
    shared = pl.BlockSpec((length, HEAD_LANES), lambda h: (0, 0))
    return pl.pallas_call(
        attend_back_kernel,
        grid=(lanes // HEAD_LANES,),
        in_specs=[own, own, shared, own, own, shared, shared, shared]
        + [pl.BlockSpec(memory_space=pl.ANY)],
        out_specs=[own, own, shared],
        out_shape=[
            jax.ShapeDtypeStruct((length, lanes), BF16),
            jax.ShapeDtypeStruct((length, lanes), BF16),
            jax.ShapeDtypeStruct((length, HEAD_LANES), F32),
        ],
        scratch_shapes=[
            pltpu.VMEM((length, HEAD_LANES), BF16),
            pltpu.VMEM((HEAD_LANES, length), F32),
            pltpu.VMEM((HEAD_LANES, length), F32),
        ],
        compiler_params=pltpu.CompilerParams(vmem_limit_bytes=48 * 1024 * 1024),
        cost_estimate=pl.CostEstimate(
            flops=8 * lanes * length * length, bytes_accessed=14 * lanes * length,
            transcendentals=length * length * lanes // HEAD_LANES,
        ),
        name="attend_back",
    )(query, pairs, rotary, logs, grad, *tables, earlier)


def ffn_kernel(weights_ref, rows_ref, grads_ref, both_ref, act_ref):
    def against(index, rows):
        return lax.dot_general(
            weights_ref[index], rows[...], (((1,), (1,)), ((), ())), preferred_element_type=F32
        )

    gate_values = against(0, rows_ref)
    upward = against(1, rows_ref)
    grad_activated = against(2, grads_ref)
    sigmoid_gate = jax.nn.sigmoid(gate_values)
    swish = gate_values * sigmoid_gate
    act_ref[...] = (swish * upward).astype(BF16)
    both_ref[1] = (grad_activated * swish).astype(BF16)
    both_ref[0] = (
        grad_activated * upward * sigmoid_gate * (1.0 + gate_values * (1.0 - sigmoid_gate))
    ).astype(BF16)


def ffn_hidden(weights, rows, grads):
    _, hidden, width = weights.shape
    count = rows.shape[0]
    block = hidden // 4
    whole = pl.BlockSpec(memory_space=pltpu.VMEM)
    own = pl.BlockSpec((block, count), lambda i: (i, 0))
    return pl.pallas_call(
        ffn_kernel,
        grid=(hidden // block,),
        in_specs=[pl.BlockSpec((3, block, width), lambda i: (0, i, 0)), whole, whole],
        out_specs=[pl.BlockSpec((2, block, count), lambda i: (0, i, 0)), own],
        out_shape=[
            jax.ShapeDtypeStruct((2, hidden, count), BF16),
            jax.ShapeDtypeStruct((hidden, count), BF16),
        ],
        compiler_params=pltpu.CompilerParams(vmem_limit_bytes=48 * 1024 * 1024),
        cost_estimate=pl.CostEstimate(
            flops=6 * hidden * width * count,
            bytes_accessed=6 * hidden * (width + count) + 4 * count * width,
            transcendentals=hidden * count,
        ),
        name="ffn_hidden",
    )(weights, rows, grads)


def ffn_grads_kernel(both_ref, act_ref, rows_ref, grads_ref, earlier_ref, out_ref):
    hidden = act_ref.shape[1]
    parts = ((both_ref[0, 0], rows_ref), (both_ref[1, 0], rows_ref), (act_ref[0], grads_ref))
    for place, (left, right) in enumerate(parts):
        out_ref[0, place * hidden : (place + 1) * hidden, :] = jnp.dot(
            left, right[...], preferred_element_type=F32
        ).astype(BF16)


def ffn_grads(grad_both, activated, rows, grads, earlier):
    steps, hidden, count = activated.shape
    width = rows.shape[1]
    whole = pl.BlockSpec(memory_space=pltpu.VMEM)
    own = pl.BlockSpec((1, hidden, count), lambda i: (i, 0, 0))
    return pl.pallas_call(
        ffn_grads_kernel,
        grid=(steps,),
        in_specs=[
            pl.BlockSpec((2, 1, hidden, count), lambda i: (0, i, 0, 0)),
            own,
            whole,
            whole,
            pl.BlockSpec(memory_space=pl.ANY),
        ],
        out_specs=pl.BlockSpec((1, 3 * hidden, width), lambda i: (i, 0, 0)),
        out_shape=jax.ShapeDtypeStruct((steps, 3 * hidden, width), BF16),
        compiler_params=pltpu.CompilerParams(vmem_limit_bytes=48 * 1024 * 1024),
        cost_estimate=pl.CostEstimate(
            flops=6 * steps * hidden * width * count,
            bytes_accessed=6 * steps * hidden * (width + count) + 4 * count * width,
            transcendentals=0,
        ),
        name="ffn_grads",
    )(grad_both, activated, rows, grads, earlier)


def done(value):
    first = value[(0,) * value.ndim].astype(F32)
    return (first != first).astype(jnp.int32)


def hold(value, token):
    return jnp.where(token == 0, value, jnp.zeros_like(value))


def flip(value):
    count = lax.axis_size("seq")
    return lax.ppermute(value, "seq", [(i, i ^ 1) for i in range(count)])


def exchange(blocks, axis, groups=None):
    return lax.all_to_all(
        blocks, axis, split_axis=0, concat_axis=0, axis_index_groups=groups, tiled=True
    )


def repeat(value, count):
    return jnp.broadcast_to(value[None], (count,) + value.shape)


def choose(value, index, axis):
    return lax.dynamic_index_in_dim(value, index, axis, keepdims=False)


def per_device_heads(
    dp_count,
    seq_count,
    layer_input,
    positions,
    attn_gain,
    query_down,
    query_gain,
    query_up,
    latent_down,
    latent_gain,
    latent_up,
    output_proj,
    ffn_gain,
    ffn_gate,
    ffn_up,
    ffn_down,
    cotangent,
):
    tokens, width = layer_input.shape
    query_rank = query_down.shape[1]
    own_rows = query_down.shape[0]
    down_width = query_rank + KV_RANK + ROPE
    heads = HEADS // seq_count
    core = lax.axis_index("seq") % 2
    chips = seq_count // 2
    both = ("dp", "seq")
    devices = dp_count * seq_count
    length = seq_count * tokens
    place = lax.axis_index("dp")
    chip = lax.axis_index("seq") // 2
    same_core = [[2 * j + c for j in range(chips)] for c in range(2)]

    def across(value, steps):
        return lax.ppermute(value, "seq", [(i, i ^ (2 * steps)) for i in range(seq_count)])

    def place_in(whole, piece, index, axis):
        return lax.dynamic_update_slice_in_dim(whole, jnp.expand_dims(piece, axis), index, axis)

    def gather_plane(value, token=0, axis=0):
        shape = value.shape[:axis] + (chips,) + value.shape[axis:]
        whole = jnp.zeros(shape, value.dtype)
        for m in range(chips):
            piece = across(value, m) if m else value
            index = chip ^ m if m < chips - 1 else (chip ^ m) + token
            whole = place_in(whole, piece, index, axis)
        return whole

    def with_other_core(mine, axis=1):
        shape = mine.shape[:axis] + (2,) + mine.shape[axis:]
        whole = place_in(jnp.zeros(shape, mine.dtype), mine, core, axis)
        return place_in(whole, flip(mine), 1 - core, axis)

    def gather_seq(value, token=0, axis=0):
        return with_other_core(gather_plane(value, token, axis), axis + 1)

    def scatter_seq(mine, theirs, token=0):
        half = mine.astype(F32) + flip(theirs.astype(BF16)).astype(F32)
        half = half.astype(BF16)
        total = choose(half, chip, 0).astype(F32)
        for m in range(1, chips):
            total = total + across(choose(half, (chip ^ m) + token, 0), m).astype(F32)
        return total

    def gather_z(value):
        whole = jnp.zeros((dp_count,) + value.shape, value.dtype)
        for k, piece in enumerate(gather_dp(value, dp_count)):
            whole = lax.dynamic_update_index_in_dim(whole, piece, (place - k) % dp_count, 0)
        return whole

    def scatter_z(blocks):
        blocks = blocks.astype(BF16)
        total = choose(blocks, place, 0).astype(F32)
        for k in range(1, dp_count):
            block = choose(blocks, (place - k) % dp_count, 0)
            total = total + shift(block, "dp", dp_count, -k).astype(F32)
        return total

    def by_core(value, token=0):
        value = value.reshape(chips, 2, tokens, value.shape[1])
        return choose(value, core, 1), choose(value, 1 - core + token, 1)

    padded_width = down_width + 4 + -(down_width + 4) % HEAD_LANES

    def column(gain):
        return jnp.pad(gain, (0, own_rows - gain.shape[0]))[:, None]

    down_own = jnp.concatenate(
        [
            query_down,
            latent_down,
            column(attn_gain),
            column(ffn_gain),
            column(query_gain),
            column(latent_gain),
            jnp.zeros((own_rows, padded_width - down_width - 4), BF16),
        ],
        1,
    )
    down_plane = gather_z(down_own)
    group_of = [s if s % 2 == 0 else (s + 2) % seq_count for s in range(seq_count)]
    to_owner = [
        (z * seq_count + s, group_of[s] * dp_count + z)
        for z in range(dp_count)
        for s in range(seq_count)
    ]
    to_group = [(owner, holder) for holder, owner in to_owner]
    up_rows = max(query_up.shape[1], latent_up.shape[1])
    up_packed = jnp.concatenate(
        [
            jnp.pad(query_up.T, ((0, up_rows - query_up.shape[1]), (0, 0))),
            jnp.pad(latent_up.T, ((0, up_rows - latent_up.shape[1]), (0, 0))),
        ],
        1,
    )
    up_moved = lax.ppermute(up_packed, both, to_group)
    up_group = gather_z(hold(up_moved, done(down_plane)))
    down_full = gather_seq(down_plane, done(up_group), 1).reshape(width, padded_width)
    gains = down_full[:, down_width : down_width + 4].T.astype(F32)
    attn_gain_full = gains[0]
    ffn_gain_full = gains[1]

    def short_gain(row, own):
        return row.reshape(devices, own_rows)[:, : own.shape[0]].reshape(-1)

    query_gain_full = short_gain(gains[2], query_gain)
    latent_gain_full = short_gain(gains[3], latent_gain)

    query_up_padded = jnp.pad(
        up_group[:, : query_up.shape[1], :query_rank].reshape(heads, NOPE + ROPE, query_rank),
        ((0, 0), (0, HEAD_LANES - NOPE - ROPE), (0, 0)),
    ).reshape(heads * HEAD_LANES, query_rank)
    latent_up_group = up_group[:, : latent_up.shape[1], query_rank:].reshape(-1, KV_RANK)

    inputs = layer_input.astype(F32)
    normal_one, inverse_one = norm_parts(inputs)
    normed = (normal_one * attn_gain_full).astype(BF16)
    down_out = jnp.dot(normed, down_full, preferred_element_type=F32)
    normal_query, inverse_query = norm_parts(down_out[:, :query_rank])
    query_normed = (normal_query * query_gain_full).astype(BF16)
    normal_latent, inverse_latent = norm_parts(down_out[:, query_rank : query_rank + KV_RANK])
    latent = (normal_latent * latent_gain_full).astype(BF16)
    cos_table, sin_table = rotary_tables(positions)
    rotary_keys = rotate(
        down_out[:, query_rank + KV_RANK : down_width], cos_table, sin_table
    ).astype(BF16)
    half = ROPE // 2

    def two_parts(table):
        high = table.astype(BF16)
        return [high, (table - high.astype(F32)).astype(BF16)]

    token_message = jnp.concatenate(
        [query_normed, latent, rotary_keys]
        + two_parts(cos_table[:, :half])
        + two_parts(sin_table[:, :half]),
        1,
    )
    proj_moved = lax.ppermute(output_proj, both, to_group)
    proj_group = gather_z(hold(proj_moved, done(token_message))).reshape(-1, width)
    token_all = gather_seq(token_message, done(proj_group)).reshape(
        length, token_message.shape[1]
    )
    grad_out = cotangent.astype(F32)
    grad_two = (RESIDUAL_SCALE * grad_out).astype(BF16)
    grad_rows = gather_z(hold(grad_two, done(proj_group))).reshape(-1, width)
    proj_padded = jnp.pad(
        proj_group.reshape(heads, VDIM, width), ((0, 0), (HEAD_LANES - VDIM, 0), (0, 0))
    ).reshape(heads * HEAD_LANES, width)
    ffn_own = hold(jnp.stack([ffn_gate.T, ffn_up.T, ffn_down]), done(down_full))
    ffn_full = lax.all_gather(ffn_own, "seq", axis=1, tiled=True)

    query_normed_all = token_all[:, :query_rank]
    latent_all = token_all[:, query_rank : query_rank + KV_RANK]
    rotary_all = token_all[:, query_rank + KV_RANK : down_width]
    angles = token_all[:, down_width:].astype(F32)
    cos_all = angles[:, :half] + angles[:, half : 2 * half]
    sin_all = angles[:, 2 * half : 3 * half] + angles[:, 3 * half :]

    def lanes(start, values):
        return jnp.pad(values, ((0, 0), (start, HEAD_LANES - start - values.shape[1])))

    tables = (
        jnp.concatenate(
            [
                jnp.ones((length, NOPE), F32),
                cos_all,
                cos_all,
                jnp.zeros((length, HEAD_LANES - NOPE - ROPE), F32),
            ],
            1,
        ),
        lanes(NOPE, -sin_all),
        lanes(NOPE + half, sin_all),
    )
    rotary_lanes = lanes(NOPE, rotary_all)
    projected = dot("tq,kq->tk", query_normed_all, query_up_padded)
    pairs = dot("tc,kc->tk", latent_all, latent_up_group).astype(BF16)
    query, attended, logs = attend(projected, pairs, rotary_lanes, tables)

    attended_mine, attended_theirs = by_core(attended)
    branch = scatter_seq(
        dot("mtk,kd->mtd", attended_mine, proj_padded),
        dot("mtk,kd->mtd", attended_theirs, proj_padded),
    )
    middle = inputs + RESIDUAL_SCALE * branch
    normal_two, inverse_two = norm_parts(middle)
    normed_two = hold((normal_two * ffn_gain_full).astype(BF16), done(grad_rows))

    normed_rows = gather_z(normed_two).reshape(-1, width)
    proj_full = lax.all_gather(hold(proj_group, done(normed_two)), "seq", axis=0, tiled=True)
    own_hidden = ffn_down.shape[0]
    count = dp_count * tokens
    grad_both, activated = ffn_hidden(ffn_full, normed_rows, grad_rows)
    grad_part = dot("gft,gfd->td", grad_both, ffn_full[:2])
    grad_parts = grad_part.astype(BF16).reshape(dp_count, tokens, width)
    returned = [
        shift(choose(grad_parts, (place - k) % dp_count, 0), "dp", dp_count, -k)
        for k in range(1, dp_count)
    ]
    grad_normed_two = choose(grad_parts, place, 0).astype(F32)
    for piece in returned:
        grad_normed_two = grad_normed_two + piece.astype(F32)
    out_part = dot("ft,fd->td", activated, ffn_full[2]).astype(BF16)

    grad_middle_norm, grad_ffn_gain_part = norm_back(
        grad_normed_two, normal_two, inverse_two, ffn_gain_full
    )
    grad_middle = grad_out + grad_middle_norm
    grad_branch = (RESIDUAL_SCALE * grad_middle).astype(BF16)
    grad_attended = dot("td,kd->tk", grad_branch, proj_full).astype(BF16)
    ffn_sums = lax.psum_scatter(
        ffn_grads(
            grad_both.reshape(2, seq_count, own_hidden, count),
            activated.reshape(seq_count, own_hidden, count),
            normed_rows,
            grad_rows,
            grad_attended,
        ),
        "seq",
        scatter_dimension=0,
    ).astype(F32)
    grad_attended = exchange(
        grad_attended.reshape(tokens, seq_count, heads * VDIM).transpose(1, 0, 2), "seq"
    ).reshape(length, heads, VDIM)
    grad_attended = jnp.pad(
        grad_attended, ((0, 0), (0, 0), (HEAD_LANES - VDIM, 0))
    ).reshape(length, heads * HEAD_LANES)
    grad_projected, grad_pairs, grad_rotary = attend_back(
        query, pairs, rotary_lanes, logs, grad_attended, tables, out_part
    )
    token_grads = []
    for projected_part, pairs_part, rotary_part in zip(
        by_core(grad_projected), by_core(grad_pairs), by_core(grad_rotary)
    ):
        token_grads.append(
            jnp.concatenate(
                [
                    dot("mtk,kq->mtq", projected_part, query_up_padded).astype(BF16),
                    dot("mtk,kc->mtc", pairs_part, latent_up_group).astype(BF16),
                    rotary_part[:, :, NOPE : NOPE + ROPE].astype(BF16),
                ],
                2,
            )
        )
    branch_plane = gather_plane(grad_branch)
    grad_own = scatter_seq(token_grads[0], token_grads[1], done(branch_plane))
    out_parts = hold(out_part.reshape(dp_count, tokens, width), done(grad_attended))
    out_sum = jnp.sum(exchange(out_parts, "dp").astype(F32), 0)
    layer_output = (middle + RESIDUAL_SCALE * out_sum).astype(BF16)

    home = done(grad_own)
    query_up_grads = dot("tk,tq->kq", hold(grad_projected, home), query_normed_all).astype(BF16)
    query_up_grads = query_up_grads.reshape(heads, HEAD_LANES, query_rank)[:, : NOPE + ROPE]
    query_up_grads = query_up_grads.reshape(dp_count, -1, query_rank)
    latent_up_grads = dot("tk,tc->kc", hold(grad_pairs, home), latent_all).astype(BF16)
    latent_up_grads = latent_up_grads.reshape(dp_count, -1, KV_RANK)
    up_grads = jnp.concatenate(
        [
            jnp.pad(
                query_up_grads, ((0, 0), (0, up_rows - query_up_grads.shape[1]), (0, 0))
            ),
            jnp.pad(
                latent_up_grads, ((0, 0), (0, up_rows - latent_up_grads.shape[1]), (0, 0))
            ),
        ],
        2,
    )
    branch_all = with_other_core(branch_plane)
    proj_grads = dot("tk,td->kd", attended, branch_all.reshape(length, width)).astype(BF16)
    proj_grads = proj_grads.reshape(heads, HEAD_LANES, width)[:, HEAD_LANES - VDIM :]
    group_grads = jnp.concatenate(
        [up_grads, proj_grads.reshape(dp_count, -1, up_grads.shape[2])], 1
    )
    group_sums = jnp.sum(exchange(group_grads, "dp").astype(F32), 0)
    group_sums = lax.ppermute(group_sums.astype(BF16), both, to_owner).astype(F32)
    sum_query_up = group_sums[: query_up.shape[1], :query_rank].T
    sum_latent_up = group_sums[: latent_up.shape[1], query_rank:].T
    sum_out = group_sums[up_rows:].reshape(-1, width)

    grad_query_latent, grad_query_gain_part = norm_back(
        grad_own[:, :query_rank], normal_query, inverse_query, query_gain_full
    )
    grad_latent_norm, grad_latent_gain_part = norm_back(
        grad_own[:, query_rank : query_rank + KV_RANK],
        normal_latent,
        inverse_latent,
        latent_gain_full,
    )
    grad_down_out = jnp.concatenate(
        [
            grad_query_latent,
            grad_latent_norm,
            rotate_back(grad_own[:, query_rank + KV_RANK :], cos_table, sin_table),
            jnp.zeros((tokens, padded_width - down_width), F32),
        ],
        -1,
    ).astype(BF16)
    grad_normed = dot("tc,dc->td", grad_down_out, down_full)
    grad_input_norm, grad_attn_gain_part = norm_back(
        grad_normed, normal_one, inverse_one, attn_gain_full
    )
    input_grad = grad_middle + grad_input_norm

    def short_column(grads, own):
        blocks = grads.reshape(devices, own.shape[0])
        return jnp.pad(blocks, ((0, 0), (0, own_rows - own.shape[0]))).reshape(-1)

    gain_columns = jnp.stack(
        [
            grad_attn_gain_part,
            grad_ffn_gain_part,
            short_column(grad_query_gain_part, query_gain),
            short_column(grad_latent_gain_part, latent_gain),
        ],
        1,
    )
    down_sums = dot("td,tc->dc", normed, grad_down_out) + jnp.pad(
        gain_columns, ((0, 0), (down_width, padded_width - down_width - 4))
    )
    down_sums = down_sums.astype(BF16).reshape(dp_count, chips, 2, own_rows, padded_width)
    down_sums = down_sums.transpose(1, 2, 0, 3, 4)
    sum_down = scatter_z(
        scatter_seq(choose(down_sums, core, 1), choose(down_sums, 1 - core, 1))
    )
    sum_gains = sum_down[:, down_width : down_width + 4].T
    return (
        layer_output,
        input_grad,
        sum_gains[0],
        sum_down[:, :query_rank],
        sum_gains[2][: query_gain.shape[0]],
        sum_query_up,
        sum_down[:, query_rank:down_width],
        sum_gains[3][: latent_gain.shape[0]],
        sum_latent_up,
        sum_out,
        sum_gains[1],
        ffn_sums[:own_hidden].T,
        ffn_sums[own_hidden : 2 * own_hidden].T,
        ffn_sums[2 * own_hidden :],
    )


def solution(mesh):
    both = ("dp", "seq")
    dp_count = mesh.shape["dp"]

    seq_count = mesh.shape["seq"]
    by_heads = HEADS % seq_count == 0 and seq_count & (seq_count - 1) == 0

    def run(*arrays):
        if by_heads:
            return per_device_heads(dp_count, seq_count, *arrays)
        return per_device_general(dp_count, *arrays)

    in_specs = (
        P(both, None),
        P(both),
        P(both),
        P(both, None),
        P(both),
        P(None, both),
        P(both, None),
        P(both),
        P(None, both),
        P(both, None),
        P(both),
        P(None, both),
        P(None, both),
        P(both, None),
        P(both, None),
    )
    out_specs = (
        P(both, None),
        P(both, None),
        P(both),
        P(both, None),
        P(both),
        P(None, both),
        P(both, None),
        P(both),
        P(None, both),
        P(both, None),
        P(both),
        P(None, both),
        P(None, both),
        P(both, None),
    )
    return jax.shard_map(run, mesh=mesh, in_specs=in_specs, out_specs=out_specs, check_vma=False)
```

```python
import math

import jax
import jax.numpy as jnp
from jax import lax
from jax.experimental import pallas as pl
from jax.experimental.pallas import tpu as pltpu
from jax.sharding import PartitionSpec as P

KV_RANK = 256
HEADS = 40
NOPE = 64
ROPE = 32
VDIM = 64


EPSILON = 1e-05
RESIDUAL_SCALE = 1.4 / math.sqrt(62.0)
F32 = jnp.float32
BF16 = jnp.bfloat16


def norm_parts(values):
    inverse = lax.rsqrt(jnp.mean(values * values, axis=-1, keepdims=True) + EPSILON)
    return (values * inverse, inverse)


def norm_back(grad_scaled, normalized, inverse, scale_gain):
    gain_grad = jnp.sum(grad_scaled * normalized, axis=0)
    grad_normal = grad_scaled * scale_gain
    values_grad = inverse * (
        grad_normal - normalized * jnp.mean(grad_normal * normalized, axis=-1, keepdims=True)
    )
    return (values_grad, gain_grad)


def rotary_tables(positions):
    half_width = ROPE // 2
    inverse = 10000.0 ** (-2.0 * jnp.arange(half_width, dtype=F32) / ROPE)
    angles = positions.astype(F32)[:, None] * inverse[None, :]
    cos_table = jnp.cos(angles)
    sin_table = jnp.sin(angles)
    return (
        jnp.concatenate([cos_table, cos_table], -1),
        jnp.concatenate([sin_table, sin_table], -1),
    )


def rotate(values, cos_table, sin_table):
    half_width = values.shape[-1] // 2
    turned = jnp.concatenate([-values[..., half_width:], values[..., :half_width]], -1)
    return values * cos_table + turned * sin_table


def rotate_back(grads, cos_table, sin_table):
    half_width = grads.shape[-1] // 2
    scaled = grads * sin_table
    return grads * cos_table + jnp.concatenate(
        [scaled[..., half_width:], -scaled[..., :half_width]], -1
    )


def score_block(query_block, keys_values, rotary_all, allowed):
    score_scale = (NOPE + ROPE) ** (-0.5)
    scores = jnp.einsum(
        "thd,lhd->htl",
        query_block[..., :NOPE],
        keys_values[..., :NOPE],
        preferred_element_type=F32,
    )
    scores = scores + jnp.einsum(
        "thr,lr->htl", query_block[..., NOPE:], rotary_all, preferred_element_type=F32
    )
    return jnp.where(allowed[None], scores * score_scale, -1e30)


def dot(spec, left, right):
    return jnp.einsum(spec, left, right, preferred_element_type=F32)


def shift(value, axis, count, step):
    return lax.ppermute(value, axis, [(i, (i + step) % count) for i in range(count)])


def gather_dp(value, count):
    return [value] + [shift(value, "dp", count, k) for k in range(1, count)]


def scatter_dp(parts, count):
    total = parts[0].astype(F32)
    for k in range(1, count):
        total = total + shift(parts[k].astype(BF16), "dp", count, -k).astype(F32)
    return total


def gather_all(rows, dp_count):
    by_place = jnp.stack(gather_dp(rows, dp_count))
    place = lax.axis_index("dp")
    order = (place - jnp.arange(dp_count)) % dp_count
    absolute = jnp.take(by_place, order, axis=0)
    whole = lax.all_gather(absolute, "seq", axis=1, tiled=True)
    return whole.reshape(-1, rows.shape[1])


def scatter_all(grads, dp_count):
    blocks = grads.astype(BF16).reshape(dp_count, -1, grads.shape[1])
    own_seq = lax.psum_scatter(blocks, "seq", scatter_dimension=1, tiled=True)
    place = lax.axis_index("dp")
    parts = [
        lax.dynamic_index_in_dim(own_seq, (place - k) % dp_count, 0, keepdims=False)
        for k in range(dp_count)
    ]
    return scatter_dp(parts, dp_count)


def per_device_general(
    dp_count,
    layer_input,
    positions,
    attn_gain,
    query_down,
    query_gain,
    query_up,
    latent_down,
    latent_gain,
    latent_up,
    output_proj,
    ffn_gain,
    ffn_gate,
    ffn_up,
    ffn_down,
    cotangent,
):
    token_count, width = layer_input.shape
    query_rank = query_down.shape[1]
    own_rows = query_down.shape[0]
    score_scale = (NOPE + ROPE) ** (-0.5)

    def column(gain):
        return jnp.pad(gain, (0, own_rows - gain.shape[0]))[:, None]

    down_width = query_rank + KV_RANK + ROPE
    pad_width = -(down_width + 4) % 128
    packed = jnp.concatenate(
        [
            query_down,
            latent_down,
            column(attn_gain),
            column(ffn_gain),
            column(query_gain),
            column(latent_gain),
            jnp.zeros((own_rows, pad_width), BF16),
        ],
        1,
    )
    packed_full = gather_all(packed, dp_count)
    down_full = packed_full[:, :down_width]
    gains = packed_full[:, down_width : down_width + 4].T.astype(F32)
    attn_gain_full = gains[0]
    ffn_gain_full = gains[1]

    def short_gain(row, own):
        return row.reshape(-1, own_rows)[:, : own.shape[0]].reshape(-1)

    query_gain_full = short_gain(gains[2], query_gain)
    latent_gain_full = short_gain(gains[3], latent_gain)

    query_up_full = gather_all(query_up.T, dp_count)
    latent_up_full = gather_all(latent_up.T, dp_count)
    proj_full = gather_all(output_proj, dp_count)
    gate_full = lax.all_gather(ffn_gate.T, "seq", axis=0, tiled=True)
    upward_full = lax.all_gather(ffn_up.T, "seq", axis=0, tiled=True)
    ffn_down_full = lax.all_gather(ffn_down, "seq", axis=0, tiled=True)

    grad_out = cotangent.astype(F32)
    grad_two = (RESIDUAL_SCALE * grad_out).astype(BF16)
    grad_rows = jnp.concatenate(gather_dp(grad_two, dp_count))

    inputs = layer_input.astype(F32)
    cos_table, sin_table = rotary_tables(positions)
    normal_one, inverse_one = norm_parts(inputs)
    normed = (normal_one * attn_gain_full).astype(BF16)
    down_out = jnp.dot(normed, down_full, preferred_element_type=F32)
    query_latent = down_out[:, :query_rank]
    compressed = down_out[:, query_rank:]
    normal_latent, inverse_latent = norm_parts(compressed[:, :KV_RANK])
    latent = (normal_latent * latent_gain_full).astype(BF16)
    rotary_keys = rotate(compressed[:, KV_RANK:], cos_table, sin_table).astype(BF16)
    keys_all = lax.all_gather(
        jnp.concatenate([latent, rotary_keys], -1), "seq", axis=0, tiled=True
    )
    latent_all = keys_all[:, :KV_RANK]
    rotary_all = keys_all[:, KV_RANK:]
    normal_query, inverse_query = norm_parts(query_latent)
    query_normed = (normal_query * query_gain_full).astype(BF16)
    projected = dot("tq,kq->tk", query_normed, query_up_full).reshape(
        token_count, HEADS, NOPE + ROPE
    )
    queries = jnp.concatenate(
        [
            projected[..., :NOPE],
            rotate(projected[..., NOPE:], cos_table[:, None, :], sin_table[:, None, :]),
        ],
        -1,
    ).astype(BF16)
    key_count = latent_all.shape[0]
    head_group = math.gcd(HEADS, 8)
    group_count = HEADS // head_group
    first_row = lax.axis_index("seq") * token_count
    allowed = (first_row + jnp.arange(token_count))[:, None] >= jnp.arange(key_count)[None, :]
    up_grouped = latent_up_full.reshape(group_count, head_group * (NOPE + VDIM), KV_RANK)
    query_grouped = queries.reshape(token_count, group_count, head_group, NOPE + ROPE).transpose(
        1, 0, 2, 3
    )

    def forward_group(operands):
        query_block, up_block = operands
        keys_values = dot("lc,kc->lk", latent_all, up_block).astype(BF16)
        keys_values = keys_values.reshape(key_count, head_group, NOPE + VDIM)
        scores = score_block(query_block, keys_values, rotary_all, allowed)
        row_peak = jnp.max(scores, axis=-1, keepdims=True)
        exponent_terms = jnp.exp(scores - row_peak)
        row_totals = jnp.sum(exponent_terms, axis=-1, keepdims=True)
        probabilities = (exponent_terms / row_totals).astype(BF16)
        attended_block = dot("htl,lhv->thv", probabilities, keys_values[..., NOPE:])
        return (keys_values, attended_block, (row_peak + jnp.log(row_totals))[..., 0])

    kept_values, attended_grouped, log_totals = lax.map(forward_group, (query_grouped, up_grouped))
    attended_low = (
        attended_grouped.transpose(1, 0, 2, 3).reshape(token_count, HEADS * VDIM).astype(BF16)
    )
    branch = jnp.dot(attended_low, proj_full, preferred_element_type=F32)
    middle = inputs + RESIDUAL_SCALE * branch
    normal_two, inverse_two = norm_parts(middle)
    normed_two = (normal_two * ffn_gain_full).astype(BF16)

    normed_rows = jnp.concatenate(gather_dp(normed_two, dp_count))
    gate_values = dot("td,fd->tf", normed_rows, gate_full)
    upward = dot("td,fd->tf", normed_rows, upward_full)
    grad_activated = dot("td,fd->tf", grad_rows, ffn_down_full)
    sigmoid_gate = jax.nn.sigmoid(gate_values)
    activated = (gate_values * sigmoid_gate * upward).astype(BF16)
    grad_upward = (grad_activated * gate_values * sigmoid_gate).astype(BF16)
    grad_gate = (
        grad_activated * upward * sigmoid_gate * (1.0 + gate_values * (1.0 - sigmoid_gate))
    ).astype(BF16)
    grad_normed_part = dot("tf,fd->td", grad_gate, gate_full) + dot(
        "tf,fd->td", grad_upward, upward_full
    )
    grad_normed_two = scatter_dp(jnp.split(grad_normed_part, dp_count), dp_count)
    down_part = dot("tf,fd->td", activated, ffn_down_full)
    layer_output = (
        middle + RESIDUAL_SCALE * scatter_dp(jnp.split(down_part, dp_count), dp_count)
    ).astype(BF16)

    def scatter_seq(grads):
        return lax.psum_scatter(
            grads.astype(BF16), "seq", scatter_dimension=0, tiled=True
        ).astype(F32)

    sum_down = scatter_seq(dot("tf,td->fd", activated, grad_rows))
    sum_gate = scatter_seq(dot("tf,td->fd", grad_gate, normed_rows)).T
    sum_up = scatter_seq(dot("tf,td->fd", grad_upward, normed_rows)).T

    grad_middle_norm, grad_ffn_gain_part = norm_back(
        grad_normed_two, normal_two, inverse_two, ffn_gain_full
    )
    grad_middle = grad_out + grad_middle_norm
    grad_branch = (RESIDUAL_SCALE * grad_middle).astype(BF16)
    sum_out = scatter_all(dot("tk,td->kd", attended_low, grad_branch), dp_count)
    grad_attended = dot("td,kd->tk", grad_branch, proj_full).astype(BF16)
    grad_att_grouped = grad_attended.reshape(token_count, group_count, head_group, VDIM).transpose(
        1, 0, 2, 3
    )

    def backward_group(carried, operands):
        latent_sum, rotary_sum = carried
        query_block, keys_values, log_block, grad_att, attended_block, up_block = operands
        scores = score_block(query_block, keys_values, rotary_all, allowed)
        probabilities = jnp.exp(scores - log_block[..., None])
        grad_probs = dot("thv,lhv->htl", grad_att, keys_values[..., NOPE:])
        row_delta = jnp.sum(grad_att.astype(F32) * attended_block, axis=-1)
        grad_scores = (probabilities * (grad_probs - jnp.transpose(row_delta)[..., None])).astype(
            BF16
        )
        grad_query_nope = dot("htl,lhd->thd", grad_scores, keys_values[..., :NOPE]) * score_scale
        grad_query_rot = dot("htl,lr->thr", grad_scores, rotary_all) * score_scale
        grad_keys = dot("htl,thd->lhd", grad_scores, query_block[..., :NOPE]) * score_scale
        grad_rotary_part = dot("htl,thr->lr", grad_scores, query_block[..., NOPE:]) * score_scale
        grad_values = dot("htl,thv->lhv", probabilities.astype(BF16), grad_att)
        grad_pairs = (
            jnp.concatenate([grad_keys, grad_values], -1)
            .astype(BF16)
            .reshape(key_count, head_group * (NOPE + VDIM))
        )
        grad_up_block = dot("lk,lc->kc", grad_pairs, latent_all)
        latent_sum = latent_sum + dot("lk,kc->lc", grad_pairs, up_block)
        return (
            (latent_sum, rotary_sum + grad_rotary_part),
            (jnp.concatenate([grad_query_nope, grad_query_rot], -1), grad_up_block),
        )

    start_sums = (
        jnp.zeros((key_count, KV_RANK), F32),
        jnp.zeros((key_count, ROPE), F32),
    )
    (grad_latent_all, grad_rotary_all), (grad_query_grouped, grad_up_grouped) = lax.scan(
        backward_group,
        start_sums,
        (query_grouped, kept_values, log_totals, grad_att_grouped, attended_grouped, up_grouped),
    )
    sum_latent_up = scatter_all(
        grad_up_grouped.reshape(HEADS * (NOPE + VDIM), KV_RANK), dp_count
    ).T
    grad_keys_own = lax.psum_scatter(
        jnp.concatenate([grad_latent_all, grad_rotary_all], -1).astype(BF16),
        "seq",
        scatter_dimension=0,
        tiled=True,
    ).astype(F32)
    grad_latent_own = grad_keys_own[:, :KV_RANK]
    grad_rotary_own = grad_keys_own[:, KV_RANK:]
    grad_queries = grad_query_grouped.transpose(1, 0, 2, 3).reshape(token_count, HEADS, NOPE + ROPE)
    grad_projected = jnp.concatenate(
        [
            grad_queries[..., :NOPE],
            rotate_back(grad_queries[..., NOPE:], cos_table[:, None, :], sin_table[:, None, :]),
        ],
        -1,
    )
    grad_projected = grad_projected.astype(BF16).reshape(token_count, HEADS * (NOPE + ROPE))
    sum_query_up = scatter_all(dot("tk,tq->kq", grad_projected, query_normed), dp_count).T
    grad_query_normed = dot("tk,kq->tq", grad_projected, query_up_full)
    grad_query_latent, grad_query_gain_part = norm_back(
        grad_query_normed, normal_query, inverse_query, query_gain_full
    )
    grad_latent_norm, grad_latent_gain_part = norm_back(
        grad_latent_own, normal_latent, inverse_latent, latent_gain_full
    )
    grad_down_out = jnp.concatenate(
        [
            grad_query_latent,
            grad_latent_norm,
            rotate_back(grad_rotary_own, cos_table, sin_table),
        ],
        -1,
    ).astype(BF16)
    grad_down_part = dot("td,tc->dc", normed, grad_down_out)
    grad_normed = dot("tc,dc->td", grad_down_out, down_full)
    grad_input_norm, grad_attn_gain_part = norm_back(
        grad_normed, normal_one, inverse_one, attn_gain_full
    )
    input_grad = grad_middle + grad_input_norm

    def short_column(grads, own):
        blocks = grads.reshape(-1, own.shape[0])
        return jnp.pad(blocks, ((0, 0), (0, own_rows - own.shape[0]))).reshape(-1)

    gain_columns = jnp.stack(
        [
            grad_attn_gain_part,
            grad_ffn_gain_part,
            short_column(grad_query_gain_part, query_gain),
            short_column(grad_latent_gain_part, latent_gain),
        ],
        1,
    )
    sum_packed = scatter_all(
        jnp.concatenate([grad_down_part, gain_columns, jnp.zeros((width, pad_width), F32)], 1),
        dp_count,
    )
    sum_gains = sum_packed[:, down_width : down_width + 4].T
    return (
        layer_output,
        input_grad,
        sum_gains[0],
        sum_packed[:, :query_rank],
        sum_gains[2][: query_gain.shape[0]],
        sum_query_up,
        sum_packed[:, query_rank:down_width],
        sum_gains[3][: latent_gain.shape[0]],
        sum_latent_up,
        sum_out,
        sum_gains[1],
        sum_gate,
        sum_up,
        sum_down,
    )


HEAD_LANES = 128
SCORE_SCALE = (NOPE + ROPE) ** (-0.5)
QUERY_BLOCK = 256


def lane_of(values):
    return lax.broadcasted_iota(jnp.int32, values.shape, 1)


def dot_rows(left, right):
    return lax.dot_general(left, right, (((1,), (1,)), ((), ())), preferred_element_type=F32)


def block_scores(query, keys, start):
    scores = dot_rows(query, keys)
    row = start + lax.broadcasted_iota(jnp.int32, scores.shape, 0)
    return jnp.where(row >= lane_of(scores), scores * SCORE_SCALE, -1e30)


def write_tables(tail, cos_ref, left_ref, right_ref):
    half = ROPE // 2
    lane = lane_of(tail)
    sums = tail + pltpu.roll(tail, HEAD_LANES - half, 1)
    upper = (lane >= NOPE + half) & (lane < NOPE + ROPE)
    lower = (lane >= NOPE) & (lane < NOPE + half)
    cos = jnp.where(lower, pltpu.roll(sums, NOPE, 1), pltpu.roll(sums, NOPE + half, 1))
    cos_ref[...] = jnp.where(lane < NOPE, 1.0, jnp.where(lower | upper, cos, 0.0))
    left_ref[...] = jnp.where(lower, -pltpu.roll(sums, NOPE - 2 * half, 1), 0.0)
    right_ref[...] = jnp.where(upper, pltpu.roll(sums, NOPE - half, 1), 0.0)


def turn(values, cos, left, right, sign):
    half = ROPE // 2
    return (
        values * cos
        + sign * (pltpu.roll(values, HEAD_LANES - half, 1) * left)
        + sign * (pltpu.roll(values, half, 1) * right)
    )


def attend_kernel(
    tokens_ref, query_up_ref, pair_up_ref,
    query_ref, pairs_ref, attended_ref, log_ref, keys_ref, cos_ref, left_ref, right_ref,
):
    length = tokens_ref.shape[0]
    rank = query_up_ref.shape[1]
    tail_start = rank + pair_up_ref.shape[1]
    block = min(QUERY_BLOCK, length)
    head = pl.program_id(0)

    @pl.when(head == 0)
    def _():
        write_tables(tokens_ref[:, tail_start:].astype(F32), cos_ref, left_ref, right_ref)

    pairs = dot_rows(tokens_ref[:, rank:tail_start], pair_up_ref[...]).astype(BF16)
    pairs_ref[...] = pairs
    keys_ref[...] = jnp.where(lane_of(pairs) < NOPE, pairs, tokens_ref[:, tail_start:])
    for start in range(0, length, block):
        rows = pl.ds(start, block)
        stop = start + block
        projected = dot_rows(tokens_ref[rows, 0:rank], query_up_ref[...])
        query = turn(
            projected, cos_ref[rows, :], left_ref[rows, :], right_ref[rows, :], 1.0
        ).astype(BF16)
        query_ref[rows, :] = query
        scores = block_scores(query, keys_ref[0:stop, :], start)
        peak = jnp.max(scores, axis=-1, keepdims=True)
        terms = jnp.exp(scores - peak)
        totals = jnp.sum(terms, axis=-1, keepdims=True)
        probs = (terms / totals).astype(BF16)
        mixed = jnp.dot(probs, pairs_ref[0:stop, :], preferred_element_type=F32)
        log_ref[rows, :] = jnp.broadcast_to(peak + jnp.log(totals), mixed.shape)
        lane = lane_of(mixed)

        @pl.when(head % 2 == 0)
        def _():
            attended_ref[rows, :] = jnp.where(
                lane < NOPE, pltpu.roll(mixed, NOPE, 1), 0.0
            ).astype(BF16)

        @pl.when(head % 2 == 1)
        def _():
            attended_ref[rows, :] = jnp.where(
                lane < NOPE, attended_ref[rows, :].astype(F32), mixed
            ).astype(BF16)


def attend(tokens, query_up, pair_up):
    length = tokens.shape[0]
    lanes = query_up.shape[0]
    heads = lanes // HEAD_LANES
    whole = pl.BlockSpec(memory_space=pltpu.VMEM)
    own = pl.BlockSpec((length, HEAD_LANES), lambda h: (0, h))
    table = pltpu.VMEM((length, HEAD_LANES), F32)
    return pl.pallas_call(
        attend_kernel,
        grid=(heads,),
        in_specs=[
            whole,
            pl.BlockSpec((HEAD_LANES, query_up.shape[1]), lambda h: (h, 0)),
            pl.BlockSpec((HEAD_LANES, pair_up.shape[1]), lambda h: (h, 0)),
        ],
        out_specs=[
            own, own, pl.BlockSpec((length, HEAD_LANES), lambda h: (0, h // 2)), own
        ],
        out_shape=[
            jax.ShapeDtypeStruct((length, lanes), BF16),
            jax.ShapeDtypeStruct((length, lanes), BF16),
            jax.ShapeDtypeStruct((length, (heads + 1) // 2 * HEAD_LANES), BF16),
            jax.ShapeDtypeStruct((length, lanes), F32),
        ],
        scratch_shapes=[pltpu.VMEM((length, HEAD_LANES), BF16), table, table, table],
        compiler_params=pltpu.CompilerParams(vmem_limit_bytes=40 * 1024 * 1024),
        cost_estimate=pl.CostEstimate(
            flops=3 * lanes * length * length, bytes_accessed=12 * lanes * length,
            transcendentals=length * length * heads,
        ),
        name="attend",
    )(tokens, query_up, pair_up)


def attend_back_kernel(
    tokens_ref, query_up_ref, pair_up_ref, query_ref, pairs_ref, log_ref, grad_ref,
    first_ref, second_ref,
    grad_query_ref, grad_pairs_ref, grad_tokens_ref,
    keys_ref, cos_ref, left_ref, right_ref, grad_ready_ref, grad_keys_ref, grad_values_ref,
    sum_ref,
):
    length = tokens_ref.shape[0]
    rank = query_up_ref.shape[1]
    tail_start = rank + pair_up_ref.shape[1]
    block = min(QUERY_BLOCK, length)
    head = pl.program_id(0)

    @pl.when(head == 0)
    def _():
        write_tables(tokens_ref[:, tail_start:].astype(F32), cos_ref, left_ref, right_ref)
        sum_ref[...] = jnp.zeros_like(sum_ref)

    pairs = pairs_ref[...]
    lane = lane_of(pairs)
    keys_ref[...] = jnp.where(lane < NOPE, pairs, tokens_ref[:, tail_start:])
    shared = grad_ref[...].astype(F32)
    shared = jnp.where(head % 2 == 0, pltpu.roll(shared, NOPE, 1), shared)
    grad_ready_ref[...] = jnp.where(lane >= NOPE, shared, 0.0).astype(BF16)
    grad_keys_ref[...] = jnp.zeros_like(grad_keys_ref)
    grad_values_ref[...] = jnp.zeros_like(grad_values_ref)
    for start in range(0, length, block):
        rows = pl.ds(start, block)
        stop = start + block
        query = query_ref[rows, :]
        grad = grad_ready_ref[rows, :]
        scores = block_scores(query, keys_ref[0:stop, :], start)
        probs = jnp.exp(scores - log_ref[rows, 0:1])
        grad_probs = dot_rows(grad, pairs_ref[0:stop, :])
        delta = jnp.sum(probs * grad_probs, axis=-1, keepdims=True)
        grad_scores = (probs * (grad_probs - delta)).astype(BF16)
        grad_query = (
            jnp.dot(grad_scores, keys_ref[0:stop, :], preferred_element_type=F32) * SCORE_SCALE
        )
        grad_query = turn(
            grad_query, cos_ref[rows, :], left_ref[rows, :], right_ref[rows, :], -1.0
        ).astype(BF16)
        grad_query_ref[rows, :] = grad_query
        sum_ref[rows, 0:rank] += jnp.dot(
            grad_query, query_up_ref[...], preferred_element_type=F32
        )
        grad_keys_ref[:, 0:stop] += jnp.dot(query.T, grad_scores, preferred_element_type=F32)
        grad_values_ref[:, 0:stop] += jnp.dot(
            grad.T, probs.astype(BF16), preferred_element_type=F32
        )
    grad_keys = grad_keys_ref[...].T * SCORE_SCALE
    grad_pairs = jnp.where(lane < NOPE, grad_keys, grad_values_ref[...].T).astype(BF16)
    grad_pairs_ref[...] = grad_pairs
    sum_ref[:, rank:tail_start] += jnp.dot(
        grad_pairs, pair_up_ref[...], preferred_element_type=F32
    )
    sum_ref[:, tail_start:] += jnp.where((lane >= NOPE) & (lane < NOPE + ROPE), grad_keys, 0.0)

    @pl.when(head == pl.num_programs(0) - 1)
    def _():
        grad_tokens_ref[...] = sum_ref[...].astype(BF16)


def attend_back(tokens, query_up, pair_up, query, pairs, logs, grad, first, second):
    length, width = tokens.shape
    lanes = query.shape[1]
    heads = lanes // HEAD_LANES
    whole = pl.BlockSpec(memory_space=pltpu.VMEM)
    anywhere = pl.BlockSpec(memory_space=pl.ANY)
    own = pl.BlockSpec((length, HEAD_LANES), lambda h: (0, h))
    table = pltpu.VMEM((length, HEAD_LANES), F32)
    turned = pltpu.VMEM((HEAD_LANES, length), F32)
    return pl.pallas_call(
        attend_back_kernel,
        grid=(heads,),
        in_specs=[
            whole,
            pl.BlockSpec((HEAD_LANES, query_up.shape[1]), lambda h: (h, 0)),
            pl.BlockSpec((HEAD_LANES, pair_up.shape[1]), lambda h: (h, 0)),
            own,
            own,
            own,
            pl.BlockSpec((length, HEAD_LANES), lambda h: (0, h // 2)),
            anywhere,
            anywhere,
        ],
        out_specs=[own, own, pl.BlockSpec((length, width), lambda h: (0, 0))],
        out_shape=[
            jax.ShapeDtypeStruct((length, lanes), BF16),
            jax.ShapeDtypeStruct((length, lanes), BF16),
            jax.ShapeDtypeStruct((length, width), BF16),
        ],
        scratch_shapes=[
            pltpu.VMEM((length, HEAD_LANES), BF16),
            table,
            table,
            table,
            pltpu.VMEM((length, HEAD_LANES), BF16),
            turned,
            turned,
            pltpu.VMEM((length, width), F32),
        ],
        compiler_params=pltpu.CompilerParams(vmem_limit_bytes=48 * 1024 * 1024),
        cost_estimate=pl.CostEstimate(
            flops=8 * lanes * length * length, bytes_accessed=14 * lanes * length,
            transcendentals=length * length * heads,
        ),
        name="attend_back",
    )(tokens, query_up, pair_up, query, pairs, logs, grad, first, second)


def ffn_kernel(weights_ref, rows_ref, grads_ref, both_ref, act_ref):
    def against(index, rows):
        return lax.dot_general(
            weights_ref[index], rows[...], (((1,), (1,)), ((), ())), preferred_element_type=F32
        )

    gate_values = against(0, rows_ref)
    upward = against(1, rows_ref)
    grad_activated = against(2, grads_ref)
    sigmoid_gate = jax.nn.sigmoid(gate_values)
    swish = gate_values * sigmoid_gate
    act_ref[...] = (swish * upward).astype(BF16)
    both_ref[1] = (grad_activated * swish).astype(BF16)
    both_ref[0] = (
        grad_activated * upward * sigmoid_gate * (1.0 + gate_values * (1.0 - sigmoid_gate))
    ).astype(BF16)


def ffn_hidden(weights, rows, grads):
    _, hidden, width = weights.shape
    count = rows.shape[0]
    block = hidden // 4
    whole = pl.BlockSpec(memory_space=pltpu.VMEM)
    own = pl.BlockSpec((block, count), lambda i: (i, 0))
    return pl.pallas_call(
        ffn_kernel,
        grid=(hidden // block,),
        in_specs=[pl.BlockSpec((3, block, width), lambda i: (0, i, 0)), whole, whole],
        out_specs=[pl.BlockSpec((2, block, count), lambda i: (0, i, 0)), own],
        out_shape=[
            jax.ShapeDtypeStruct((2, hidden, count), BF16),
            jax.ShapeDtypeStruct((hidden, count), BF16),
        ],
        compiler_params=pltpu.CompilerParams(vmem_limit_bytes=48 * 1024 * 1024),
        cost_estimate=pl.CostEstimate(
            flops=6 * hidden * width * count,
            bytes_accessed=6 * hidden * (width + count) + 4 * count * width,
            transcendentals=hidden * count,
        ),
        name="ffn_hidden",
    )(weights, rows, grads)


def ffn_grads_kernel(both_ref, act_ref, rows_ref, grads_ref, earlier_ref, out_ref):
    hidden = act_ref.shape[1]
    parts = ((both_ref[0, 0], rows_ref), (both_ref[1, 0], rows_ref), (act_ref[0], grads_ref))
    for place, (left, right) in enumerate(parts):
        out_ref[0, place * hidden : (place + 1) * hidden, :] = jnp.dot(
            left, right[...], preferred_element_type=F32
        ).astype(BF16)


def ffn_grads(grad_both, activated, rows, grads, earlier):
    steps, hidden, count = activated.shape
    width = rows.shape[1]
    whole = pl.BlockSpec(memory_space=pltpu.VMEM)
    own = pl.BlockSpec((1, hidden, count), lambda i: (i, 0, 0))
    return pl.pallas_call(
        ffn_grads_kernel,
        grid=(steps,),
        in_specs=[
            pl.BlockSpec((2, 1, hidden, count), lambda i: (0, i, 0, 0)),
            own,
            whole,
            whole,
            pl.BlockSpec(memory_space=pl.ANY),
        ],
        out_specs=pl.BlockSpec((1, 3 * hidden, width), lambda i: (i, 0, 0)),
        out_shape=jax.ShapeDtypeStruct((steps, 3 * hidden, width), BF16),
        compiler_params=pltpu.CompilerParams(vmem_limit_bytes=48 * 1024 * 1024),
        cost_estimate=pl.CostEstimate(
            flops=6 * steps * hidden * width * count,
            bytes_accessed=6 * steps * hidden * (width + count) + 4 * count * width,
            transcendentals=0,
        ),
        name="ffn_grads",
    )(grad_both, activated, rows, grads, earlier)


def done(value):
    first = value[(0,) * value.ndim].astype(F32)
    return (first != first).astype(jnp.int32)


def hold(value, token):
    return jnp.where(token == 0, value, jnp.zeros_like(value))


def flip(value):
    count = lax.axis_size("seq")
    return lax.ppermute(value, "seq", [(i, i ^ 1) for i in range(count)])


def exchange(blocks, axis, groups=None):
    return lax.all_to_all(
        blocks, axis, split_axis=0, concat_axis=0, axis_index_groups=groups, tiled=True
    )


def repeat(value, count):
    return jnp.broadcast_to(value[None], (count,) + value.shape)


def choose(value, index, axis):
    return lax.dynamic_index_in_dim(value, index, axis, keepdims=False)


def per_device_heads(
    dp_count,
    seq_count,
    layer_input,
    positions,
    attn_gain,
    query_down,
    query_gain,
    query_up,
    latent_down,
    latent_gain,
    latent_up,
    output_proj,
    ffn_gain,
    ffn_gate,
    ffn_up,
    ffn_down,
    cotangent,
):
    tokens, width = layer_input.shape
    query_rank = query_down.shape[1]
    own_rows = query_down.shape[0]
    down_width = query_rank + KV_RANK + ROPE
    heads = HEADS // seq_count
    core = lax.axis_index("seq") % 2
    chips = seq_count // 2
    both = ("dp", "seq")
    devices = dp_count * seq_count
    length = seq_count * tokens
    place = lax.axis_index("dp")
    chip = lax.axis_index("seq") // 2
    same_core = [[2 * j + c for j in range(chips)] for c in range(2)]

    def across(value, steps):
        return lax.ppermute(value, "seq", [(i, i ^ (2 * steps)) for i in range(seq_count)])

    def place_in(whole, piece, index, axis):
        return lax.dynamic_update_slice_in_dim(whole, jnp.expand_dims(piece, axis), index, axis)

    def gather_plane(value, token=0, axis=0):
        shape = value.shape[:axis] + (chips,) + value.shape[axis:]
        whole = jnp.zeros(shape, value.dtype)
        for m in range(chips):
            piece = across(value, m) if m else value
            index = chip ^ m if m < chips - 1 else (chip ^ m) + token
            whole = place_in(whole, piece, index, axis)
        return whole

    def with_other_core(mine, axis=1):
        shape = mine.shape[:axis] + (2,) + mine.shape[axis:]
        whole = place_in(jnp.zeros(shape, mine.dtype), mine, core, axis)
        return place_in(whole, flip(mine), 1 - core, axis)

    def gather_seq(value, token=0, axis=0):
        return with_other_core(gather_plane(value, token, axis), axis + 1)

    def scatter_seq(mine, theirs, token=0):
        half = mine.astype(F32) + flip(theirs.astype(BF16)).astype(F32)
        half = half.astype(BF16)
        total = choose(half, chip, 0).astype(F32)
        for m in range(1, chips):
            total = total + across(choose(half, (chip ^ m) + token, 0), m).astype(F32)
        return total

    def gather_z(value):
        whole = jnp.zeros((dp_count,) + value.shape, value.dtype)
        for k, piece in enumerate(gather_dp(value, dp_count)):
            whole = lax.dynamic_update_index_in_dim(whole, piece, (place - k) % dp_count, 0)
        return whole

    def scatter_z(blocks):
        blocks = blocks.astype(BF16)
        total = choose(blocks, place, 0).astype(F32)
        for k in range(1, dp_count):
            block = choose(blocks, (place - k) % dp_count, 0)
            total = total + shift(block, "dp", dp_count, -k).astype(F32)
        return total

    def by_core(value, token=0):
        value = value.reshape(chips, 2, tokens, value.shape[1])
        return choose(value, core, 1), choose(value, 1 - core + token, 1)

    padded_width = down_width + 4 + -(down_width + 4) % HEAD_LANES

    def column(gain):
        return jnp.pad(gain, (0, own_rows - gain.shape[0]))[:, None]

    down_own = jnp.concatenate(
        [
            query_down,
            latent_down,
            column(attn_gain),
            column(ffn_gain),
            column(query_gain),
            column(latent_gain),
            jnp.zeros((own_rows, padded_width - down_width - 4), BF16),
        ],
        1,
    )
    down_plane = gather_z(down_own)
    group_of = [s if s % 2 == 0 else (s + 2) % seq_count for s in range(seq_count)]
    to_owner = [
        (z * seq_count + s, group_of[s] * dp_count + z)
        for z in range(dp_count)
        for s in range(seq_count)
    ]
    to_group = [(owner, holder) for holder, owner in to_owner]
    up_rows = max(query_up.shape[1], latent_up.shape[1])
    up_packed = jnp.concatenate(
        [
            jnp.pad(query_up.T, ((0, up_rows - query_up.shape[1]), (0, 0))),
            jnp.pad(latent_up.T, ((0, up_rows - latent_up.shape[1]), (0, 0))),
        ],
        1,
    )
    up_moved = lax.ppermute(up_packed, both, to_group)
    up_group = gather_z(hold(up_moved, done(down_plane)))
    down_full = gather_seq(down_plane, done(up_group), 1).reshape(width, padded_width)
    gains = down_full[:, down_width : down_width + 4].T.astype(F32)
    attn_gain_full = gains[0]
    ffn_gain_full = gains[1]

    def short_gain(row, own):
        return row.reshape(devices, own_rows)[:, : own.shape[0]].reshape(-1)

    query_gain_full = short_gain(gains[2], query_gain)
    latent_gain_full = short_gain(gains[3], latent_gain)

    query_up_padded = jnp.pad(
        up_group[:, : query_up.shape[1], :query_rank].reshape(heads, NOPE + ROPE, query_rank),
        ((0, 0), (0, HEAD_LANES - NOPE - ROPE), (0, 0)),
    ).reshape(heads * HEAD_LANES, query_rank)
    latent_up_group = up_group[:, : latent_up.shape[1], query_rank:].reshape(-1, KV_RANK)

    inputs = layer_input.astype(F32)
    normal_one, inverse_one = norm_parts(inputs)
    normed = (normal_one * attn_gain_full).astype(BF16)
    down_out = jnp.dot(normed, down_full, preferred_element_type=F32)
    normal_query, inverse_query = norm_parts(down_out[:, :query_rank])
    query_normed = (normal_query * query_gain_full).astype(BF16)
    normal_latent, inverse_latent = norm_parts(down_out[:, query_rank : query_rank + KV_RANK])
    latent = (normal_latent * latent_gain_full).astype(BF16)
    cos_table, sin_table = rotary_tables(positions)
    rotary_keys = rotate(
        down_out[:, query_rank + KV_RANK : down_width], cos_table, sin_table
    ).astype(BF16)
    half = ROPE // 2

    def two_parts(table):
        high = table.astype(BF16)
        return [high, (table - high.astype(F32)).astype(BF16)]

    token_message = jnp.concatenate(
        [query_normed, latent]
        + two_parts(cos_table[:, :half])
        + two_parts(sin_table[:, :half])
        + [rotary_keys, jnp.zeros((tokens, HEAD_LANES - NOPE - ROPE), BF16)],
        1,
    )
    tail_start = query_rank + KV_RANK
    token_all = gather_seq(token_message).reshape(length, token_message.shape[1])
    proj_full = lax.all_gather(hold(output_proj, done(down_plane)), both, axis=0, tiled=True)
    grad_out = cotangent.astype(F32)
    grad_two = (RESIDUAL_SCALE * grad_out).astype(BF16)
    grad_rows = gather_z(hold(grad_two, done(token_message))).reshape(-1, width)
    ffn_own = hold(jnp.stack([ffn_gate.T, ffn_up.T, ffn_down]), done(down_full))
    ffn_full = lax.all_gather(ffn_own, "seq", axis=1, tiled=True)

    query, pairs, attended, logs = attend(token_all, query_up_padded, latent_up_group)
    head_width = heads * VDIM
    group_place = [group_of.index(g) for g in range(seq_count)]
    attended_own = exchange(attended.reshape(seq_count, tokens, -1), "seq")[:, :, :head_width]
    attended_own = jnp.concatenate([attended_own[s] for s in group_place], 1)
    branch = jnp.dot(attended_own, proj_full, preferred_element_type=F32)
    middle = inputs + RESIDUAL_SCALE * branch
    normal_two, inverse_two = norm_parts(middle)
    normed_two = hold((normal_two * ffn_gain_full).astype(BF16), done(grad_rows))

    normed_rows = gather_z(normed_two).reshape(-1, width)
    own_hidden = ffn_down.shape[0]
    count = dp_count * tokens
    grad_both, activated = ffn_hidden(ffn_full, normed_rows, grad_rows)
    grad_part = dot("gft,gfd->td", grad_both, ffn_full[:2])
    grad_parts = grad_part.astype(BF16).reshape(dp_count, tokens, width)
    returned = [
        shift(choose(grad_parts, (place - k) % dp_count, 0), "dp", dp_count, -k)
        for k in range(1, dp_count)
    ]
    grad_normed_two = choose(grad_parts, place, 0).astype(F32)
    for piece in returned:
        grad_normed_two = grad_normed_two + piece.astype(F32)
    out_part = dot("ft,fd->td", activated, ffn_full[2]).reshape(dp_count, tokens, width)
    layer_output = (middle + RESIDUAL_SCALE * scatter_z(out_part)).astype(BF16)

    grad_middle_norm, grad_ffn_gain_part = norm_back(
        grad_normed_two, normal_two, inverse_two, ffn_gain_full
    )
    grad_middle = grad_out + grad_middle_norm
    grad_branch = (RESIDUAL_SCALE * grad_middle).astype(BF16)
    grad_attended = dot("td,kd->tk", grad_branch, proj_full).astype(BF16)
    ffn_sums = lax.psum_scatter(
        ffn_grads(
            grad_both.reshape(2, seq_count, own_hidden, count),
            activated.reshape(seq_count, own_hidden, count),
            normed_rows,
            grad_rows,
            grad_attended,
        ),
        "seq",
        scatter_dimension=0,
    ).astype(F32)
    grad_blocks = jnp.stack(
        [grad_attended[:, g * head_width : (g + 1) * head_width] for g in group_of]
    )
    grad_blocks = jnp.pad(
        grad_blocks, ((0, 0), (0, 0), (0, attended.shape[1] - head_width))
    )
    grad_heads = exchange(grad_blocks, "seq").reshape(length, -1)
    branch_plane = gather_plane(grad_branch)
    grad_projected, grad_pairs, grad_tokens = attend_back(
        token_all,
        query_up_padded,
        latent_up_group,
        query,
        pairs,
        logs,
        grad_heads,
        layer_output,
        branch_plane,
    )
    grad_own = scatter_seq(*by_core(grad_tokens))

    query_up_grads = dot("tk,tq->kq", grad_projected, token_all[:, :query_rank]).astype(BF16)
    query_up_grads = query_up_grads.reshape(heads, HEAD_LANES, query_rank)[:, : NOPE + ROPE]
    query_up_grads = query_up_grads.reshape(dp_count, -1, query_rank)
    latent_up_grads = dot("tk,tc->kc", grad_pairs, token_all[:, query_rank:tail_start])
    latent_up_grads = latent_up_grads.astype(BF16).reshape(dp_count, -1, KV_RANK)
    up_grads = jnp.concatenate(
        [
            jnp.pad(
                query_up_grads, ((0, 0), (0, up_rows - query_up_grads.shape[1]), (0, 0))
            ),
            jnp.pad(
                latent_up_grads, ((0, 0), (0, up_rows - latent_up_grads.shape[1]), (0, 0))
            ),
        ],
        2,
    )
    branch_all = with_other_core(branch_plane)
    proj_grads = dot("tk,td->kd", attended, branch_all.reshape(length, width)).astype(BF16)
    proj_grads = proj_grads[:head_width]
    group_grads = jnp.concatenate(
        [up_grads, proj_grads.reshape(dp_count, -1, up_grads.shape[2])], 1
    )
    group_sums = jnp.sum(exchange(group_grads, "dp").astype(F32), 0)
    group_sums = lax.ppermute(group_sums.astype(BF16), both, to_owner).astype(F32)
    sum_query_up = group_sums[: query_up.shape[1], :query_rank].T
    sum_latent_up = group_sums[: latent_up.shape[1], query_rank:].T
    sum_out = group_sums[up_rows:].reshape(-1, width)

    grad_query_latent, grad_query_gain_part = norm_back(
        grad_own[:, :query_rank], normal_query, inverse_query, query_gain_full
    )
    grad_latent_norm, grad_latent_gain_part = norm_back(
        grad_own[:, query_rank : query_rank + KV_RANK],
        normal_latent,
        inverse_latent,
        latent_gain_full,
    )
    grad_down_out = jnp.concatenate(
        [
            grad_query_latent,
            grad_latent_norm,
            rotate_back(
                grad_own[:, tail_start + NOPE : tail_start + NOPE + ROPE], cos_table, sin_table
            ),
            jnp.zeros((tokens, padded_width - down_width), F32),
        ],
        -1,
    ).astype(BF16)
    grad_normed = dot("tc,dc->td", grad_down_out, down_full)
    grad_input_norm, grad_attn_gain_part = norm_back(
        grad_normed, normal_one, inverse_one, attn_gain_full
    )
    input_grad = grad_middle + grad_input_norm

    def short_column(grads, own):
        blocks = grads.reshape(devices, own.shape[0])
        return jnp.pad(blocks, ((0, 0), (0, own_rows - own.shape[0]))).reshape(-1)

    gain_columns = jnp.stack(
        [
            grad_attn_gain_part,
            grad_ffn_gain_part,
            short_column(grad_query_gain_part, query_gain),
            short_column(grad_latent_gain_part, latent_gain),
        ],
        1,
    )
    down_sums = dot("td,tc->dc", normed, grad_down_out) + jnp.pad(
        gain_columns, ((0, 0), (down_width, padded_width - down_width - 4))
    )
    down_sums = down_sums.astype(BF16).reshape(dp_count, chips, 2, own_rows, padded_width)
    down_sums = down_sums.transpose(1, 2, 0, 3, 4)
    sum_down = scatter_z(
        scatter_seq(
            choose(down_sums, core, 1), choose(down_sums, 1 - core + done(group_grads), 1)
        )
    )
    sum_gains = sum_down[:, down_width : down_width + 4].T
    return (
        layer_output,
        input_grad,
        sum_gains[0],
        sum_down[:, :query_rank],
        sum_gains[2][: query_gain.shape[0]],
        sum_query_up,
        sum_down[:, query_rank:down_width],
        sum_gains[3][: latent_gain.shape[0]],
        sum_latent_up,
        sum_out,
        sum_gains[1],
        ffn_sums[:own_hidden].T,
        ffn_sums[own_hidden : 2 * own_hidden].T,
        ffn_sums[2 * own_hidden :],
    )


def solution(mesh):
    both = ("dp", "seq")
    dp_count = mesh.shape["dp"]

    seq_count = mesh.shape["seq"]
    by_heads = HEADS % seq_count == 0 and seq_count & (seq_count - 1) == 0

    def run(*arrays):
        if by_heads:
            return per_device_heads(dp_count, seq_count, *arrays)
        return per_device_general(dp_count, *arrays)

    in_specs = (
        P(both, None),
        P(both),
        P(both),
        P(both, None),
        P(both),
        P(None, both),
        P(both, None),
        P(both),
        P(None, both),
        P(both, None),
        P(both),
        P(None, both),
        P(None, both),
        P(both, None),
        P(both, None),
    )
    out_specs = (
        P(both, None),
        P(both, None),
        P(both),
        P(both, None),
        P(both),
        P(None, both),
        P(both, None),
        P(both),
        P(None, both),
        P(both, None),
        P(both),
        P(None, both),
        P(None, both),
        P(both, None),
    )
    return jax.shard_map(run, mesh=mesh, in_specs=in_specs, out_specs=out_specs, check_vma=False)
```

```python
import math

import jax
import jax.numpy as jnp
from jax import lax
from jax.experimental import pallas as pl
from jax.experimental.pallas import tpu as pltpu
from jax.sharding import PartitionSpec as P

KV_RANK = 256
HEADS = 40
NOPE = 64
ROPE = 32
VDIM = 64


EPSILON = 1e-05
RESIDUAL_SCALE = 1.4 / math.sqrt(62.0)
F32 = jnp.float32
BF16 = jnp.bfloat16


def norm_parts(values):
    inverse = lax.rsqrt(jnp.mean(values * values, axis=-1, keepdims=True) + EPSILON)
    return (values * inverse, inverse)


def norm_back(grad_scaled, normalized, inverse, scale_gain):
    gain_grad = jnp.sum(grad_scaled * normalized, axis=0)
    grad_normal = grad_scaled * scale_gain
    values_grad = inverse * (
        grad_normal - normalized * jnp.mean(grad_normal * normalized, axis=-1, keepdims=True)
    )
    return (values_grad, gain_grad)


def rotary_tables(positions):
    half_width = ROPE // 2
    inverse = 10000.0 ** (-2.0 * jnp.arange(half_width, dtype=F32) / ROPE)
    angles = positions.astype(F32)[:, None] * inverse[None, :]
    cos_table = jnp.cos(angles)
    sin_table = jnp.sin(angles)
    return (
        jnp.concatenate([cos_table, cos_table], -1),
        jnp.concatenate([sin_table, sin_table], -1),
    )


def rotate(values, cos_table, sin_table):
    half_width = values.shape[-1] // 2
    turned = jnp.concatenate([-values[..., half_width:], values[..., :half_width]], -1)
    return values * cos_table + turned * sin_table


def rotate_back(grads, cos_table, sin_table):
    half_width = grads.shape[-1] // 2
    scaled = grads * sin_table
    return grads * cos_table + jnp.concatenate(
        [scaled[..., half_width:], -scaled[..., :half_width]], -1
    )


def score_block(query_block, keys_values, rotary_all, allowed):
    score_scale = (NOPE + ROPE) ** (-0.5)
    scores = jnp.einsum(
        "thd,lhd->htl",
        query_block[..., :NOPE],
        keys_values[..., :NOPE],
        preferred_element_type=F32,
    )
    scores = scores + jnp.einsum(
        "thr,lr->htl", query_block[..., NOPE:], rotary_all, preferred_element_type=F32
    )
    return jnp.where(allowed[None], scores * score_scale, -1e30)


def dot(spec, left, right):
    return jnp.einsum(spec, left, right, preferred_element_type=F32)


def shift(value, axis, count, step):
    return lax.ppermute(value, axis, [(i, (i + step) % count) for i in range(count)])


def gather_dp(value, count):
    return [value] + [shift(value, "dp", count, k) for k in range(1, count)]


def scatter_dp(parts, count):
    total = parts[0].astype(F32)
    for k in range(1, count):
        total = total + shift(parts[k].astype(BF16), "dp", count, -k).astype(F32)
    return total


def gather_all(rows, dp_count):
    by_place = jnp.stack(gather_dp(rows, dp_count))
    place = lax.axis_index("dp")
    order = (place - jnp.arange(dp_count)) % dp_count
    absolute = jnp.take(by_place, order, axis=0)
    whole = lax.all_gather(absolute, "seq", axis=1, tiled=True)
    return whole.reshape(-1, rows.shape[1])


def scatter_all(grads, dp_count):
    blocks = grads.astype(BF16).reshape(dp_count, -1, grads.shape[1])
    own_seq = lax.psum_scatter(blocks, "seq", scatter_dimension=1, tiled=True)
    place = lax.axis_index("dp")
    parts = [
        lax.dynamic_index_in_dim(own_seq, (place - k) % dp_count, 0, keepdims=False)
        for k in range(dp_count)
    ]
    return scatter_dp(parts, dp_count)


def per_device_general(
    dp_count,
    layer_input,
    positions,
    attn_gain,
    query_down,
    query_gain,
    query_up,
    latent_down,
    latent_gain,
    latent_up,
    output_proj,
    ffn_gain,
    ffn_gate,
    ffn_up,
    ffn_down,
    cotangent,
):
    token_count, width = layer_input.shape
    query_rank = query_down.shape[1]
    own_rows = query_down.shape[0]
    score_scale = (NOPE + ROPE) ** (-0.5)

    def column(gain):
        return jnp.pad(gain, (0, own_rows - gain.shape[0]))[:, None]

    down_width = query_rank + KV_RANK + ROPE
    pad_width = -(down_width + 4) % 128
    packed = jnp.concatenate(
        [
            query_down,
            latent_down,
            column(attn_gain),
            column(ffn_gain),
            column(query_gain),
            column(latent_gain),
            jnp.zeros((own_rows, pad_width), BF16),
        ],
        1,
    )
    packed_full = gather_all(packed, dp_count)
    down_full = packed_full[:, :down_width]
    gains = packed_full[:, down_width : down_width + 4].T.astype(F32)
    attn_gain_full = gains[0]
    ffn_gain_full = gains[1]

    def short_gain(row, own):
        return row.reshape(-1, own_rows)[:, : own.shape[0]].reshape(-1)

    query_gain_full = short_gain(gains[2], query_gain)
    latent_gain_full = short_gain(gains[3], latent_gain)

    query_up_full = gather_all(query_up.T, dp_count)
    latent_up_full = gather_all(latent_up.T, dp_count)
    proj_full = gather_all(output_proj, dp_count)
    gate_full = lax.all_gather(ffn_gate.T, "seq", axis=0, tiled=True)
    upward_full = lax.all_gather(ffn_up.T, "seq", axis=0, tiled=True)
    ffn_down_full = lax.all_gather(ffn_down, "seq", axis=0, tiled=True)

    grad_out = cotangent.astype(F32)
    grad_two = (RESIDUAL_SCALE * grad_out).astype(BF16)
    grad_rows = jnp.concatenate(gather_dp(grad_two, dp_count))

    inputs = layer_input.astype(F32)
    cos_table, sin_table = rotary_tables(positions)
    normal_one, inverse_one = norm_parts(inputs)
    normed = (normal_one * attn_gain_full).astype(BF16)
    down_out = jnp.dot(normed, down_full, preferred_element_type=F32)
    query_latent = down_out[:, :query_rank]
    compressed = down_out[:, query_rank:]
    normal_latent, inverse_latent = norm_parts(compressed[:, :KV_RANK])
    latent = (normal_latent * latent_gain_full).astype(BF16)
    rotary_keys = rotate(compressed[:, KV_RANK:], cos_table, sin_table).astype(BF16)
    keys_all = lax.all_gather(
        jnp.concatenate([latent, rotary_keys], -1), "seq", axis=0, tiled=True
    )
    latent_all = keys_all[:, :KV_RANK]
    rotary_all = keys_all[:, KV_RANK:]
    normal_query, inverse_query = norm_parts(query_latent)
    query_normed = (normal_query * query_gain_full).astype(BF16)
    projected = dot("tq,kq->tk", query_normed, query_up_full).reshape(
        token_count, HEADS, NOPE + ROPE
    )
    queries = jnp.concatenate(
        [
            projected[..., :NOPE],
            rotate(projected[..., NOPE:], cos_table[:, None, :], sin_table[:, None, :]),
        ],
        -1,
    ).astype(BF16)
    key_count = latent_all.shape[0]
    head_group = math.gcd(HEADS, 8)
    group_count = HEADS // head_group
    first_row = lax.axis_index("seq") * token_count
    allowed = (first_row + jnp.arange(token_count))[:, None] >= jnp.arange(key_count)[None, :]
    up_grouped = latent_up_full.reshape(group_count, head_group * (NOPE + VDIM), KV_RANK)
    query_grouped = queries.reshape(token_count, group_count, head_group, NOPE + ROPE).transpose(
        1, 0, 2, 3
    )

    def forward_group(operands):
        query_block, up_block = operands
        keys_values = dot("lc,kc->lk", latent_all, up_block).astype(BF16)
        keys_values = keys_values.reshape(key_count, head_group, NOPE + VDIM)
        scores = score_block(query_block, keys_values, rotary_all, allowed)
        row_peak = jnp.max(scores, axis=-1, keepdims=True)
        exponent_terms = jnp.exp(scores - row_peak)
        row_totals = jnp.sum(exponent_terms, axis=-1, keepdims=True)
        probabilities = (exponent_terms / row_totals).astype(BF16)
        attended_block = dot("htl,lhv->thv", probabilities, keys_values[..., NOPE:])
        return (keys_values, attended_block, (row_peak + jnp.log(row_totals))[..., 0])

    kept_values, attended_grouped, log_totals = lax.map(forward_group, (query_grouped, up_grouped))
    attended_low = (
        attended_grouped.transpose(1, 0, 2, 3).reshape(token_count, HEADS * VDIM).astype(BF16)
    )
    branch = jnp.dot(attended_low, proj_full, preferred_element_type=F32)
    middle = inputs + RESIDUAL_SCALE * branch
    normal_two, inverse_two = norm_parts(middle)
    normed_two = (normal_two * ffn_gain_full).astype(BF16)

    normed_rows = jnp.concatenate(gather_dp(normed_two, dp_count))
    gate_values = dot("td,fd->tf", normed_rows, gate_full)
    upward = dot("td,fd->tf", normed_rows, upward_full)
    grad_activated = dot("td,fd->tf", grad_rows, ffn_down_full)
    sigmoid_gate = jax.nn.sigmoid(gate_values)
    activated = (gate_values * sigmoid_gate * upward).astype(BF16)
    grad_upward = (grad_activated * gate_values * sigmoid_gate).astype(BF16)
    grad_gate = (
        grad_activated * upward * sigmoid_gate * (1.0 + gate_values * (1.0 - sigmoid_gate))
    ).astype(BF16)
    grad_normed_part = dot("tf,fd->td", grad_gate, gate_full) + dot(
        "tf,fd->td", grad_upward, upward_full
    )
    grad_normed_two = scatter_dp(jnp.split(grad_normed_part, dp_count), dp_count)
    down_part = dot("tf,fd->td", activated, ffn_down_full)
    layer_output = (
        middle + RESIDUAL_SCALE * scatter_dp(jnp.split(down_part, dp_count), dp_count)
    ).astype(BF16)

    def scatter_seq(grads):
        return lax.psum_scatter(
            grads.astype(BF16), "seq", scatter_dimension=0, tiled=True
        ).astype(F32)

    sum_down = scatter_seq(dot("tf,td->fd", activated, grad_rows))
    sum_gate = scatter_seq(dot("tf,td->fd", grad_gate, normed_rows)).T
    sum_up = scatter_seq(dot("tf,td->fd", grad_upward, normed_rows)).T

    grad_middle_norm, grad_ffn_gain_part = norm_back(
        grad_normed_two, normal_two, inverse_two, ffn_gain_full
    )
    grad_middle = grad_out + grad_middle_norm
    grad_branch = (RESIDUAL_SCALE * grad_middle).astype(BF16)
    sum_out = scatter_all(dot("tk,td->kd", attended_low, grad_branch), dp_count)
    grad_attended = dot("td,kd->tk", grad_branch, proj_full).astype(BF16)
    grad_att_grouped = grad_attended.reshape(token_count, group_count, head_group, VDIM).transpose(
        1, 0, 2, 3
    )

    def backward_group(carried, operands):
        latent_sum, rotary_sum = carried
        query_block, keys_values, log_block, grad_att, attended_block, up_block = operands
        scores = score_block(query_block, keys_values, rotary_all, allowed)
        probabilities = jnp.exp(scores - log_block[..., None])
        grad_probs = dot("thv,lhv->htl", grad_att, keys_values[..., NOPE:])
        row_delta = jnp.sum(grad_att.astype(F32) * attended_block, axis=-1)
        grad_scores = (probabilities * (grad_probs - jnp.transpose(row_delta)[..., None])).astype(
            BF16
        )
        grad_query_nope = dot("htl,lhd->thd", grad_scores, keys_values[..., :NOPE]) * score_scale
        grad_query_rot = dot("htl,lr->thr", grad_scores, rotary_all) * score_scale
        grad_keys = dot("htl,thd->lhd", grad_scores, query_block[..., :NOPE]) * score_scale
        grad_rotary_part = dot("htl,thr->lr", grad_scores, query_block[..., NOPE:]) * score_scale
        grad_values = dot("htl,thv->lhv", probabilities.astype(BF16), grad_att)
        grad_pairs = (
            jnp.concatenate([grad_keys, grad_values], -1)
            .astype(BF16)
            .reshape(key_count, head_group * (NOPE + VDIM))
        )
        grad_up_block = dot("lk,lc->kc", grad_pairs, latent_all)
        latent_sum = latent_sum + dot("lk,kc->lc", grad_pairs, up_block)
        return (
            (latent_sum, rotary_sum + grad_rotary_part),
            (jnp.concatenate([grad_query_nope, grad_query_rot], -1), grad_up_block),
        )

    start_sums = (
        jnp.zeros((key_count, KV_RANK), F32),
        jnp.zeros((key_count, ROPE), F32),
    )
    (grad_latent_all, grad_rotary_all), (grad_query_grouped, grad_up_grouped) = lax.scan(
        backward_group,
        start_sums,
        (query_grouped, kept_values, log_totals, grad_att_grouped, attended_grouped, up_grouped),
    )
    sum_latent_up = scatter_all(
        grad_up_grouped.reshape(HEADS * (NOPE + VDIM), KV_RANK), dp_count
    ).T
    grad_keys_own = lax.psum_scatter(
        jnp.concatenate([grad_latent_all, grad_rotary_all], -1).astype(BF16),
        "seq",
        scatter_dimension=0,
        tiled=True,
    ).astype(F32)
    grad_latent_own = grad_keys_own[:, :KV_RANK]
    grad_rotary_own = grad_keys_own[:, KV_RANK:]
    grad_queries = grad_query_grouped.transpose(1, 0, 2, 3).reshape(token_count, HEADS, NOPE + ROPE)
    grad_projected = jnp.concatenate(
        [
            grad_queries[..., :NOPE],
            rotate_back(grad_queries[..., NOPE:], cos_table[:, None, :], sin_table[:, None, :]),
        ],
        -1,
    )
    grad_projected = grad_projected.astype(BF16).reshape(token_count, HEADS * (NOPE + ROPE))
    sum_query_up = scatter_all(dot("tk,tq->kq", grad_projected, query_normed), dp_count).T
    grad_query_normed = dot("tk,kq->tq", grad_projected, query_up_full)
    grad_query_latent, grad_query_gain_part = norm_back(
        grad_query_normed, normal_query, inverse_query, query_gain_full
    )
    grad_latent_norm, grad_latent_gain_part = norm_back(
        grad_latent_own, normal_latent, inverse_latent, latent_gain_full
    )
    grad_down_out = jnp.concatenate(
        [
            grad_query_latent,
            grad_latent_norm,
            rotate_back(grad_rotary_own, cos_table, sin_table),
        ],
        -1,
    ).astype(BF16)
    grad_down_part = dot("td,tc->dc", normed, grad_down_out)
    grad_normed = dot("tc,dc->td", grad_down_out, down_full)
    grad_input_norm, grad_attn_gain_part = norm_back(
        grad_normed, normal_one, inverse_one, attn_gain_full
    )
    input_grad = grad_middle + grad_input_norm

    def short_column(grads, own):
        blocks = grads.reshape(-1, own.shape[0])
        return jnp.pad(blocks, ((0, 0), (0, own_rows - own.shape[0]))).reshape(-1)

    gain_columns = jnp.stack(
        [
            grad_attn_gain_part,
            grad_ffn_gain_part,
            short_column(grad_query_gain_part, query_gain),
            short_column(grad_latent_gain_part, latent_gain),
        ],
        1,
    )
    sum_packed = scatter_all(
        jnp.concatenate([grad_down_part, gain_columns, jnp.zeros((width, pad_width), F32)], 1),
        dp_count,
    )
    sum_gains = sum_packed[:, down_width : down_width + 4].T
    return (
        layer_output,
        input_grad,
        sum_gains[0],
        sum_packed[:, :query_rank],
        sum_gains[2][: query_gain.shape[0]],
        sum_query_up,
        sum_packed[:, query_rank:down_width],
        sum_gains[3][: latent_gain.shape[0]],
        sum_latent_up,
        sum_out,
        sum_gains[1],
        sum_gate,
        sum_up,
        sum_down,
    )


HEAD_LANES = 128
SCORE_SCALE = (NOPE + ROPE) ** (-0.5)
QUERY_BLOCK = 256


def lane_of(values):
    return lax.broadcasted_iota(jnp.int32, values.shape, 1)


def dot_rows(left, right):
    return lax.dot_general(left, right, (((1,), (1,)), ((), ())), preferred_element_type=F32)


def block_scores(query, keys, start):
    scores = dot_rows(query, keys)
    row = start + lax.broadcasted_iota(jnp.int32, scores.shape, 0)
    return jnp.where(row >= lane_of(scores), scores * SCORE_SCALE, -1e30)


def write_tables(tail, cos_ref, left_ref, right_ref):
    half = ROPE // 2
    lane = lane_of(tail)
    sums = tail + pltpu.roll(tail, HEAD_LANES - half, 1)
    upper = (lane >= NOPE + half) & (lane < NOPE + ROPE)
    lower = (lane >= NOPE) & (lane < NOPE + half)
    cos = jnp.where(lower, pltpu.roll(sums, NOPE, 1), pltpu.roll(sums, NOPE + half, 1))
    cos_ref[...] = jnp.where(lane < NOPE, 1.0, jnp.where(lower | upper, cos, 0.0))
    left_ref[...] = jnp.where(lower, -pltpu.roll(sums, NOPE - 2 * half, 1), 0.0)
    right_ref[...] = jnp.where(upper, pltpu.roll(sums, NOPE - half, 1), 0.0)


def turn(values, cos, left, right, sign):
    half = ROPE // 2
    return (
        values * cos
        + sign * (pltpu.roll(values, HEAD_LANES - half, 1) * left)
        + sign * (pltpu.roll(values, half, 1) * right)
    )


def attend_kernel(
    tokens_ref, query_up_ref, pair_up_ref,
    query_ref, pairs_ref, attended_ref, log_ref, keys_ref, cos_ref, left_ref, right_ref,
):
    length = tokens_ref.shape[0]
    rank = query_up_ref.shape[1]
    tail_start = rank + pair_up_ref.shape[1]
    block = min(QUERY_BLOCK, length)
    head = pl.program_id(0)

    @pl.when(head == 0)
    def _():
        write_tables(tokens_ref[:, tail_start:].astype(F32), cos_ref, left_ref, right_ref)

    pairs = dot_rows(tokens_ref[:, rank:tail_start], pair_up_ref[...]).astype(BF16)
    pairs_ref[...] = pairs
    keys_ref[...] = jnp.where(lane_of(pairs) < NOPE, pairs, tokens_ref[:, tail_start:])
    for start in range(0, length, block):
        rows = pl.ds(start, block)
        stop = start + block
        projected = dot_rows(tokens_ref[rows, 0:rank], query_up_ref[...])
        query = turn(
            projected, cos_ref[rows, :], left_ref[rows, :], right_ref[rows, :], 1.0
        ).astype(BF16)
        query_ref[rows, :] = query
        scores = block_scores(query, keys_ref[0:stop, :], start)
        peak = jnp.max(scores, axis=-1, keepdims=True)
        terms = jnp.exp(scores - peak)
        totals = jnp.sum(terms, axis=-1, keepdims=True)
        probs = (terms / totals).astype(BF16)
        mixed = jnp.dot(probs, pairs_ref[0:stop, :], preferred_element_type=F32)
        log_ref[rows, :] = jnp.broadcast_to(peak + jnp.log(totals), mixed.shape)
        lane = lane_of(mixed)

        @pl.when(head % 2 == 0)
        def _():
            attended_ref[rows, :] = jnp.where(
                lane < NOPE, pltpu.roll(mixed, NOPE, 1), 0.0
            ).astype(BF16)

        @pl.when(head % 2 == 1)
        def _():
            attended_ref[rows, :] = jnp.where(
                lane < NOPE, attended_ref[rows, :].astype(F32), mixed
            ).astype(BF16)


def attend(tokens, query_up, pair_up):
    length = tokens.shape[0]
    lanes = query_up.shape[0]
    heads = lanes // HEAD_LANES
    whole = pl.BlockSpec(memory_space=pltpu.VMEM)
    own = pl.BlockSpec((length, HEAD_LANES), lambda h: (0, h))
    table = pltpu.VMEM((length, HEAD_LANES), F32)
    return pl.pallas_call(
        attend_kernel,
        grid=(heads,),
        in_specs=[
            whole,
            pl.BlockSpec((HEAD_LANES, query_up.shape[1]), lambda h: (h, 0)),
            pl.BlockSpec((HEAD_LANES, pair_up.shape[1]), lambda h: (h, 0)),
        ],
        out_specs=[
            own, own, pl.BlockSpec((length, HEAD_LANES), lambda h: (0, h // 2)), own
        ],
        out_shape=[
            jax.ShapeDtypeStruct((length, lanes), BF16),
            jax.ShapeDtypeStruct((length, lanes), BF16),
            jax.ShapeDtypeStruct((length, (heads + 1) // 2 * HEAD_LANES), BF16),
            jax.ShapeDtypeStruct((length, lanes), F32),
        ],
        scratch_shapes=[pltpu.VMEM((length, HEAD_LANES), BF16), table, table, table],
        compiler_params=pltpu.CompilerParams(vmem_limit_bytes=40 * 1024 * 1024),
        cost_estimate=pl.CostEstimate(
            flops=3 * lanes * length * length, bytes_accessed=12 * lanes * length,
            transcendentals=length * length * heads,
        ),
        name="attend",
    )(tokens, query_up, pair_up)


def attend_back_kernel(
    tokens_ref, query_up_ref, pair_up_ref, query_ref, pairs_ref, log_ref, grad_ref,
    earlier_ref,
    grad_query_ref, grad_pairs_ref, grad_tokens_ref,
    keys_ref, cos_ref, left_ref, right_ref, grad_ready_ref, grad_keys_ref, grad_values_ref,
    sum_ref,
):
    length = tokens_ref.shape[0]
    rank = query_up_ref.shape[1]
    tail_start = rank + pair_up_ref.shape[1]
    block = min(QUERY_BLOCK, length)
    head = pl.program_id(0)

    @pl.when(head == 0)
    def _():
        write_tables(tokens_ref[:, tail_start:].astype(F32), cos_ref, left_ref, right_ref)
        sum_ref[...] = jnp.zeros_like(sum_ref)

    pairs = pairs_ref[...]
    lane = lane_of(pairs)
    keys_ref[...] = jnp.where(lane < NOPE, pairs, tokens_ref[:, tail_start:])
    shared = grad_ref[...].astype(F32)
    shared = jnp.where(head % 2 == 0, pltpu.roll(shared, NOPE, 1), shared)
    grad_ready_ref[...] = jnp.where(lane >= NOPE, shared, 0.0).astype(BF16)
    grad_keys_ref[...] = jnp.zeros_like(grad_keys_ref)
    grad_values_ref[...] = jnp.zeros_like(grad_values_ref)
    for start in range(0, length, block):
        rows = pl.ds(start, block)
        stop = start + block
        query = query_ref[rows, :]
        grad = grad_ready_ref[rows, :]
        scores = block_scores(query, keys_ref[0:stop, :], start)
        probs = jnp.exp(scores - log_ref[rows, 0:1])
        grad_probs = dot_rows(grad, pairs_ref[0:stop, :])
        delta = jnp.sum(probs * grad_probs, axis=-1, keepdims=True)
        grad_scores = (probs * (grad_probs - delta)).astype(BF16)
        grad_query = (
            jnp.dot(grad_scores, keys_ref[0:stop, :], preferred_element_type=F32) * SCORE_SCALE
        )
        grad_query = turn(
            grad_query, cos_ref[rows, :], left_ref[rows, :], right_ref[rows, :], -1.0
        ).astype(BF16)
        grad_query_ref[rows, :] = grad_query
        sum_ref[rows, 0:rank] += jnp.dot(
            grad_query, query_up_ref[...], preferred_element_type=F32
        )
        grad_keys_ref[:, 0:stop] += jnp.dot(query.T, grad_scores, preferred_element_type=F32)
        grad_values_ref[:, 0:stop] += jnp.dot(
            grad.T, probs.astype(BF16), preferred_element_type=F32
        )
    grad_keys = grad_keys_ref[...].T * SCORE_SCALE
    grad_pairs = jnp.where(lane < NOPE, grad_keys, grad_values_ref[...].T).astype(BF16)
    grad_pairs_ref[...] = grad_pairs
    sum_ref[:, rank:tail_start] += jnp.dot(
        grad_pairs, pair_up_ref[...], preferred_element_type=F32
    )
    sum_ref[:, tail_start:] += jnp.where((lane >= NOPE) & (lane < NOPE + ROPE), grad_keys, 0.0)

    @pl.when(head == pl.num_programs(0) - 1)
    def _():
        grad_tokens_ref[...] = sum_ref[...].astype(BF16)


def attend_back(tokens, query_up, pair_up, query, pairs, logs, grad, earlier):
    length, width = tokens.shape
    lanes = query.shape[1]
    heads = lanes // HEAD_LANES
    whole = pl.BlockSpec(memory_space=pltpu.VMEM)
    own = pl.BlockSpec((length, HEAD_LANES), lambda h: (0, h))
    table = pltpu.VMEM((length, HEAD_LANES), F32)
    turned = pltpu.VMEM((HEAD_LANES, length), F32)
    return pl.pallas_call(
        attend_back_kernel,
        grid=(heads,),
        in_specs=[
            whole,
            pl.BlockSpec((HEAD_LANES, query_up.shape[1]), lambda h: (h, 0)),
            pl.BlockSpec((HEAD_LANES, pair_up.shape[1]), lambda h: (h, 0)),
            own,
            own,
            own,
            pl.BlockSpec((length, HEAD_LANES), lambda h: (0, h // 2)),
            pl.BlockSpec(memory_space=pl.ANY),
        ],
        out_specs=[own, own, pl.BlockSpec((length, width), lambda h: (0, 0))],
        out_shape=[
            jax.ShapeDtypeStruct((length, lanes), BF16),
            jax.ShapeDtypeStruct((length, lanes), BF16),
            jax.ShapeDtypeStruct((length, width), BF16),
        ],
        scratch_shapes=[
            pltpu.VMEM((length, HEAD_LANES), BF16),
            table,
            table,
            table,
            pltpu.VMEM((length, HEAD_LANES), BF16),
            turned,
            turned,
            pltpu.VMEM((length, width), F32),
        ],
        compiler_params=pltpu.CompilerParams(vmem_limit_bytes=48 * 1024 * 1024),
        cost_estimate=pl.CostEstimate(
            flops=8 * lanes * length * length, bytes_accessed=14 * lanes * length,
            transcendentals=length * length * heads,
        ),
        name="attend_back",
    )(tokens, query_up, pair_up, query, pairs, logs, grad, earlier)


def ffn_kernel(weights_ref, rows_ref, grads_ref, both_ref, act_ref):
    def against(index, rows):
        return lax.dot_general(
            weights_ref[index], rows[...], (((1,), (1,)), ((), ())), preferred_element_type=F32
        )

    gate_values = against(0, rows_ref)
    upward = against(1, rows_ref)
    grad_activated = against(2, grads_ref)
    sigmoid_gate = jax.nn.sigmoid(gate_values)
    swish = gate_values * sigmoid_gate
    act_ref[...] = (swish * upward).astype(BF16)
    both_ref[1] = (grad_activated * swish).astype(BF16)
    both_ref[0] = (
        grad_activated * upward * sigmoid_gate * (1.0 + gate_values * (1.0 - sigmoid_gate))
    ).astype(BF16)


def ffn_hidden(weights, rows, grads):
    _, hidden, width = weights.shape
    count = rows.shape[0]
    block = hidden // 4
    whole = pl.BlockSpec(memory_space=pltpu.VMEM)
    own = pl.BlockSpec((block, count), lambda i: (i, 0))
    return pl.pallas_call(
        ffn_kernel,
        grid=(hidden // block,),
        in_specs=[pl.BlockSpec((3, block, width), lambda i: (0, i, 0)), whole, whole],
        out_specs=[pl.BlockSpec((2, block, count), lambda i: (0, i, 0)), own],
        out_shape=[
            jax.ShapeDtypeStruct((2, hidden, count), BF16),
            jax.ShapeDtypeStruct((hidden, count), BF16),
        ],
        compiler_params=pltpu.CompilerParams(vmem_limit_bytes=48 * 1024 * 1024),
        cost_estimate=pl.CostEstimate(
            flops=6 * hidden * width * count,
            bytes_accessed=6 * hidden * (width + count) + 4 * count * width,
            transcendentals=hidden * count,
        ),
        name="ffn_hidden",
    )(weights, rows, grads)


def ffn_grads_kernel(both_ref, act_ref, rows_ref, grads_ref, out_ref):
    hidden = act_ref.shape[1]
    parts = ((both_ref[0, 0], rows_ref), (both_ref[1, 0], rows_ref), (act_ref[0], grads_ref))
    for place, (left, right) in enumerate(parts):
        out_ref[0, place * hidden : (place + 1) * hidden, :] = jnp.dot(
            left, right[...], preferred_element_type=F32
        ).astype(BF16)


def ffn_grads(grad_both, activated, rows, grads):
    steps, hidden, count = activated.shape
    width = rows.shape[1]
    whole = pl.BlockSpec(memory_space=pltpu.VMEM)
    own = pl.BlockSpec((1, hidden, count), lambda i: (i, 0, 0))
    return pl.pallas_call(
        ffn_grads_kernel,
        grid=(steps,),
        in_specs=[
            pl.BlockSpec((2, 1, hidden, count), lambda i: (0, i, 0, 0)),
            own,
            whole,
            whole,
        ],
        out_specs=pl.BlockSpec((1, 3 * hidden, width), lambda i: (i, 0, 0)),
        out_shape=jax.ShapeDtypeStruct((steps, 3 * hidden, width), BF16),
        compiler_params=pltpu.CompilerParams(vmem_limit_bytes=48 * 1024 * 1024),
        cost_estimate=pl.CostEstimate(
            flops=6 * steps * hidden * width * count,
            bytes_accessed=6 * steps * hidden * (width + count) + 4 * count * width,
            transcendentals=0,
        ),
        name="ffn_grads",
    )(grad_both, activated, rows, grads)


def done(value):
    last = value[(-1,) * value.ndim].astype(F32)
    return (last != last).astype(jnp.int32)


def hold(value, token):
    return jnp.where(token == 0, value, jnp.zeros_like(value))


def flip(value):
    count = lax.axis_size("seq")
    return lax.ppermute(value, "seq", [(i, i ^ 1) for i in range(count)])


def exchange(blocks, axis, groups=None):
    return lax.all_to_all(
        blocks, axis, split_axis=0, concat_axis=0, axis_index_groups=groups, tiled=True
    )


def repeat(value, count):
    return jnp.broadcast_to(value[None], (count,) + value.shape)


def choose(value, index, axis):
    return lax.dynamic_index_in_dim(value, index, axis, keepdims=False)


def per_device_heads(
    dp_count,
    seq_count,
    layer_input,
    positions,
    attn_gain,
    query_down,
    query_gain,
    query_up,
    latent_down,
    latent_gain,
    latent_up,
    output_proj,
    ffn_gain,
    ffn_gate,
    ffn_up,
    ffn_down,
    cotangent,
):
    tokens, width = layer_input.shape
    query_rank = query_down.shape[1]
    own_rows = query_down.shape[0]
    down_width = query_rank + KV_RANK + ROPE
    heads = HEADS // seq_count
    core = lax.axis_index("seq") % 2
    chips = seq_count // 2
    both = ("dp", "seq")
    devices = dp_count * seq_count
    length = seq_count * tokens
    place = lax.axis_index("dp")
    chip = lax.axis_index("seq") // 2
    same_core = [[2 * j + c for j in range(chips)] for c in range(2)]

    def across(value, steps):
        return lax.ppermute(value, "seq", [(i, i ^ (2 * steps)) for i in range(seq_count)])

    def place_in(whole, piece, index, axis):
        return lax.dynamic_update_slice_in_dim(whole, jnp.expand_dims(piece, axis), index, axis)

    def gather_plane(value, token=0, axis=0):
        shape = value.shape[:axis] + (chips,) + value.shape[axis:]
        whole = jnp.zeros(shape, value.dtype)
        for m in range(chips):
            piece = across(value, m) if m else value
            index = chip ^ m if m < chips - 1 else (chip ^ m) + token
            whole = place_in(whole, piece, index, axis)
        return whole

    def with_other_core(mine, axis=1):
        shape = mine.shape[:axis] + (2,) + mine.shape[axis:]
        whole = place_in(jnp.zeros(shape, mine.dtype), mine, core, axis)
        return place_in(whole, flip(mine), 1 - core, axis)

    def gather_seq(value, token=0, axis=0):
        return with_other_core(gather_plane(value, token, axis), axis + 1)

    def scatter_seq(mine, theirs, token=0):
        half = mine.astype(F32) + flip(theirs.astype(BF16)).astype(F32)
        half = half.astype(BF16)
        core_done = done(half)
        total = choose(half, chip, 0).astype(F32)
        for m in range(1, chips):
            total = total + across(choose(half, (chip ^ m) + token, 0), m).astype(F32)
        return total, core_done

    def gather_z(value):
        whole = jnp.zeros((dp_count,) + value.shape, value.dtype)
        for k, piece in enumerate(gather_dp(value, dp_count)):
            whole = lax.dynamic_update_index_in_dim(whole, piece, (place - k) % dp_count, 0)
        return whole

    def scatter_z(blocks):
        blocks = blocks.astype(BF16)
        total = choose(blocks, place, 0).astype(F32)
        for k in range(1, dp_count):
            block = choose(blocks, (place - k) % dp_count, 0)
            total = total + shift(block, "dp", dp_count, -k).astype(F32)
        return total

    def send_home(parts):
        total = parts[0].astype(F32)
        for k in range(1, dp_count):
            total = total + shift(parts[k], "dp", dp_count, -k).astype(F32)
        return total

    def by_core(value, token=0):
        value = value.reshape(chips, 2, tokens, value.shape[1])
        return choose(value, core, 1), choose(value, 1 - core + token, 1)

    padded_width = down_width + 4 + -(down_width + 4) % HEAD_LANES

    def column(gain):
        return jnp.pad(gain, (0, own_rows - gain.shape[0]))[:, None]

    down_own = jnp.concatenate(
        [
            query_down,
            latent_down,
            column(attn_gain),
            column(ffn_gain),
            column(query_gain),
            column(latent_gain),
            jnp.zeros((own_rows, padded_width - down_width - 4), BF16),
        ],
        1,
    )
    down_plane = gather_z(down_own)
    group_of = [s if s % 2 == 0 else (s + 2) % seq_count for s in range(seq_count)]
    to_owner = [
        (z * seq_count + s, group_of[s] * dp_count + z)
        for z in range(dp_count)
        for s in range(seq_count)
    ]
    to_group = [(owner, holder) for holder, owner in to_owner]
    up_rows = max(query_up.shape[1], latent_up.shape[1])
    up_packed = jnp.concatenate(
        [
            jnp.pad(query_up.T, ((0, up_rows - query_up.shape[1]), (0, 0))),
            jnp.pad(latent_up.T, ((0, up_rows - latent_up.shape[1]), (0, 0))),
        ],
        1,
    )
    up_moved = lax.ppermute(up_packed, both, to_group)
    up_group = exchange(repeat(hold(up_moved, done(down_plane)), dp_count), "dp")
    down_full = gather_seq(down_plane, done(up_group), 1).reshape(width, padded_width)
    gains = down_full[:, down_width : down_width + 4].T.astype(F32)
    attn_gain_full = gains[0]
    ffn_gain_full = gains[1]

    def short_gain(row, own):
        return row.reshape(devices, own_rows)[:, : own.shape[0]].reshape(-1)

    query_gain_full = short_gain(gains[2], query_gain)
    latent_gain_full = short_gain(gains[3], latent_gain)

    query_up_padded = jnp.pad(
        up_group[:, : query_up.shape[1], :query_rank].reshape(heads, NOPE + ROPE, query_rank),
        ((0, 0), (0, HEAD_LANES - NOPE - ROPE), (0, 0)),
    ).reshape(heads * HEAD_LANES, query_rank)
    latent_up_group = up_group[:, : latent_up.shape[1], query_rank:].reshape(-1, KV_RANK)

    inputs = layer_input.astype(F32)
    normal_one, inverse_one = norm_parts(inputs)
    normed = (normal_one * attn_gain_full).astype(BF16)
    down_out = jnp.dot(normed, down_full, preferred_element_type=F32)
    normal_query, inverse_query = norm_parts(down_out[:, :query_rank])
    query_normed = (normal_query * query_gain_full).astype(BF16)
    normal_latent, inverse_latent = norm_parts(down_out[:, query_rank : query_rank + KV_RANK])
    latent = (normal_latent * latent_gain_full).astype(BF16)
    cos_table, sin_table = rotary_tables(positions)
    rotary_keys = rotate(
        down_out[:, query_rank + KV_RANK : down_width], cos_table, sin_table
    ).astype(BF16)
    half = ROPE // 2

    def two_parts(table):
        high = table.astype(BF16)
        return [high, (table - high.astype(F32)).astype(BF16)]

    token_message = jnp.concatenate(
        [query_normed, latent]
        + two_parts(cos_table[:, :half])
        + two_parts(sin_table[:, :half])
        + [rotary_keys, jnp.zeros((tokens, HEAD_LANES - NOPE - ROPE), BF16)],
        1,
    )
    tail_start = query_rank + KV_RANK
    token_all = gather_seq(token_message).reshape(length, token_message.shape[1])
    proj_moved = lax.ppermute(output_proj, both, to_group)
    proj_group = exchange(repeat(hold(proj_moved, done(token_message)), dp_count), "dp")
    proj_group = proj_group.reshape(-1, width)
    proj_rows = jnp.pad(
        proj_group, ((0, (heads + 1) // 2 * HEAD_LANES - proj_group.shape[0]), (0, 0))
    )
    grad_out = cotangent.astype(F32)
    grad_two = (RESIDUAL_SCALE * grad_out).astype(BF16)
    grad_all = exchange(repeat(hold(grad_two, done(token_all)), dp_count), "dp")
    grad_rows = jnp.concatenate(
        [choose(grad_all, (place - k) % dp_count, 0) for k in range(dp_count)]
    )
    ffn_own = hold(jnp.stack([ffn_gate.T, ffn_up.T, ffn_down]), done(down_full))
    ffn_full = lax.all_gather(ffn_own, "seq", axis=1, tiled=True)

    query, pairs, attended, logs = attend(token_all, query_up_padded, latent_up_group)
    head_width = heads * VDIM
    attended_mine, attended_theirs = by_core(attended)
    branch, _ = scatter_seq(
        dot("mtk,kd->mtd", attended_mine, proj_rows),
        dot("mtk,kd->mtd", attended_theirs, proj_rows),
    )
    middle = inputs + RESIDUAL_SCALE * branch
    normal_two, inverse_two = norm_parts(middle)
    normed_two = hold((normal_two * ffn_gain_full).astype(BF16), done(grad_all))

    normed_rows = jnp.concatenate(gather_dp(normed_two, dp_count))
    proj_full = lax.all_gather(hold(proj_group, done(normed_two)), "seq", axis=0, tiled=True)
    own_hidden = ffn_down.shape[0]
    count = dp_count * tokens
    grad_both, activated = ffn_hidden(ffn_full, normed_rows, grad_rows)
    grad_part = dot("gft,gfd->td", grad_both, ffn_full[:2])
    grad_normed_two = send_home(jnp.split(grad_part.astype(BF16), dp_count))
    out_part = dot("ft,fd->td", activated, ffn_full[2]).astype(BF16)
    ffn_sums = lax.psum_scatter(
        ffn_grads(
            grad_both.reshape(2, seq_count, own_hidden, count),
            activated.reshape(seq_count, own_hidden, count),
            normed_rows,
            grad_rows,
        ),
        "seq",
        scatter_dimension=0,
    ).astype(F32)

    grad_middle_norm, grad_ffn_gain_part = norm_back(
        grad_normed_two, normal_two, inverse_two, ffn_gain_full
    )
    grad_middle = grad_out + grad_middle_norm
    grad_branch = (RESIDUAL_SCALE * grad_middle).astype(BF16)
    grad_attended = dot("td,kd->tk", grad_branch, proj_full).astype(BF16)
    grad_blocks = grad_attended.reshape(tokens, seq_count, head_width).transpose(1, 0, 2)
    grad_blocks = jnp.pad(
        grad_blocks, ((0, 0), (0, 0), (0, attended.shape[1] - head_width))
    )
    grad_blocks = grad_blocks.reshape(chips, 2, tokens, -1)
    arrived = flip(choose(grad_blocks, 1 - core, 1))
    by_chip = jnp.zeros((chips, 2) + grad_blocks.shape[2:], BF16)
    by_chip = place_in(by_chip, choose(grad_blocks, core, 1), core, 1)
    by_chip = place_in(by_chip, arrived, 1 - core, 1)
    grad_heads = jnp.zeros_like(by_chip)
    for m in range(chips):
        piece = choose(by_chip, chip ^ m, 0)
        grad_heads = place_in(grad_heads, across(piece, m) if m else piece, chip ^ m, 0)
    grad_heads = grad_heads.reshape(length, -1)
    branch_plane = gather_plane(hold(grad_branch, done(grad_heads)))
    grad_projected, grad_pairs, grad_tokens = attend_back(
        token_all,
        query_up_padded,
        latent_up_group,
        query,
        pairs,
        logs,
        grad_heads,
        out_part,
    )
    grad_own, _ = scatter_seq(*by_core(grad_tokens), done(branch_plane))
    out_slots = hold(out_part, done(grad_heads)).reshape(dp_count, tokens, width)
    out_blocks = jnp.stack(
        [choose(out_slots, (place - j) % dp_count, 0) for j in range(dp_count)]
    )
    out_all = exchange(out_blocks, "dp")
    layer_output = (middle + RESIDUAL_SCALE * jnp.sum(out_all.astype(F32), 0)).astype(BF16)
    grad_own = hold(grad_own, done(out_all))

    query_up_grads = dot("tk,tq->kq", grad_projected, token_all[:, :query_rank]).astype(BF16)
    query_up_grads = query_up_grads.reshape(heads, HEAD_LANES, query_rank)[:, : NOPE + ROPE]
    query_up_grads = query_up_grads.reshape(dp_count, -1, query_rank)
    latent_up_grads = dot("tk,tc->kc", grad_pairs, token_all[:, query_rank:tail_start])
    latent_up_grads = latent_up_grads.astype(BF16).reshape(dp_count, -1, KV_RANK)
    up_grads = jnp.concatenate(
        [
            jnp.pad(
                query_up_grads, ((0, 0), (0, up_rows - query_up_grads.shape[1]), (0, 0))
            ),
            jnp.pad(
                latent_up_grads, ((0, 0), (0, up_rows - latent_up_grads.shape[1]), (0, 0))
            ),
        ],
        2,
    )
    branch_all = with_other_core(branch_plane)
    proj_grads = dot("tk,td->kd", attended, branch_all.reshape(length, width)).astype(BF16)
    proj_grads = proj_grads[:head_width]
    group_grads = jnp.concatenate(
        [up_grads, proj_grads.reshape(dp_count, -1, up_grads.shape[2])], 1
    )
    grad_query_latent, grad_query_gain_part = norm_back(
        grad_own[:, :query_rank], normal_query, inverse_query, query_gain_full
    )
    grad_latent_norm, grad_latent_gain_part = norm_back(
        grad_own[:, query_rank : query_rank + KV_RANK],
        normal_latent,
        inverse_latent,
        latent_gain_full,
    )
    grad_down_out = jnp.concatenate(
        [
            grad_query_latent,
            grad_latent_norm,
            rotate_back(
                grad_own[:, tail_start + NOPE : tail_start + NOPE + ROPE], cos_table, sin_table
            ),
            jnp.zeros((tokens, padded_width - down_width), F32),
        ],
        -1,
    ).astype(BF16)
    grad_normed = dot("tc,dc->td", grad_down_out, down_full)
    grad_input_norm, grad_attn_gain_part = norm_back(
        grad_normed, normal_one, inverse_one, attn_gain_full
    )
    input_grad = grad_middle + grad_input_norm

    def short_column(grads, own):
        blocks = grads.reshape(devices, own.shape[0])
        return jnp.pad(blocks, ((0, 0), (0, own_rows - own.shape[0]))).reshape(-1)

    gain_columns = jnp.stack(
        [
            grad_attn_gain_part,
            grad_ffn_gain_part,
            short_column(grad_query_gain_part, query_gain),
            short_column(grad_latent_gain_part, latent_gain),
        ],
        1,
    )
    down_sums = dot("td,tc->dc", normed, grad_down_out) + jnp.pad(
        gain_columns, ((0, 0), (down_width, padded_width - down_width - 4))
    )
    down_sums = down_sums.astype(BF16).reshape(dp_count, chips, 2, own_rows, padded_width)
    down_sums = down_sums.transpose(1, 2, 0, 3, 4)
    sum_down, core_done = scatter_seq(
        choose(down_sums, core, 1),
        choose(down_sums, 1 - core + done(group_grads), 1),
    )
    sum_down = scatter_z(sum_down)
    group_sums = jnp.sum(exchange(hold(group_grads, core_done), "dp").astype(F32), 0)
    group_sums = lax.ppermute(group_sums.astype(BF16), both, to_owner).astype(F32)
    sum_query_up = group_sums[: query_up.shape[1], :query_rank].T
    sum_latent_up = group_sums[: latent_up.shape[1], query_rank:].T
    sum_out = group_sums[up_rows:].reshape(-1, width)
    sum_gains = sum_down[:, down_width : down_width + 4].T
    return (
        layer_output,
        input_grad,
        sum_gains[0],
        sum_down[:, :query_rank],
        sum_gains[2][: query_gain.shape[0]],
        sum_query_up,
        sum_down[:, query_rank:down_width],
        sum_gains[3][: latent_gain.shape[0]],
        sum_latent_up,
        sum_out,
        sum_gains[1],
        ffn_sums[:own_hidden].T,
        ffn_sums[own_hidden : 2 * own_hidden].T,
        ffn_sums[2 * own_hidden :],
    )


def solution(mesh):
    both = ("dp", "seq")
    dp_count = mesh.shape["dp"]

    seq_count = mesh.shape["seq"]
    by_heads = HEADS % seq_count == 0 and seq_count & (seq_count - 1) == 0

    def run(*arrays):
        if by_heads:
            return per_device_heads(dp_count, seq_count, *arrays)
        return per_device_general(dp_count, *arrays)

    in_specs = (
        P(both, None),
        P(both),
        P(both),
        P(both, None),
        P(both),
        P(None, both),
        P(both, None),
        P(both),
        P(None, both),
        P(both, None),
        P(both),
        P(None, both),
        P(None, both),
        P(both, None),
        P(both, None),
    )
    out_specs = (
        P(both, None),
        P(both, None),
        P(both),
        P(both, None),
        P(both),
        P(None, both),
        P(both, None),
        P(both),
        P(None, both),
        P(both, None),
        P(both),
        P(None, both),
        P(None, both),
        P(both, None),
    )
    return jax.shard_map(run, mesh=mesh, in_specs=in_specs, out_specs=out_specs, check_vma=False)
```

```python
import math

import jax
import jax.numpy as jnp
from jax import lax
from jax.experimental import pallas as pl
from jax.experimental.pallas import tpu as pltpu
from jax.sharding import PartitionSpec as P

KV_RANK = 256
HEADS = 40
NOPE = 64
ROPE = 32
VDIM = 64


EPSILON = 1e-05
RESIDUAL_SCALE = 1.4 / math.sqrt(62.0)
F32 = jnp.float32
BF16 = jnp.bfloat16


def norm_parts(values):
    inverse = lax.rsqrt(jnp.mean(values * values, axis=-1, keepdims=True) + EPSILON)
    return (values * inverse, inverse)


def norm_back(grad_scaled, normalized, inverse, scale_gain):
    gain_grad = jnp.sum(grad_scaled * normalized, axis=0)
    grad_normal = grad_scaled * scale_gain
    values_grad = inverse * (
        grad_normal - normalized * jnp.mean(grad_normal * normalized, axis=-1, keepdims=True)
    )
    return (values_grad, gain_grad)


def rotary_tables(positions):
    half_width = ROPE // 2
    inverse = 10000.0 ** (-2.0 * jnp.arange(half_width, dtype=F32) / ROPE)
    angles = positions.astype(F32)[:, None] * inverse[None, :]
    cos_table = jnp.cos(angles)
    sin_table = jnp.sin(angles)
    return (
        jnp.concatenate([cos_table, cos_table], -1),
        jnp.concatenate([sin_table, sin_table], -1),
    )


def rotate(values, cos_table, sin_table):
    half_width = values.shape[-1] // 2
    turned = jnp.concatenate([-values[..., half_width:], values[..., :half_width]], -1)
    return values * cos_table + turned * sin_table


def rotate_back(grads, cos_table, sin_table):
    half_width = grads.shape[-1] // 2
    scaled = grads * sin_table
    return grads * cos_table + jnp.concatenate(
        [scaled[..., half_width:], -scaled[..., :half_width]], -1
    )


def score_block(query_block, keys_values, rotary_all, allowed):
    score_scale = (NOPE + ROPE) ** (-0.5)
    scores = jnp.einsum(
        "thd,lhd->htl",
        query_block[..., :NOPE],
        keys_values[..., :NOPE],
        preferred_element_type=F32,
    )
    scores = scores + jnp.einsum(
        "thr,lr->htl", query_block[..., NOPE:], rotary_all, preferred_element_type=F32
    )
    return jnp.where(allowed[None], scores * score_scale, -1e30)


def dot(spec, left, right):
    return jnp.einsum(spec, left, right, preferred_element_type=F32)


def shift(value, axis, count, step):
    return lax.ppermute(value, axis, [(i, (i + step) % count) for i in range(count)])


def gather_dp(value, count):
    return [value] + [shift(value, "dp", count, k) for k in range(1, count)]


def scatter_dp(parts, count):
    total = parts[0].astype(F32)
    for k in range(1, count):
        total = total + shift(parts[k].astype(BF16), "dp", count, -k).astype(F32)
    return total


def gather_all(rows, dp_count):
    by_place = jnp.stack(gather_dp(rows, dp_count))
    place = lax.axis_index("dp")
    order = (place - jnp.arange(dp_count)) % dp_count
    absolute = jnp.take(by_place, order, axis=0)
    whole = lax.all_gather(absolute, "seq", axis=1, tiled=True)
    return whole.reshape(-1, rows.shape[1])


def scatter_all(grads, dp_count):
    blocks = grads.astype(BF16).reshape(dp_count, -1, grads.shape[1])
    own_seq = lax.psum_scatter(blocks, "seq", scatter_dimension=1, tiled=True)
    place = lax.axis_index("dp")
    parts = [
        lax.dynamic_index_in_dim(own_seq, (place - k) % dp_count, 0, keepdims=False)
        for k in range(dp_count)
    ]
    return scatter_dp(parts, dp_count)


def per_device_general(
    dp_count,
    layer_input,
    positions,
    attn_gain,
    query_down,
    query_gain,
    query_up,
    latent_down,
    latent_gain,
    latent_up,
    output_proj,
    ffn_gain,
    ffn_gate,
    ffn_up,
    ffn_down,
    cotangent,
):
    token_count, width = layer_input.shape
    query_rank = query_down.shape[1]
    own_rows = query_down.shape[0]
    score_scale = (NOPE + ROPE) ** (-0.5)

    def column(gain):
        return jnp.pad(gain, (0, own_rows - gain.shape[0]))[:, None]

    down_width = query_rank + KV_RANK + ROPE
    pad_width = -(down_width + 4) % 128
    packed = jnp.concatenate(
        [
            query_down,
            latent_down,
            column(attn_gain),
            column(ffn_gain),
            column(query_gain),
            column(latent_gain),
            jnp.zeros((own_rows, pad_width), BF16),
        ],
        1,
    )
    packed_full = gather_all(packed, dp_count)
    down_full = packed_full[:, :down_width]
    gains = packed_full[:, down_width : down_width + 4].T.astype(F32)
    attn_gain_full = gains[0]
    ffn_gain_full = gains[1]

    def short_gain(row, own):
        return row.reshape(-1, own_rows)[:, : own.shape[0]].reshape(-1)

    query_gain_full = short_gain(gains[2], query_gain)
    latent_gain_full = short_gain(gains[3], latent_gain)

    query_up_full = gather_all(query_up.T, dp_count)
    latent_up_full = gather_all(latent_up.T, dp_count)
    proj_full = gather_all(output_proj, dp_count)
    gate_full = lax.all_gather(ffn_gate.T, "seq", axis=0, tiled=True)
    upward_full = lax.all_gather(ffn_up.T, "seq", axis=0, tiled=True)
    ffn_down_full = lax.all_gather(ffn_down, "seq", axis=0, tiled=True)

    grad_out = cotangent.astype(F32)
    grad_two = (RESIDUAL_SCALE * grad_out).astype(BF16)
    grad_rows = jnp.concatenate(gather_dp(grad_two, dp_count))

    inputs = layer_input.astype(F32)
    cos_table, sin_table = rotary_tables(positions)
    normal_one, inverse_one = norm_parts(inputs)
    normed = (normal_one * attn_gain_full).astype(BF16)
    down_out = jnp.dot(normed, down_full, preferred_element_type=F32)
    query_latent = down_out[:, :query_rank]
    compressed = down_out[:, query_rank:]
    normal_latent, inverse_latent = norm_parts(compressed[:, :KV_RANK])
    latent = (normal_latent * latent_gain_full).astype(BF16)
    rotary_keys = rotate(compressed[:, KV_RANK:], cos_table, sin_table).astype(BF16)
    keys_all = lax.all_gather(
        jnp.concatenate([latent, rotary_keys], -1), "seq", axis=0, tiled=True
    )
    latent_all = keys_all[:, :KV_RANK]
    rotary_all = keys_all[:, KV_RANK:]
    normal_query, inverse_query = norm_parts(query_latent)
    query_normed = (normal_query * query_gain_full).astype(BF16)
    projected = dot("tq,kq->tk", query_normed, query_up_full).reshape(
        token_count, HEADS, NOPE + ROPE
    )
    queries = jnp.concatenate(
        [
            projected[..., :NOPE],
            rotate(projected[..., NOPE:], cos_table[:, None, :], sin_table[:, None, :]),
        ],
        -1,
    ).astype(BF16)
    key_count = latent_all.shape[0]
    head_group = math.gcd(HEADS, 8)
    group_count = HEADS // head_group
    first_row = lax.axis_index("seq") * token_count
    allowed = (first_row + jnp.arange(token_count))[:, None] >= jnp.arange(key_count)[None, :]
    up_grouped = latent_up_full.reshape(group_count, head_group * (NOPE + VDIM), KV_RANK)
    query_grouped = queries.reshape(token_count, group_count, head_group, NOPE + ROPE).transpose(
        1, 0, 2, 3
    )

    def forward_group(operands):
        query_block, up_block = operands
        keys_values = dot("lc,kc->lk", latent_all, up_block).astype(BF16)
        keys_values = keys_values.reshape(key_count, head_group, NOPE + VDIM)
        scores = score_block(query_block, keys_values, rotary_all, allowed)
        row_peak = jnp.max(scores, axis=-1, keepdims=True)
        exponent_terms = jnp.exp(scores - row_peak)
        row_totals = jnp.sum(exponent_terms, axis=-1, keepdims=True)
        probabilities = (exponent_terms / row_totals).astype(BF16)
        attended_block = dot("htl,lhv->thv", probabilities, keys_values[..., NOPE:])
        return (keys_values, attended_block, (row_peak + jnp.log(row_totals))[..., 0])

    kept_values, attended_grouped, log_totals = lax.map(forward_group, (query_grouped, up_grouped))
    attended_low = (
        attended_grouped.transpose(1, 0, 2, 3).reshape(token_count, HEADS * VDIM).astype(BF16)
    )
    branch = jnp.dot(attended_low, proj_full, preferred_element_type=F32)
    middle = inputs + RESIDUAL_SCALE * branch
    normal_two, inverse_two = norm_parts(middle)
    normed_two = (normal_two * ffn_gain_full).astype(BF16)

    normed_rows = jnp.concatenate(gather_dp(normed_two, dp_count))
    gate_values = dot("td,fd->tf", normed_rows, gate_full)
    upward = dot("td,fd->tf", normed_rows, upward_full)
    grad_activated = dot("td,fd->tf", grad_rows, ffn_down_full)
    sigmoid_gate = jax.nn.sigmoid(gate_values)
    activated = (gate_values * sigmoid_gate * upward).astype(BF16)
    grad_upward = (grad_activated * gate_values * sigmoid_gate).astype(BF16)
    grad_gate = (
        grad_activated * upward * sigmoid_gate * (1.0 + gate_values * (1.0 - sigmoid_gate))
    ).astype(BF16)
    grad_normed_part = dot("tf,fd->td", grad_gate, gate_full) + dot(
        "tf,fd->td", grad_upward, upward_full
    )
    grad_normed_two = scatter_dp(jnp.split(grad_normed_part, dp_count), dp_count)
    down_part = dot("tf,fd->td", activated, ffn_down_full)
    layer_output = (
        middle + RESIDUAL_SCALE * scatter_dp(jnp.split(down_part, dp_count), dp_count)
    ).astype(BF16)

    def scatter_seq(grads):
        return lax.psum_scatter(
            grads.astype(BF16), "seq", scatter_dimension=0, tiled=True
        ).astype(F32)

    sum_down = scatter_seq(dot("tf,td->fd", activated, grad_rows))
    sum_gate = scatter_seq(dot("tf,td->fd", grad_gate, normed_rows)).T
    sum_up = scatter_seq(dot("tf,td->fd", grad_upward, normed_rows)).T

    grad_middle_norm, grad_ffn_gain_part = norm_back(
        grad_normed_two, normal_two, inverse_two, ffn_gain_full
    )
    grad_middle = grad_out + grad_middle_norm
    grad_branch = (RESIDUAL_SCALE * grad_middle).astype(BF16)
    sum_out = scatter_all(dot("tk,td->kd", attended_low, grad_branch), dp_count)
    grad_attended = dot("td,kd->tk", grad_branch, proj_full).astype(BF16)
    grad_att_grouped = grad_attended.reshape(token_count, group_count, head_group, VDIM).transpose(
        1, 0, 2, 3
    )

    def backward_group(carried, operands):
        latent_sum, rotary_sum = carried
        query_block, keys_values, log_block, grad_att, attended_block, up_block = operands
        scores = score_block(query_block, keys_values, rotary_all, allowed)
        probabilities = jnp.exp(scores - log_block[..., None])
        grad_probs = dot("thv,lhv->htl", grad_att, keys_values[..., NOPE:])
        row_delta = jnp.sum(grad_att.astype(F32) * attended_block, axis=-1)
        grad_scores = (probabilities * (grad_probs - jnp.transpose(row_delta)[..., None])).astype(
            BF16
        )
        grad_query_nope = dot("htl,lhd->thd", grad_scores, keys_values[..., :NOPE]) * score_scale
        grad_query_rot = dot("htl,lr->thr", grad_scores, rotary_all) * score_scale
        grad_keys = dot("htl,thd->lhd", grad_scores, query_block[..., :NOPE]) * score_scale
        grad_rotary_part = dot("htl,thr->lr", grad_scores, query_block[..., NOPE:]) * score_scale
        grad_values = dot("htl,thv->lhv", probabilities.astype(BF16), grad_att)
        grad_pairs = (
            jnp.concatenate([grad_keys, grad_values], -1)
            .astype(BF16)
            .reshape(key_count, head_group * (NOPE + VDIM))
        )
        grad_up_block = dot("lk,lc->kc", grad_pairs, latent_all)
        latent_sum = latent_sum + dot("lk,kc->lc", grad_pairs, up_block)
        return (
            (latent_sum, rotary_sum + grad_rotary_part),
            (jnp.concatenate([grad_query_nope, grad_query_rot], -1), grad_up_block),
        )

    start_sums = (
        jnp.zeros((key_count, KV_RANK), F32),
        jnp.zeros((key_count, ROPE), F32),
    )
    (grad_latent_all, grad_rotary_all), (grad_query_grouped, grad_up_grouped) = lax.scan(
        backward_group,
        start_sums,
        (query_grouped, kept_values, log_totals, grad_att_grouped, attended_grouped, up_grouped),
    )
    sum_latent_up = scatter_all(
        grad_up_grouped.reshape(HEADS * (NOPE + VDIM), KV_RANK), dp_count
    ).T
    grad_keys_own = lax.psum_scatter(
        jnp.concatenate([grad_latent_all, grad_rotary_all], -1).astype(BF16),
        "seq",
        scatter_dimension=0,
        tiled=True,
    ).astype(F32)
    grad_latent_own = grad_keys_own[:, :KV_RANK]
    grad_rotary_own = grad_keys_own[:, KV_RANK:]
    grad_queries = grad_query_grouped.transpose(1, 0, 2, 3).reshape(token_count, HEADS, NOPE + ROPE)
    grad_projected = jnp.concatenate(
        [
            grad_queries[..., :NOPE],
            rotate_back(grad_queries[..., NOPE:], cos_table[:, None, :], sin_table[:, None, :]),
        ],
        -1,
    )
    grad_projected = grad_projected.astype(BF16).reshape(token_count, HEADS * (NOPE + ROPE))
    sum_query_up = scatter_all(dot("tk,tq->kq", grad_projected, query_normed), dp_count).T
    grad_query_normed = dot("tk,kq->tq", grad_projected, query_up_full)
    grad_query_latent, grad_query_gain_part = norm_back(
        grad_query_normed, normal_query, inverse_query, query_gain_full
    )
    grad_latent_norm, grad_latent_gain_part = norm_back(
        grad_latent_own, normal_latent, inverse_latent, latent_gain_full
    )
    grad_down_out = jnp.concatenate(
        [
            grad_query_latent,
            grad_latent_norm,
            rotate_back(grad_rotary_own, cos_table, sin_table),
        ],
        -1,
    ).astype(BF16)
    grad_down_part = dot("td,tc->dc", normed, grad_down_out)
    grad_normed = dot("tc,dc->td", grad_down_out, down_full)
    grad_input_norm, grad_attn_gain_part = norm_back(
        grad_normed, normal_one, inverse_one, attn_gain_full
    )
    input_grad = grad_middle + grad_input_norm

    def short_column(grads, own):
        blocks = grads.reshape(-1, own.shape[0])
        return jnp.pad(blocks, ((0, 0), (0, own_rows - own.shape[0]))).reshape(-1)

    gain_columns = jnp.stack(
        [
            grad_attn_gain_part,
            grad_ffn_gain_part,
            short_column(grad_query_gain_part, query_gain),
            short_column(grad_latent_gain_part, latent_gain),
        ],
        1,
    )
    sum_packed = scatter_all(
        jnp.concatenate([grad_down_part, gain_columns, jnp.zeros((width, pad_width), F32)], 1),
        dp_count,
    )
    sum_gains = sum_packed[:, down_width : down_width + 4].T
    return (
        layer_output,
        input_grad,
        sum_gains[0],
        sum_packed[:, :query_rank],
        sum_gains[2][: query_gain.shape[0]],
        sum_query_up,
        sum_packed[:, query_rank:down_width],
        sum_gains[3][: latent_gain.shape[0]],
        sum_latent_up,
        sum_out,
        sum_gains[1],
        sum_gate,
        sum_up,
        sum_down,
    )


HEAD_LANES = 128
SCORE_SCALE = (NOPE + ROPE) ** (-0.5)
QUERY_BLOCK = 256


def lane_of(values):
    return lax.broadcasted_iota(jnp.int32, values.shape, 1)


def dot_rows(left, right):
    return lax.dot_general(left, right, (((1,), (1,)), ((), ())), preferred_element_type=F32)


def block_scores(query, keys, start):
    scores = dot_rows(query, keys)
    row = start + lax.broadcasted_iota(jnp.int32, scores.shape, 0)
    return jnp.where(row >= lane_of(scores), scores * SCORE_SCALE, -1e30)


def write_tables(tail, cos_ref, left_ref, right_ref):
    half = ROPE // 2
    lane = lane_of(tail)
    sums = tail + pltpu.roll(tail, HEAD_LANES - half, 1)
    upper = (lane >= NOPE + half) & (lane < NOPE + ROPE)
    lower = (lane >= NOPE) & (lane < NOPE + half)
    cos = jnp.where(lower, pltpu.roll(sums, NOPE, 1), pltpu.roll(sums, NOPE + half, 1))
    cos_ref[...] = jnp.where(lane < NOPE, 1.0, jnp.where(lower | upper, cos, 0.0))
    left_ref[...] = jnp.where(lower, -pltpu.roll(sums, NOPE - 2 * half, 1), 0.0)
    right_ref[...] = jnp.where(upper, pltpu.roll(sums, NOPE - half, 1), 0.0)


def turn(values, cos, left, right, sign):
    half = ROPE // 2
    return (
        values * cos
        + sign * (pltpu.roll(values, HEAD_LANES - half, 1) * left)
        + sign * (pltpu.roll(values, half, 1) * right)
    )


def attend_kernel(
    tokens_ref, query_up_ref, pair_up_ref,
    query_ref, pairs_ref, attended_ref, log_ref, keys_ref, cos_ref, left_ref, right_ref,
):
    length = tokens_ref.shape[0]
    rank = query_up_ref.shape[1]
    tail_start = rank + pair_up_ref.shape[1]
    block = min(QUERY_BLOCK, length)
    head = pl.program_id(0)

    @pl.when(head == 0)
    def _():
        write_tables(tokens_ref[:, tail_start:].astype(F32), cos_ref, left_ref, right_ref)

    pairs = dot_rows(tokens_ref[:, rank:tail_start], pair_up_ref[...]).astype(BF16)
    pairs_ref[...] = pairs
    keys_ref[...] = jnp.where(lane_of(pairs) < NOPE, pairs, tokens_ref[:, tail_start:])
    for start in range(0, length, block):
        rows = pl.ds(start, block)
        stop = start + block
        projected = dot_rows(tokens_ref[rows, 0:rank], query_up_ref[...])
        query = turn(
            projected, cos_ref[rows, :], left_ref[rows, :], right_ref[rows, :], 1.0
        ).astype(BF16)
        query_ref[rows, :] = query
        scores = block_scores(query, keys_ref[0:stop, :], start)
        peak = jnp.max(scores, axis=-1, keepdims=True)
        terms = jnp.exp(scores - peak)
        totals = jnp.sum(terms, axis=-1, keepdims=True)
        probs = (terms / totals).astype(BF16)
        mixed = jnp.dot(probs, pairs_ref[0:stop, :], preferred_element_type=F32)
        log_ref[rows, :] = jnp.broadcast_to(peak + jnp.log(totals), mixed.shape)
        lane = lane_of(mixed)

        @pl.when(head % 2 == 0)
        def _():
            attended_ref[rows, :] = jnp.where(
                lane < NOPE, pltpu.roll(mixed, NOPE, 1), 0.0
            ).astype(BF16)

        @pl.when(head % 2 == 1)
        def _():
            attended_ref[rows, :] = jnp.where(
                lane < NOPE, attended_ref[rows, :].astype(F32), mixed
            ).astype(BF16)


def attend(tokens, query_up, pair_up):
    length = tokens.shape[0]
    lanes = query_up.shape[0]
    heads = lanes // HEAD_LANES
    whole = pl.BlockSpec(memory_space=pltpu.VMEM)
    own = pl.BlockSpec((length, HEAD_LANES), lambda h: (0, h))
    table = pltpu.VMEM((length, HEAD_LANES), F32)
    return pl.pallas_call(
        attend_kernel,
        grid=(heads,),
        in_specs=[
            whole,
            pl.BlockSpec((HEAD_LANES, query_up.shape[1]), lambda h: (h, 0)),
            pl.BlockSpec((HEAD_LANES, pair_up.shape[1]), lambda h: (h, 0)),
        ],
        out_specs=[
            own, own, pl.BlockSpec((length, HEAD_LANES), lambda h: (0, h // 2)), own
        ],
        out_shape=[
            jax.ShapeDtypeStruct((length, lanes), BF16),
            jax.ShapeDtypeStruct((length, lanes), BF16),
            jax.ShapeDtypeStruct((length, (heads + 1) // 2 * HEAD_LANES), BF16),
            jax.ShapeDtypeStruct((length, lanes), F32),
        ],
        scratch_shapes=[pltpu.VMEM((length, HEAD_LANES), BF16), table, table, table],
        compiler_params=pltpu.CompilerParams(vmem_limit_bytes=40 * 1024 * 1024),
        cost_estimate=pl.CostEstimate(
            flops=3 * lanes * length * length, bytes_accessed=12 * lanes * length,
            transcendentals=length * length * heads,
        ),
        name="attend",
    )(tokens, query_up, pair_up)


def attend_back_kernel(
    tokens_ref, query_up_ref, pair_up_ref, query_ref, pairs_ref, log_ref, grad_ref,
    earlier_ref,
    grad_query_ref, grad_pairs_ref, grad_tokens_ref,
    keys_ref, cos_ref, left_ref, right_ref, grad_ready_ref, grad_keys_ref, grad_values_ref,
    sum_ref,
):
    length = tokens_ref.shape[0]
    rank = query_up_ref.shape[1]
    tail_start = rank + pair_up_ref.shape[1]
    block = min(QUERY_BLOCK, length)
    head = pl.program_id(0)

    @pl.when(head == 0)
    def _():
        write_tables(tokens_ref[:, tail_start:].astype(F32), cos_ref, left_ref, right_ref)
        sum_ref[...] = jnp.zeros_like(sum_ref)

    pairs = pairs_ref[...]
    lane = lane_of(pairs)
    keys_ref[...] = jnp.where(lane < NOPE, pairs, tokens_ref[:, tail_start:])
    shared = grad_ref[...].astype(F32)
    shared = jnp.where(head % 2 == 0, pltpu.roll(shared, NOPE, 1), shared)
    grad_ready_ref[...] = jnp.where(lane >= NOPE, shared, 0.0).astype(BF16)
    grad_keys_ref[...] = jnp.zeros_like(grad_keys_ref)
    grad_values_ref[...] = jnp.zeros_like(grad_values_ref)
    for start in range(0, length, block):
        rows = pl.ds(start, block)
        stop = start + block
        query = query_ref[rows, :]
        grad = grad_ready_ref[rows, :]
        scores = block_scores(query, keys_ref[0:stop, :], start)
        probs = jnp.exp(scores - log_ref[rows, 0:1])
        grad_probs = dot_rows(grad, pairs_ref[0:stop, :])
        delta = jnp.sum(probs * grad_probs, axis=-1, keepdims=True)
        grad_scores = (probs * (grad_probs - delta)).astype(BF16)
        grad_query = (
            jnp.dot(grad_scores, keys_ref[0:stop, :], preferred_element_type=F32) * SCORE_SCALE
        )
        grad_query = turn(
            grad_query, cos_ref[rows, :], left_ref[rows, :], right_ref[rows, :], -1.0
        ).astype(BF16)
        grad_query_ref[rows, :] = grad_query
        sum_ref[rows, 0:rank] += jnp.dot(
            grad_query, query_up_ref[...], preferred_element_type=F32
        )
        grad_keys_ref[:, 0:stop] += jnp.dot(query.T, grad_scores, preferred_element_type=F32)
        grad_values_ref[:, 0:stop] += jnp.dot(
            grad.T, probs.astype(BF16), preferred_element_type=F32
        )
    grad_keys = grad_keys_ref[...].T * SCORE_SCALE
    grad_pairs = jnp.where(lane < NOPE, grad_keys, grad_values_ref[...].T).astype(BF16)
    grad_pairs_ref[...] = grad_pairs
    sum_ref[:, rank:tail_start] += jnp.dot(
        grad_pairs, pair_up_ref[...], preferred_element_type=F32
    )
    sum_ref[:, tail_start:] += jnp.where((lane >= NOPE) & (lane < NOPE + ROPE), grad_keys, 0.0)

    @pl.when(head == pl.num_programs(0) - 1)
    def _():
        grad_tokens_ref[...] = sum_ref[...].astype(BF16)


def attend_back(tokens, query_up, pair_up, query, pairs, logs, grad, earlier):
    length, width = tokens.shape
    lanes = query.shape[1]
    heads = lanes // HEAD_LANES
    whole = pl.BlockSpec(memory_space=pltpu.VMEM)
    own = pl.BlockSpec((length, HEAD_LANES), lambda h: (0, h))
    table = pltpu.VMEM((length, HEAD_LANES), F32)
    turned = pltpu.VMEM((HEAD_LANES, length), F32)
    return pl.pallas_call(
        attend_back_kernel,
        grid=(heads,),
        in_specs=[
            whole,
            pl.BlockSpec((HEAD_LANES, query_up.shape[1]), lambda h: (h, 0)),
            pl.BlockSpec((HEAD_LANES, pair_up.shape[1]), lambda h: (h, 0)),
            own,
            own,
            own,
            pl.BlockSpec((length, HEAD_LANES), lambda h: (0, h // 2)),
            pl.BlockSpec(memory_space=pl.ANY),
        ],
        out_specs=[own, own, pl.BlockSpec((length, width), lambda h: (0, 0))],
        out_shape=[
            jax.ShapeDtypeStruct((length, lanes), BF16),
            jax.ShapeDtypeStruct((length, lanes), BF16),
            jax.ShapeDtypeStruct((length, width), BF16),
        ],
        scratch_shapes=[
            pltpu.VMEM((length, HEAD_LANES), BF16),
            table,
            table,
            table,
            pltpu.VMEM((length, HEAD_LANES), BF16),
            turned,
            turned,
            pltpu.VMEM((length, width), F32),
        ],
        compiler_params=pltpu.CompilerParams(vmem_limit_bytes=48 * 1024 * 1024),
        cost_estimate=pl.CostEstimate(
            flops=8 * lanes * length * length, bytes_accessed=14 * lanes * length,
            transcendentals=length * length * heads,
        ),
        name="attend_back",
    )(tokens, query_up, pair_up, query, pairs, logs, grad, earlier)


def ffn_kernel(weights_ref, rows_ref, grads_ref, both_ref, act_ref):
    def against(index, rows):
        return lax.dot_general(
            weights_ref[index], rows[...], (((1,), (1,)), ((), ())), preferred_element_type=F32
        )

    gate_values = against(0, rows_ref)
    upward = against(1, rows_ref)
    grad_activated = against(2, grads_ref)
    sigmoid_gate = jax.nn.sigmoid(gate_values)
    swish = gate_values * sigmoid_gate
    act_ref[...] = (swish * upward).astype(BF16)
    both_ref[1] = (grad_activated * swish).astype(BF16)
    both_ref[0] = (
        grad_activated * upward * sigmoid_gate * (1.0 + gate_values * (1.0 - sigmoid_gate))
    ).astype(BF16)


def ffn_hidden(weights, rows, grads):
    _, hidden, width = weights.shape
    count = rows.shape[0]
    block = hidden // 4
    whole = pl.BlockSpec(memory_space=pltpu.VMEM)
    own = pl.BlockSpec((block, count), lambda i: (i, 0))
    return pl.pallas_call(
        ffn_kernel,
        grid=(hidden // block,),
        in_specs=[pl.BlockSpec((3, block, width), lambda i: (0, i, 0)), whole, whole],
        out_specs=[pl.BlockSpec((2, block, count), lambda i: (0, i, 0)), own],
        out_shape=[
            jax.ShapeDtypeStruct((2, hidden, count), BF16),
            jax.ShapeDtypeStruct((hidden, count), BF16),
        ],
        compiler_params=pltpu.CompilerParams(vmem_limit_bytes=48 * 1024 * 1024),
        cost_estimate=pl.CostEstimate(
            flops=6 * hidden * width * count,
            bytes_accessed=6 * hidden * (width + count) + 4 * count * width,
            transcendentals=hidden * count,
        ),
        name="ffn_hidden",
    )(weights, rows, grads)


def ffn_grads_kernel(both_ref, act_ref, rows_ref, grads_ref, earlier_ref, out_ref):
    hidden = act_ref.shape[1]
    parts = ((both_ref[0, 0], rows_ref), (both_ref[1, 0], rows_ref), (act_ref[0], grads_ref))
    for place, (left, right) in enumerate(parts):
        out_ref[0, place * hidden : (place + 1) * hidden, :] = jnp.dot(
            left, right[...], preferred_element_type=F32
        ).astype(BF16)


def ffn_grads(grad_both, activated, rows, grads, earlier):
    steps, hidden, count = activated.shape
    width = rows.shape[1]
    whole = pl.BlockSpec(memory_space=pltpu.VMEM)
    own = pl.BlockSpec((1, hidden, count), lambda i: (i, 0, 0))
    return pl.pallas_call(
        ffn_grads_kernel,
        grid=(steps,),
        in_specs=[
            pl.BlockSpec((2, 1, hidden, count), lambda i: (0, i, 0, 0)),
            own,
            whole,
            whole,
            pl.BlockSpec(memory_space=pl.ANY),
        ],
        out_specs=pl.BlockSpec((1, 3 * hidden, width), lambda i: (i, 0, 0)),
        out_shape=jax.ShapeDtypeStruct((steps, 3 * hidden, width), BF16),
        compiler_params=pltpu.CompilerParams(vmem_limit_bytes=48 * 1024 * 1024),
        cost_estimate=pl.CostEstimate(
            flops=6 * steps * hidden * width * count,
            bytes_accessed=6 * steps * hidden * (width + count) + 4 * count * width,
            transcendentals=0,
        ),
        name="ffn_grads",
    )(grad_both, activated, rows, grads, earlier)


def done(value):
    last = value[(-1,) * value.ndim].astype(F32)
    return (last != last).astype(jnp.int32)


def hold(value, token):
    return jnp.where(token == 0, value, jnp.zeros_like(value))


def flip(value):
    count = lax.axis_size("seq")
    return lax.ppermute(value, "seq", [(i, i ^ 1) for i in range(count)])


def exchange(blocks, axis, groups=None):
    return lax.all_to_all(
        blocks, axis, split_axis=0, concat_axis=0, axis_index_groups=groups, tiled=True
    )


def repeat(value, count):
    return jnp.broadcast_to(value[None], (count,) + value.shape)


def choose(value, index, axis):
    return lax.dynamic_index_in_dim(value, index, axis, keepdims=False)


def per_device_heads(
    dp_count,
    seq_count,
    layer_input,
    positions,
    attn_gain,
    query_down,
    query_gain,
    query_up,
    latent_down,
    latent_gain,
    latent_up,
    output_proj,
    ffn_gain,
    ffn_gate,
    ffn_up,
    ffn_down,
    cotangent,
):
    tokens, width = layer_input.shape
    query_rank = query_down.shape[1]
    own_rows = query_down.shape[0]
    down_width = query_rank + KV_RANK + ROPE
    heads = HEADS // seq_count
    core = lax.axis_index("seq") % 2
    chips = seq_count // 2
    both = ("dp", "seq")
    devices = dp_count * seq_count
    length = seq_count * tokens
    place = lax.axis_index("dp")
    chip = lax.axis_index("seq") // 2
    same_core = [[2 * j + c for j in range(chips)] for c in range(2)]

    def across(value, steps):
        return lax.ppermute(value, "seq", [(i, i ^ (2 * steps)) for i in range(seq_count)])

    def place_in(whole, piece, index, axis):
        return lax.dynamic_update_slice_in_dim(whole, jnp.expand_dims(piece, axis), index, axis)

    def gather_plane(value, token=0, axis=0):
        shape = value.shape[:axis] + (chips,) + value.shape[axis:]
        whole = jnp.zeros(shape, value.dtype)
        for m in range(chips):
            piece = across(value, m) if m else value
            index = chip ^ m if m < chips - 1 else (chip ^ m) + token
            whole = place_in(whole, piece, index, axis)
        return whole

    def with_other_core(mine, axis=1):
        shape = mine.shape[:axis] + (2,) + mine.shape[axis:]
        whole = place_in(jnp.zeros(shape, mine.dtype), mine, core, axis)
        return place_in(whole, flip(mine), 1 - core, axis)

    def gather_seq(value, token=0, axis=0):
        return with_other_core(gather_plane(value, token, axis), axis + 1)

    def scatter_seq(mine, theirs, token=0):
        half = mine.astype(F32) + flip(theirs.astype(BF16)).astype(F32)
        half = half.astype(BF16)
        core_done = done(half)
        total = choose(half, chip, 0).astype(F32)
        for m in range(1, chips):
            total = total + across(choose(half, (chip ^ m) + token, 0), m).astype(F32)
        return total, core_done

    def gather_z(value):
        whole = jnp.zeros((dp_count,) + value.shape, value.dtype)
        for k, piece in enumerate(gather_dp(value, dp_count)):
            whole = lax.dynamic_update_index_in_dim(whole, piece, (place - k) % dp_count, 0)
        return whole

    def scatter_z(blocks, token=0):
        blocks = blocks.astype(BF16)
        total = choose(blocks, place, 0).astype(F32)
        for k in range(1, dp_count):
            block = choose(blocks, (place - k) % dp_count + token, 0)
            total = total + shift(block, "dp", dp_count, -k).astype(F32)
        return total

    def send_home(parts):
        total = parts[0].astype(F32)
        for k in range(1, dp_count):
            total = total + shift(parts[k], "dp", dp_count, -k).astype(F32)
        return total

    def by_core(value, token=0):
        value = value.reshape(chips, 2, tokens, value.shape[1])
        return choose(value, core, 1), choose(value, 1 - core + token, 1)

    padded_width = down_width + 4 + -(down_width + 4) % HEAD_LANES

    def column(gain):
        return jnp.pad(gain, (0, own_rows - gain.shape[0]))[:, None]

    down_own = jnp.concatenate(
        [
            query_down,
            latent_down,
            column(attn_gain),
            column(ffn_gain),
            column(query_gain),
            column(latent_gain),
            jnp.zeros((own_rows, padded_width - down_width - 4), BF16),
        ],
        1,
    )
    down_plane = gather_z(down_own)
    group_of = [s if s % 2 == 0 else (s + 2) % seq_count for s in range(seq_count)]
    to_owner = [
        (z * seq_count + s, group_of[s] * dp_count + z)
        for z in range(dp_count)
        for s in range(seq_count)
    ]
    to_group = [(owner, holder) for holder, owner in to_owner]
    up_rows = max(query_up.shape[1], latent_up.shape[1])
    up_packed = jnp.concatenate(
        [
            jnp.pad(query_up.T, ((0, up_rows - query_up.shape[1]), (0, 0))),
            jnp.pad(latent_up.T, ((0, up_rows - latent_up.shape[1]), (0, 0))),
        ],
        1,
    )
    up_moved = lax.ppermute(up_packed, both, to_group)
    up_group = exchange(repeat(hold(up_moved, done(down_plane)), dp_count), "dp")
    down_full = gather_seq(down_plane, done(up_group), 1).reshape(width, padded_width)
    gains = down_full[:, down_width : down_width + 4].T.astype(F32)
    attn_gain_full = gains[0]
    ffn_gain_full = gains[1]

    def short_gain(row, own):
        return row.reshape(devices, own_rows)[:, : own.shape[0]].reshape(-1)

    query_gain_full = short_gain(gains[2], query_gain)
    latent_gain_full = short_gain(gains[3], latent_gain)

    query_up_padded = jnp.pad(
        up_group[:, : query_up.shape[1], :query_rank].reshape(heads, NOPE + ROPE, query_rank),
        ((0, 0), (0, HEAD_LANES - NOPE - ROPE), (0, 0)),
    ).reshape(heads * HEAD_LANES, query_rank)
    latent_up_group = up_group[:, : latent_up.shape[1], query_rank:].reshape(-1, KV_RANK)

    inputs = layer_input.astype(F32)
    normal_one, inverse_one = norm_parts(inputs)
    normed = (normal_one * attn_gain_full).astype(BF16)
    down_out = jnp.dot(normed, down_full, preferred_element_type=F32)
    normal_query, inverse_query = norm_parts(down_out[:, :query_rank])
    query_normed = (normal_query * query_gain_full).astype(BF16)
    normal_latent, inverse_latent = norm_parts(down_out[:, query_rank : query_rank + KV_RANK])
    latent = (normal_latent * latent_gain_full).astype(BF16)
    cos_table, sin_table = rotary_tables(positions)
    rotary_keys = rotate(
        down_out[:, query_rank + KV_RANK : down_width], cos_table, sin_table
    ).astype(BF16)
    half = ROPE // 2

    def two_parts(table):
        high = table.astype(BF16)
        return [high, (table - high.astype(F32)).astype(BF16)]

    token_message = jnp.concatenate(
        [query_normed, latent]
        + two_parts(cos_table[:, :half])
        + two_parts(sin_table[:, :half])
        + [rotary_keys, jnp.zeros((tokens, HEAD_LANES - NOPE - ROPE), BF16)],
        1,
    )
    tail_start = query_rank + KV_RANK
    token_all = gather_seq(token_message).reshape(length, token_message.shape[1])
    proj_moved = lax.ppermute(output_proj, both, to_group)
    proj_group = exchange(repeat(hold(proj_moved, done(token_message)), dp_count), "dp")
    proj_group = proj_group.reshape(-1, width)
    proj_rows = jnp.pad(
        proj_group, ((0, (heads + 1) // 2 * HEAD_LANES - proj_group.shape[0]), (0, 0))
    )
    grad_out = cotangent.astype(F32)
    grad_two = (RESIDUAL_SCALE * grad_out).astype(BF16)
    grad_all = exchange(repeat(hold(grad_two, done(token_all)), dp_count), "dp")
    grad_rows = jnp.concatenate(
        [choose(grad_all, (place - k) % dp_count, 0) for k in range(dp_count)]
    )
    ffn_own = hold(jnp.stack([ffn_gate.T, ffn_up.T, ffn_down]), done(down_full))
    ffn_full = lax.all_gather(ffn_own, "seq", axis=1, tiled=True)

    query, pairs, attended, logs = attend(token_all, query_up_padded, latent_up_group)
    head_width = heads * VDIM
    attended_mine, attended_theirs = by_core(attended)
    branch, _ = scatter_seq(
        dot("mtk,kd->mtd", attended_mine, proj_rows),
        dot("mtk,kd->mtd", attended_theirs, proj_rows),
    )
    middle = inputs + RESIDUAL_SCALE * branch
    normal_two, inverse_two = norm_parts(middle)
    normed_two = hold((normal_two * ffn_gain_full).astype(BF16), done(grad_all))

    normed_rows = jnp.concatenate(gather_dp(normed_two, dp_count))
    proj_full = lax.all_gather(hold(proj_group, done(normed_two)), "seq", axis=0, tiled=True)
    own_hidden = ffn_down.shape[0]
    count = dp_count * tokens
    grad_both, activated = ffn_hidden(ffn_full, normed_rows, grad_rows)
    grad_part = dot("gft,gfd->td", grad_both, ffn_full[:2])
    grad_low = grad_part.astype(BF16)
    grad_normed_two = send_home(jnp.split(grad_low, dp_count))
    out_part = dot("ft,fd->td", activated, ffn_full[2]).astype(BF16)
    hidden_grads = ffn_grads(
        grad_both.reshape(2, seq_count, own_hidden, count),
        activated.reshape(seq_count, own_hidden, count),
        normed_rows,
        grad_rows,
        grad_low,
    )
    ffn_sums = lax.psum_scatter(hidden_grads, "seq", scatter_dimension=0).astype(F32)

    grad_middle_norm, grad_ffn_gain_part = norm_back(
        grad_normed_two, normal_two, inverse_two, ffn_gain_full
    )
    grad_middle = grad_out + grad_middle_norm
    grad_branch = hold(
        (RESIDUAL_SCALE * grad_middle).astype(BF16), done(out_part) + done(hidden_grads)
    )
    grad_attended = dot("td,kd->tk", grad_branch, proj_full).astype(BF16)
    grad_blocks = grad_attended.reshape(tokens, seq_count, head_width).transpose(1, 0, 2)
    grad_blocks = jnp.pad(
        grad_blocks, ((0, 0), (0, 0), (0, attended.shape[1] - head_width))
    )
    grad_blocks = grad_blocks.reshape(chips, 2, tokens, -1)
    arrived = flip(choose(grad_blocks, 1 - core, 1))
    by_chip = jnp.zeros((chips, 2) + grad_blocks.shape[2:], BF16)
    by_chip = place_in(by_chip, choose(grad_blocks, core, 1), core, 1)
    by_chip = place_in(by_chip, arrived, 1 - core, 1)
    grad_heads = jnp.zeros_like(by_chip)
    for m in range(chips):
        piece = choose(by_chip, chip ^ m, 0)
        grad_heads = place_in(grad_heads, across(piece, m) if m else piece, chip ^ m, 0)
    grad_heads = grad_heads.reshape(length, -1)
    branch_plane = gather_plane(hold(grad_branch, done(grad_heads)))
    grad_projected, grad_pairs, grad_tokens = attend_back(
        token_all,
        query_up_padded,
        latent_up_group,
        query,
        pairs,
        logs,
        grad_heads,
        out_part,
    )
    grad_own, _ = scatter_seq(*by_core(grad_tokens), done(branch_plane))
    out_slots = hold(out_part, done(grad_heads)).reshape(dp_count, tokens, width)
    out_blocks = jnp.stack(
        [choose(out_slots, (place - j) % dp_count, 0) for j in range(dp_count)]
    )
    out_all = exchange(out_blocks, "dp")
    layer_output = (middle + RESIDUAL_SCALE * jnp.sum(out_all.astype(F32), 0)).astype(BF16)
    grad_own = hold(grad_own, done(out_all))

    query_up_grads = dot("tk,tq->kq", grad_projected, token_all[:, :query_rank]).astype(BF16)
    query_up_grads = query_up_grads.reshape(heads, HEAD_LANES, query_rank)[:, : NOPE + ROPE]
    query_up_grads = query_up_grads.reshape(dp_count, -1, query_rank)
    latent_up_grads = dot("tk,tc->kc", grad_pairs, token_all[:, query_rank:tail_start])
    latent_up_grads = latent_up_grads.astype(BF16).reshape(dp_count, -1, KV_RANK)
    up_grads = jnp.concatenate(
        [
            jnp.pad(
                query_up_grads, ((0, 0), (0, up_rows - query_up_grads.shape[1]), (0, 0))
            ),
            jnp.pad(
                latent_up_grads, ((0, 0), (0, up_rows - latent_up_grads.shape[1]), (0, 0))
            ),
        ],
        2,
    )
    branch_all = with_other_core(branch_plane)
    proj_grads = dot("tk,td->kd", attended, branch_all.reshape(length, width)).astype(BF16)
    proj_grads = proj_grads[:head_width]
    group_grads = jnp.concatenate(
        [up_grads, proj_grads.reshape(dp_count, -1, up_grads.shape[2])], 1
    )
    grad_query_latent, grad_query_gain_part = norm_back(
        grad_own[:, :query_rank], normal_query, inverse_query, query_gain_full
    )
    grad_latent_norm, grad_latent_gain_part = norm_back(
        grad_own[:, query_rank : query_rank + KV_RANK],
        normal_latent,
        inverse_latent,
        latent_gain_full,
    )
    grad_down_out = jnp.concatenate(
        [
            grad_query_latent,
            grad_latent_norm,
            rotate_back(
                grad_own[:, tail_start + NOPE : tail_start + NOPE + ROPE], cos_table, sin_table
            ),
            jnp.zeros((tokens, padded_width - down_width), F32),
        ],
        -1,
    ).astype(BF16)
    grad_normed = dot("tc,dc->td", grad_down_out, down_full)
    grad_input_norm, grad_attn_gain_part = norm_back(
        grad_normed, normal_one, inverse_one, attn_gain_full
    )
    input_grad = grad_middle + grad_input_norm

    def short_column(grads, own):
        blocks = grads.reshape(devices, own.shape[0])
        return jnp.pad(blocks, ((0, 0), (0, own_rows - own.shape[0]))).reshape(-1)

    gain_columns = jnp.stack(
        [
            grad_attn_gain_part,
            grad_ffn_gain_part,
            short_column(grad_query_gain_part, query_gain),
            short_column(grad_latent_gain_part, latent_gain),
        ],
        1,
    )
    down_sums = dot("td,tc->dc", normed, grad_down_out) + jnp.pad(
        gain_columns, ((0, 0), (down_width, padded_width - down_width - 4))
    )
    down_sums = down_sums.astype(BF16).reshape(dp_count, chips, 2, own_rows, padded_width)
    down_sums = down_sums.transpose(1, 2, 0, 3, 4)
    sum_down, core_done = scatter_seq(
        choose(down_sums, core, 1),
        choose(down_sums, 1 - core + done(group_grads), 1),
    )
    group_sums = jnp.sum(exchange(hold(group_grads, core_done), "dp").astype(F32), 0)
    sum_down = scatter_z(sum_down, done(group_sums))
    group_sums = lax.ppermute(group_sums.astype(BF16), both, to_owner).astype(F32)
    sum_query_up = group_sums[: query_up.shape[1], :query_rank].T
    sum_latent_up = group_sums[: latent_up.shape[1], query_rank:].T
    sum_out = group_sums[up_rows:].reshape(-1, width)
    sum_gains = sum_down[:, down_width : down_width + 4].T
    return (
        layer_output,
        input_grad,
        sum_gains[0],
        sum_down[:, :query_rank],
        sum_gains[2][: query_gain.shape[0]],
        sum_query_up,
        sum_down[:, query_rank:down_width],
        sum_gains[3][: latent_gain.shape[0]],
        sum_latent_up,
        sum_out,
        sum_gains[1],
        ffn_sums[:own_hidden].T,
        ffn_sums[own_hidden : 2 * own_hidden].T,
        ffn_sums[2 * own_hidden :],
    )


def solution(mesh):
    both = ("dp", "seq")
    dp_count = mesh.shape["dp"]

    seq_count = mesh.shape["seq"]
    by_heads = HEADS % seq_count == 0 and seq_count & (seq_count - 1) == 0

    def run(*arrays):
        if by_heads:
            return per_device_heads(dp_count, seq_count, *arrays)
        return per_device_general(dp_count, *arrays)

    in_specs = (
        P(both, None),
        P(both),
        P(both),
        P(both, None),
        P(both),
        P(None, both),
        P(both, None),
        P(both),
        P(None, both),
        P(both, None),
        P(both),
        P(None, both),
        P(None, both),
        P(both, None),
        P(both, None),
    )
    out_specs = (
        P(both, None),
        P(both, None),
        P(both),
        P(both, None),
        P(both),
        P(None, both),
        P(both, None),
        P(both),
        P(None, both),
        P(both, None),
        P(both),
        P(None, both),
        P(None, both),
        P(both, None),
    )
    return jax.shard_map(run, mesh=mesh, in_specs=in_specs, out_specs=out_specs, check_vma=False)
```

```python
import math

import jax
import jax.numpy as jnp
from jax import lax
from jax.experimental import pallas as pl
from jax.experimental.pallas import tpu as pltpu
from jax.sharding import PartitionSpec as P

KV_RANK = 256
HEADS = 40
NOPE = 64
ROPE = 32
VDIM = 64


EPSILON = 1e-05
RESIDUAL_SCALE = 1.4 / math.sqrt(62.0)
F32 = jnp.float32
BF16 = jnp.bfloat16


def norm_parts(values):
    inverse = lax.rsqrt(jnp.mean(values * values, axis=-1, keepdims=True) + EPSILON)
    return (values * inverse, inverse)


def norm_back(grad_scaled, normalized, inverse, scale_gain):
    gain_grad = jnp.sum(grad_scaled * normalized, axis=0)
    grad_normal = grad_scaled * scale_gain
    values_grad = inverse * (
        grad_normal - normalized * jnp.mean(grad_normal * normalized, axis=-1, keepdims=True)
    )
    return (values_grad, gain_grad)


def rotary_tables(positions):
    half_width = ROPE // 2
    inverse = 10000.0 ** (-2.0 * jnp.arange(half_width, dtype=F32) / ROPE)
    angles = positions.astype(F32)[:, None] * inverse[None, :]
    cos_table = jnp.cos(angles)
    sin_table = jnp.sin(angles)
    return (
        jnp.concatenate([cos_table, cos_table], -1),
        jnp.concatenate([sin_table, sin_table], -1),
    )


def rotate(values, cos_table, sin_table):
    half_width = values.shape[-1] // 2
    turned = jnp.concatenate([-values[..., half_width:], values[..., :half_width]], -1)
    return values * cos_table + turned * sin_table


def rotate_back(grads, cos_table, sin_table):
    half_width = grads.shape[-1] // 2
    scaled = grads * sin_table
    return grads * cos_table + jnp.concatenate(
        [scaled[..., half_width:], -scaled[..., :half_width]], -1
    )


def score_block(query_block, keys_values, rotary_all, allowed):
    score_scale = (NOPE + ROPE) ** (-0.5)
    scores = jnp.einsum(
        "thd,lhd->htl",
        query_block[..., :NOPE],
        keys_values[..., :NOPE],
        preferred_element_type=F32,
    )
    scores = scores + jnp.einsum(
        "thr,lr->htl", query_block[..., NOPE:], rotary_all, preferred_element_type=F32
    )
    return jnp.where(allowed[None], scores * score_scale, -1e30)


def dot(spec, left, right):
    return jnp.einsum(spec, left, right, preferred_element_type=F32)


def shift(value, axis, count, step):
    return lax.ppermute(value, axis, [(i, (i + step) % count) for i in range(count)])


def gather_dp(value, count):
    return [value] + [shift(value, "dp", count, k) for k in range(1, count)]


def scatter_dp(parts, count):
    total = parts[0].astype(F32)
    for k in range(1, count):
        total = total + shift(parts[k].astype(BF16), "dp", count, -k).astype(F32)
    return total


def gather_all(rows, dp_count):
    by_place = jnp.stack(gather_dp(rows, dp_count))
    place = lax.axis_index("dp")
    order = (place - jnp.arange(dp_count)) % dp_count
    absolute = jnp.take(by_place, order, axis=0)
    whole = lax.all_gather(absolute, "seq", axis=1, tiled=True)
    return whole.reshape(-1, rows.shape[1])


def scatter_all(grads, dp_count):
    blocks = grads.astype(BF16).reshape(dp_count, -1, grads.shape[1])
    own_seq = lax.psum_scatter(blocks, "seq", scatter_dimension=1, tiled=True)
    place = lax.axis_index("dp")
    parts = [
        lax.dynamic_index_in_dim(own_seq, (place - k) % dp_count, 0, keepdims=False)
        for k in range(dp_count)
    ]
    return scatter_dp(parts, dp_count)


def per_device_general(
    dp_count,
    layer_input,
    positions,
    attn_gain,
    query_down,
    query_gain,
    query_up,
    latent_down,
    latent_gain,
    latent_up,
    output_proj,
    ffn_gain,
    ffn_gate,
    ffn_up,
    ffn_down,
    cotangent,
):
    token_count, width = layer_input.shape
    query_rank = query_down.shape[1]
    own_rows = query_down.shape[0]
    score_scale = (NOPE + ROPE) ** (-0.5)

    def column(gain):
        return jnp.pad(gain, (0, own_rows - gain.shape[0]))[:, None]

    down_width = query_rank + KV_RANK + ROPE
    pad_width = -(down_width + 4) % 128
    packed = jnp.concatenate(
        [
            query_down,
            latent_down,
            column(attn_gain),
            column(ffn_gain),
            column(query_gain),
            column(latent_gain),
            jnp.zeros((own_rows, pad_width), BF16),
        ],
        1,
    )
    packed_full = gather_all(packed, dp_count)
    down_full = packed_full[:, :down_width]
    gains = packed_full[:, down_width : down_width + 4].T.astype(F32)
    attn_gain_full = gains[0]
    ffn_gain_full = gains[1]

    def short_gain(row, own):
        return row.reshape(-1, own_rows)[:, : own.shape[0]].reshape(-1)

    query_gain_full = short_gain(gains[2], query_gain)
    latent_gain_full = short_gain(gains[3], latent_gain)

    query_up_full = gather_all(query_up.T, dp_count)
    latent_up_full = gather_all(latent_up.T, dp_count)
    proj_full = gather_all(output_proj, dp_count)
    gate_full = lax.all_gather(ffn_gate.T, "seq", axis=0, tiled=True)
    upward_full = lax.all_gather(ffn_up.T, "seq", axis=0, tiled=True)
    ffn_down_full = lax.all_gather(ffn_down, "seq", axis=0, tiled=True)

    grad_out = cotangent.astype(F32)
    grad_two = (RESIDUAL_SCALE * grad_out).astype(BF16)
    grad_rows = jnp.concatenate(gather_dp(grad_two, dp_count))

    inputs = layer_input.astype(F32)
    cos_table, sin_table = rotary_tables(positions)
    normal_one, inverse_one = norm_parts(inputs)
    normed = (normal_one * attn_gain_full).astype(BF16)
    down_out = jnp.dot(normed, down_full, preferred_element_type=F32)
    query_latent = down_out[:, :query_rank]
    compressed = down_out[:, query_rank:]
    normal_latent, inverse_latent = norm_parts(compressed[:, :KV_RANK])
    latent = (normal_latent * latent_gain_full).astype(BF16)
    rotary_keys = rotate(compressed[:, KV_RANK:], cos_table, sin_table).astype(BF16)
    keys_all = lax.all_gather(
        jnp.concatenate([latent, rotary_keys], -1), "seq", axis=0, tiled=True
    )
    latent_all = keys_all[:, :KV_RANK]
    rotary_all = keys_all[:, KV_RANK:]
    normal_query, inverse_query = norm_parts(query_latent)
    query_normed = (normal_query * query_gain_full).astype(BF16)
    projected = dot("tq,kq->tk", query_normed, query_up_full).reshape(
        token_count, HEADS, NOPE + ROPE
    )
    queries = jnp.concatenate(
        [
            projected[..., :NOPE],
            rotate(projected[..., NOPE:], cos_table[:, None, :], sin_table[:, None, :]),
        ],
        -1,
    ).astype(BF16)
    key_count = latent_all.shape[0]
    head_group = math.gcd(HEADS, 8)
    group_count = HEADS // head_group
    first_row = lax.axis_index("seq") * token_count
    allowed = (first_row + jnp.arange(token_count))[:, None] >= jnp.arange(key_count)[None, :]
    up_grouped = latent_up_full.reshape(group_count, head_group * (NOPE + VDIM), KV_RANK)
    query_grouped = queries.reshape(token_count, group_count, head_group, NOPE + ROPE).transpose(
        1, 0, 2, 3
    )

    def forward_group(operands):
        query_block, up_block = operands
        keys_values = dot("lc,kc->lk", latent_all, up_block).astype(BF16)
        keys_values = keys_values.reshape(key_count, head_group, NOPE + VDIM)
        scores = score_block(query_block, keys_values, rotary_all, allowed)
        row_peak = jnp.max(scores, axis=-1, keepdims=True)
        exponent_terms = jnp.exp(scores - row_peak)
        row_totals = jnp.sum(exponent_terms, axis=-1, keepdims=True)
        probabilities = (exponent_terms / row_totals).astype(BF16)
        attended_block = dot("htl,lhv->thv", probabilities, keys_values[..., NOPE:])
        return (keys_values, attended_block, (row_peak + jnp.log(row_totals))[..., 0])

    kept_values, attended_grouped, log_totals = lax.map(forward_group, (query_grouped, up_grouped))
    attended_low = (
        attended_grouped.transpose(1, 0, 2, 3).reshape(token_count, HEADS * VDIM).astype(BF16)
    )
    branch = jnp.dot(attended_low, proj_full, preferred_element_type=F32)
    middle = inputs + RESIDUAL_SCALE * branch
    normal_two, inverse_two = norm_parts(middle)
    normed_two = (normal_two * ffn_gain_full).astype(BF16)

    normed_rows = jnp.concatenate(gather_dp(normed_two, dp_count))
    gate_values = dot("td,fd->tf", normed_rows, gate_full)
    upward = dot("td,fd->tf", normed_rows, upward_full)
    grad_activated = dot("td,fd->tf", grad_rows, ffn_down_full)
    sigmoid_gate = jax.nn.sigmoid(gate_values)
    activated = (gate_values * sigmoid_gate * upward).astype(BF16)
    grad_upward = (grad_activated * gate_values * sigmoid_gate).astype(BF16)
    grad_gate = (
        grad_activated * upward * sigmoid_gate * (1.0 + gate_values * (1.0 - sigmoid_gate))
    ).astype(BF16)
    grad_normed_part = dot("tf,fd->td", grad_gate, gate_full) + dot(
        "tf,fd->td", grad_upward, upward_full
    )
    grad_normed_two = scatter_dp(jnp.split(grad_normed_part, dp_count), dp_count)
    down_part = dot("tf,fd->td", activated, ffn_down_full)
    layer_output = (
        middle + RESIDUAL_SCALE * scatter_dp(jnp.split(down_part, dp_count), dp_count)
    ).astype(BF16)

    def scatter_seq(grads):
        return lax.psum_scatter(
            grads.astype(BF16), "seq", scatter_dimension=0, tiled=True
        ).astype(F32)

    sum_down = scatter_seq(dot("tf,td->fd", activated, grad_rows))
    sum_gate = scatter_seq(dot("tf,td->fd", grad_gate, normed_rows)).T
    sum_up = scatter_seq(dot("tf,td->fd", grad_upward, normed_rows)).T

    grad_middle_norm, grad_ffn_gain_part = norm_back(
        grad_normed_two, normal_two, inverse_two, ffn_gain_full
    )
    grad_middle = grad_out + grad_middle_norm
    grad_branch = (RESIDUAL_SCALE * grad_middle).astype(BF16)
    sum_out = scatter_all(dot("tk,td->kd", attended_low, grad_branch), dp_count)
    grad_attended = dot("td,kd->tk", grad_branch, proj_full).astype(BF16)
    grad_att_grouped = grad_attended.reshape(token_count, group_count, head_group, VDIM).transpose(
        1, 0, 2, 3
    )

    def backward_group(carried, operands):
        latent_sum, rotary_sum = carried
        query_block, keys_values, log_block, grad_att, attended_block, up_block = operands
        scores = score_block(query_block, keys_values, rotary_all, allowed)
        probabilities = jnp.exp(scores - log_block[..., None])
        grad_probs = dot("thv,lhv->htl", grad_att, keys_values[..., NOPE:])
        row_delta = jnp.sum(grad_att.astype(F32) * attended_block, axis=-1)
        grad_scores = (probabilities * (grad_probs - jnp.transpose(row_delta)[..., None])).astype(
            BF16
        )
        grad_query_nope = dot("htl,lhd->thd", grad_scores, keys_values[..., :NOPE]) * score_scale
        grad_query_rot = dot("htl,lr->thr", grad_scores, rotary_all) * score_scale
        grad_keys = dot("htl,thd->lhd", grad_scores, query_block[..., :NOPE]) * score_scale
        grad_rotary_part = dot("htl,thr->lr", grad_scores, query_block[..., NOPE:]) * score_scale
        grad_values = dot("htl,thv->lhv", probabilities.astype(BF16), grad_att)
        grad_pairs = (
            jnp.concatenate([grad_keys, grad_values], -1)
            .astype(BF16)
            .reshape(key_count, head_group * (NOPE + VDIM))
        )
        grad_up_block = dot("lk,lc->kc", grad_pairs, latent_all)
        latent_sum = latent_sum + dot("lk,kc->lc", grad_pairs, up_block)
        return (
            (latent_sum, rotary_sum + grad_rotary_part),
            (jnp.concatenate([grad_query_nope, grad_query_rot], -1), grad_up_block),
        )

    start_sums = (
        jnp.zeros((key_count, KV_RANK), F32),
        jnp.zeros((key_count, ROPE), F32),
    )
    (grad_latent_all, grad_rotary_all), (grad_query_grouped, grad_up_grouped) = lax.scan(
        backward_group,
        start_sums,
        (query_grouped, kept_values, log_totals, grad_att_grouped, attended_grouped, up_grouped),
    )
    sum_latent_up = scatter_all(
        grad_up_grouped.reshape(HEADS * (NOPE + VDIM), KV_RANK), dp_count
    ).T
    grad_keys_own = lax.psum_scatter(
        jnp.concatenate([grad_latent_all, grad_rotary_all], -1).astype(BF16),
        "seq",
        scatter_dimension=0,
        tiled=True,
    ).astype(F32)
    grad_latent_own = grad_keys_own[:, :KV_RANK]
    grad_rotary_own = grad_keys_own[:, KV_RANK:]
    grad_queries = grad_query_grouped.transpose(1, 0, 2, 3).reshape(token_count, HEADS, NOPE + ROPE)
    grad_projected = jnp.concatenate(
        [
            grad_queries[..., :NOPE],
            rotate_back(grad_queries[..., NOPE:], cos_table[:, None, :], sin_table[:, None, :]),
        ],
        -1,
    )
    grad_projected = grad_projected.astype(BF16).reshape(token_count, HEADS * (NOPE + ROPE))
    sum_query_up = scatter_all(dot("tk,tq->kq", grad_projected, query_normed), dp_count).T
    grad_query_normed = dot("tk,kq->tq", grad_projected, query_up_full)
    grad_query_latent, grad_query_gain_part = norm_back(
        grad_query_normed, normal_query, inverse_query, query_gain_full
    )
    grad_latent_norm, grad_latent_gain_part = norm_back(
        grad_latent_own, normal_latent, inverse_latent, latent_gain_full
    )
    grad_down_out = jnp.concatenate(
        [
            grad_query_latent,
            grad_latent_norm,
            rotate_back(grad_rotary_own, cos_table, sin_table),
        ],
        -1,
    ).astype(BF16)
    grad_down_part = dot("td,tc->dc", normed, grad_down_out)
    grad_normed = dot("tc,dc->td", grad_down_out, down_full)
    grad_input_norm, grad_attn_gain_part = norm_back(
        grad_normed, normal_one, inverse_one, attn_gain_full
    )
    input_grad = grad_middle + grad_input_norm

    def short_column(grads, own):
        blocks = grads.reshape(-1, own.shape[0])
        return jnp.pad(blocks, ((0, 0), (0, own_rows - own.shape[0]))).reshape(-1)

    gain_columns = jnp.stack(
        [
            grad_attn_gain_part,
            grad_ffn_gain_part,
            short_column(grad_query_gain_part, query_gain),
            short_column(grad_latent_gain_part, latent_gain),
        ],
        1,
    )
    sum_packed = scatter_all(
        jnp.concatenate([grad_down_part, gain_columns, jnp.zeros((width, pad_width), F32)], 1),
        dp_count,
    )
    sum_gains = sum_packed[:, down_width : down_width + 4].T
    return (
        layer_output,
        input_grad,
        sum_gains[0],
        sum_packed[:, :query_rank],
        sum_gains[2][: query_gain.shape[0]],
        sum_query_up,
        sum_packed[:, query_rank:down_width],
        sum_gains[3][: latent_gain.shape[0]],
        sum_latent_up,
        sum_out,
        sum_gains[1],
        sum_gate,
        sum_up,
        sum_down,
    )


HEAD_LANES = 128
SCORE_SCALE = (NOPE + ROPE) ** (-0.5)
QUERY_BLOCK = 256


def lane_of(values):
    return lax.broadcasted_iota(jnp.int32, values.shape, 1)


def dot_rows(left, right):
    return lax.dot_general(left, right, (((1,), (1,)), ((), ())), preferred_element_type=F32)


def block_scores(query, keys, start):
    scores = dot_rows(query, keys)
    row = start + lax.broadcasted_iota(jnp.int32, scores.shape, 0)
    return jnp.where(row >= lane_of(scores), scores * SCORE_SCALE, -1e30)


def write_tables(tail, cos_ref, left_ref, right_ref):
    half = ROPE // 2
    lane = lane_of(tail)
    sums = tail + pltpu.roll(tail, HEAD_LANES - half, 1)
    upper = (lane >= NOPE + half) & (lane < NOPE + ROPE)
    lower = (lane >= NOPE) & (lane < NOPE + half)
    cos = jnp.where(lower, pltpu.roll(sums, NOPE, 1), pltpu.roll(sums, NOPE + half, 1))
    cos_ref[...] = jnp.where(lane < NOPE, 1.0, jnp.where(lower | upper, cos, 0.0))
    left_ref[...] = jnp.where(lower, -pltpu.roll(sums, NOPE - 2 * half, 1), 0.0)
    right_ref[...] = jnp.where(upper, pltpu.roll(sums, NOPE - half, 1), 0.0)


def turn(values, cos, left, right, sign):
    half = ROPE // 2
    return (
        values * cos
        + sign * (pltpu.roll(values, HEAD_LANES - half, 1) * left)
        + sign * (pltpu.roll(values, half, 1) * right)
    )


def attend_kernel(
    tokens_ref, query_up_ref, pair_up_ref,
    query_ref, pairs_ref, attended_ref, log_ref, keys_ref, cos_ref, left_ref, right_ref,
):
    length = tokens_ref.shape[0]
    rank = query_up_ref.shape[1]
    tail_start = rank + pair_up_ref.shape[1]
    block = min(QUERY_BLOCK, length)
    head = pl.program_id(0)

    @pl.when(head == 0)
    def _():
        write_tables(tokens_ref[:, tail_start:].astype(F32), cos_ref, left_ref, right_ref)

    pairs = dot_rows(tokens_ref[:, rank:tail_start], pair_up_ref[...]).astype(BF16)
    pairs_ref[...] = pairs
    keys_ref[...] = jnp.where(lane_of(pairs) < NOPE, pairs, tokens_ref[:, tail_start:])
    for start in range(0, length, block):
        rows = pl.ds(start, block)
        stop = start + block
        projected = dot_rows(tokens_ref[rows, 0:rank], query_up_ref[...])
        query = turn(
            projected, cos_ref[rows, :], left_ref[rows, :], right_ref[rows, :], 1.0
        ).astype(BF16)
        query_ref[rows, :] = query
        scores = block_scores(query, keys_ref[0:stop, :], start)
        peak = jnp.max(scores, axis=-1, keepdims=True)
        terms = jnp.exp(scores - peak)
        totals = jnp.sum(terms, axis=-1, keepdims=True)
        probs = (terms / totals).astype(BF16)
        mixed = jnp.dot(probs, pairs_ref[0:stop, :], preferred_element_type=F32)
        log_ref[rows, :] = jnp.broadcast_to(peak + jnp.log(totals), mixed.shape)
        lane = lane_of(mixed)

        @pl.when(head % 2 == 0)
        def _():
            attended_ref[rows, :] = jnp.where(
                lane < NOPE, pltpu.roll(mixed, NOPE, 1), 0.0
            ).astype(BF16)

        @pl.when(head % 2 == 1)
        def _():
            attended_ref[rows, :] = jnp.where(
                lane < NOPE, attended_ref[rows, :].astype(F32), mixed
            ).astype(BF16)


def attend(tokens, query_up, pair_up):
    length = tokens.shape[0]
    lanes = query_up.shape[0]
    heads = lanes // HEAD_LANES
    whole = pl.BlockSpec(memory_space=pltpu.VMEM)
    own = pl.BlockSpec((length, HEAD_LANES), lambda h: (0, h))
    table = pltpu.VMEM((length, HEAD_LANES), F32)
    return pl.pallas_call(
        attend_kernel,
        grid=(heads,),
        in_specs=[
            whole,
            pl.BlockSpec((HEAD_LANES, query_up.shape[1]), lambda h: (h, 0)),
            pl.BlockSpec((HEAD_LANES, pair_up.shape[1]), lambda h: (h, 0)),
        ],
        out_specs=[
            own, own, pl.BlockSpec((length, HEAD_LANES), lambda h: (0, h // 2)), own
        ],
        out_shape=[
            jax.ShapeDtypeStruct((length, lanes), BF16),
            jax.ShapeDtypeStruct((length, lanes), BF16),
            jax.ShapeDtypeStruct((length, (heads + 1) // 2 * HEAD_LANES), BF16),
            jax.ShapeDtypeStruct((length, lanes), F32),
        ],
        scratch_shapes=[pltpu.VMEM((length, HEAD_LANES), BF16), table, table, table],
        compiler_params=pltpu.CompilerParams(vmem_limit_bytes=40 * 1024 * 1024),
        cost_estimate=pl.CostEstimate(
            flops=3 * lanes * length * length, bytes_accessed=12 * lanes * length,
            transcendentals=length * length * heads,
        ),
        name="attend",
    )(tokens, query_up, pair_up)


def attend_back_kernel(
    tokens_ref, query_up_ref, pair_up_ref, query_ref, pairs_ref, log_ref, grad_ref,
    earlier_ref,
    grad_query_ref, grad_pairs_ref, grad_tokens_ref,
    keys_ref, cos_ref, left_ref, right_ref, grad_ready_ref, grad_keys_ref, grad_values_ref,
    sum_ref,
):
    length = tokens_ref.shape[0]
    rank = query_up_ref.shape[1]
    tail_start = rank + pair_up_ref.shape[1]
    block = min(QUERY_BLOCK, length)
    head = pl.program_id(0)

    @pl.when(head == 0)
    def _():
        write_tables(tokens_ref[:, tail_start:].astype(F32), cos_ref, left_ref, right_ref)
        sum_ref[...] = jnp.zeros_like(sum_ref)

    pairs = pairs_ref[...]
    lane = lane_of(pairs)
    keys_ref[...] = jnp.where(lane < NOPE, pairs, tokens_ref[:, tail_start:])
    shared = grad_ref[...].astype(F32)
    shared = jnp.where(head % 2 == 0, pltpu.roll(shared, NOPE, 1), shared)
    grad_ready_ref[...] = jnp.where(lane >= NOPE, shared, 0.0).astype(BF16)
    grad_keys_ref[...] = jnp.zeros_like(grad_keys_ref)
    grad_values_ref[...] = jnp.zeros_like(grad_values_ref)
    for start in range(0, length, block):
        rows = pl.ds(start, block)
        stop = start + block
        query = query_ref[rows, :]
        grad = grad_ready_ref[rows, :]
        scores = block_scores(query, keys_ref[0:stop, :], start)
        probs = jnp.exp(scores - log_ref[rows, 0:1])
        grad_probs = dot_rows(grad, pairs_ref[0:stop, :])
        delta = jnp.sum(probs * grad_probs, axis=-1, keepdims=True)
        grad_scores = (probs * (grad_probs - delta)).astype(BF16)
        grad_query = (
            jnp.dot(grad_scores, keys_ref[0:stop, :], preferred_element_type=F32) * SCORE_SCALE
        )
        grad_query = turn(
            grad_query, cos_ref[rows, :], left_ref[rows, :], right_ref[rows, :], -1.0
        ).astype(BF16)
        grad_query_ref[rows, :] = grad_query
        sum_ref[rows, 0:rank] += jnp.dot(
            grad_query, query_up_ref[...], preferred_element_type=F32
        )
        grad_keys_ref[:, 0:stop] += jnp.dot(query.T, grad_scores, preferred_element_type=F32)
        grad_values_ref[:, 0:stop] += jnp.dot(
            grad.T, probs.astype(BF16), preferred_element_type=F32
        )
    grad_keys = grad_keys_ref[...].T * SCORE_SCALE
    grad_pairs = jnp.where(lane < NOPE, grad_keys, grad_values_ref[...].T).astype(BF16)
    grad_pairs_ref[...] = grad_pairs
    sum_ref[:, rank:tail_start] += jnp.dot(
        grad_pairs, pair_up_ref[...], preferred_element_type=F32
    )
    sum_ref[:, tail_start:] += jnp.where((lane >= NOPE) & (lane < NOPE + ROPE), grad_keys, 0.0)

    @pl.when(head == pl.num_programs(0) - 1)
    def _():
        grad_tokens_ref[...] = sum_ref[...].astype(BF16)


def attend_back(tokens, query_up, pair_up, query, pairs, logs, grad, earlier):
    length, width = tokens.shape
    lanes = query.shape[1]
    heads = lanes // HEAD_LANES
    whole = pl.BlockSpec(memory_space=pltpu.VMEM)
    own = pl.BlockSpec((length, HEAD_LANES), lambda h: (0, h))
    table = pltpu.VMEM((length, HEAD_LANES), F32)
    turned = pltpu.VMEM((HEAD_LANES, length), F32)
    return pl.pallas_call(
        attend_back_kernel,
        grid=(heads,),
        in_specs=[
            whole,
            pl.BlockSpec((HEAD_LANES, query_up.shape[1]), lambda h: (h, 0)),
            pl.BlockSpec((HEAD_LANES, pair_up.shape[1]), lambda h: (h, 0)),
            own,
            own,
            own,
            pl.BlockSpec((length, HEAD_LANES), lambda h: (0, h // 2)),
            pl.BlockSpec(memory_space=pl.ANY),
        ],
        out_specs=[own, own, pl.BlockSpec((length, width), lambda h: (0, 0))],
        out_shape=[
            jax.ShapeDtypeStruct((length, lanes), BF16),
            jax.ShapeDtypeStruct((length, lanes), BF16),
            jax.ShapeDtypeStruct((length, width), BF16),
        ],
        scratch_shapes=[
            pltpu.VMEM((length, HEAD_LANES), BF16),
            table,
            table,
            table,
            pltpu.VMEM((length, HEAD_LANES), BF16),
            turned,
            turned,
            pltpu.VMEM((length, width), F32),
        ],
        compiler_params=pltpu.CompilerParams(vmem_limit_bytes=48 * 1024 * 1024),
        cost_estimate=pl.CostEstimate(
            flops=8 * lanes * length * length, bytes_accessed=14 * lanes * length,
            transcendentals=length * length * heads,
        ),
        name="attend_back",
    )(tokens, query_up, pair_up, query, pairs, logs, grad, earlier)


def ffn_kernel(weights_ref, rows_ref, grads_ref, both_ref, act_ref):
    def against(index, rows):
        return lax.dot_general(
            weights_ref[index], rows[...], (((1,), (1,)), ((), ())), preferred_element_type=F32
        )

    gate_values = against(0, rows_ref)
    upward = against(1, rows_ref)
    grad_activated = against(2, grads_ref)
    sigmoid_gate = jax.nn.sigmoid(gate_values)
    swish = gate_values * sigmoid_gate
    act_ref[...] = (swish * upward).astype(BF16)
    both_ref[1] = (grad_activated * swish).astype(BF16)
    both_ref[0] = (
        grad_activated * upward * sigmoid_gate * (1.0 + gate_values * (1.0 - sigmoid_gate))
    ).astype(BF16)


def ffn_hidden(weights, rows, grads):
    _, hidden, width = weights.shape
    count = rows.shape[0]
    block = hidden // 4
    whole = pl.BlockSpec(memory_space=pltpu.VMEM)
    own = pl.BlockSpec((block, count), lambda i: (i, 0))
    return pl.pallas_call(
        ffn_kernel,
        grid=(hidden // block,),
        in_specs=[pl.BlockSpec((3, block, width), lambda i: (0, i, 0)), whole, whole],
        out_specs=[pl.BlockSpec((2, block, count), lambda i: (0, i, 0)), own],
        out_shape=[
            jax.ShapeDtypeStruct((2, hidden, count), BF16),
            jax.ShapeDtypeStruct((hidden, count), BF16),
        ],
        compiler_params=pltpu.CompilerParams(vmem_limit_bytes=48 * 1024 * 1024),
        cost_estimate=pl.CostEstimate(
            flops=6 * hidden * width * count,
            bytes_accessed=6 * hidden * (width + count) + 4 * count * width,
            transcendentals=hidden * count,
        ),
        name="ffn_hidden",
    )(weights, rows, grads)


def ffn_grads_kernel(both_ref, act_ref, rows_ref, grads_ref, out_ref):
    parts = ((both_ref[0, 0], rows_ref), (both_ref[1, 0], rows_ref), (act_ref[0], grads_ref))
    for place, (left, right) in enumerate(parts):
        out_ref[0, place] = jnp.dot(left, right[...], preferred_element_type=F32).astype(BF16)


def ffn_grads(grad_both, activated, rows, grads):
    steps, hidden, count = activated.shape
    width = rows.shape[1]
    whole = pl.BlockSpec(memory_space=pltpu.VMEM)
    own = pl.BlockSpec((1, hidden, count), lambda i: (i, 0, 0))
    return pl.pallas_call(
        ffn_grads_kernel,
        grid=(steps,),
        in_specs=[
            pl.BlockSpec((2, 1, hidden, count), lambda i: (0, i, 0, 0)),
            own,
            whole,
            whole,
        ],
        out_specs=pl.BlockSpec((1, 3, hidden, width), lambda i: (i, 0, 0, 0)),
        out_shape=jax.ShapeDtypeStruct((steps, 3, hidden, width), BF16),
        compiler_params=pltpu.CompilerParams(vmem_limit_bytes=48 * 1024 * 1024),
        cost_estimate=pl.CostEstimate(
            flops=6 * steps * hidden * width * count,
            bytes_accessed=6 * steps * hidden * (width + count) + 4 * count * width,
            transcendentals=0,
        ),
        name="ffn_grads",
    )(grad_both, activated, rows, grads)


def ffn_sums_kernel(sums_ref, gate_ref, up_ref, down_ref):
    gate_ref[...] = sums_ref[0].astype(F32).T
    up_ref[...] = sums_ref[1].astype(F32).T
    down_ref[...] = sums_ref[2].astype(F32)


def ffn_outputs(sums):
    _, hidden, width = sums.shape
    whole = pl.BlockSpec(memory_space=pltpu.VMEM)
    turned = jax.ShapeDtypeStruct((width, hidden), F32)
    return pl.pallas_call(
        ffn_sums_kernel,
        in_specs=[whole],
        out_specs=[whole, whole, whole],
        out_shape=[turned, turned, jax.ShapeDtypeStruct((hidden, width), F32)],
        compiler_params=pltpu.CompilerParams(vmem_limit_bytes=40 * 1024 * 1024),
        cost_estimate=pl.CostEstimate(
            flops=3 * hidden * width, bytes_accessed=18 * hidden * width, transcendentals=0
        ),
        name="ffn_outputs",
    )(sums)


def done(value):
    last = value[(-1,) * value.ndim].astype(F32)
    return (last != last).astype(jnp.int32)


def hold(value, token):
    return jnp.where(token == 0, value, jnp.zeros_like(value))


def flip(value):
    count = lax.axis_size("seq")
    return lax.ppermute(value, "seq", [(i, i ^ 1) for i in range(count)])


def exchange(blocks, axis, groups=None):
    return lax.all_to_all(
        blocks, axis, split_axis=0, concat_axis=0, axis_index_groups=groups, tiled=True
    )


def repeat(value, count):
    return jnp.broadcast_to(value[None], (count,) + value.shape)


def choose(value, index, axis):
    return lax.dynamic_index_in_dim(value, index, axis, keepdims=False)


def per_device_heads(
    dp_count,
    seq_count,
    layer_input,
    positions,
    attn_gain,
    query_down,
    query_gain,
    query_up,
    latent_down,
    latent_gain,
    latent_up,
    output_proj,
    ffn_gain,
    ffn_gate,
    ffn_up,
    ffn_down,
    cotangent,
):
    tokens, width = layer_input.shape
    query_rank = query_down.shape[1]
    own_rows = query_down.shape[0]
    down_width = query_rank + KV_RANK + ROPE
    heads = HEADS // seq_count
    core = lax.axis_index("seq") % 2
    chips = seq_count // 2
    both = ("dp", "seq")
    devices = dp_count * seq_count
    length = seq_count * tokens
    place = lax.axis_index("dp")
    chip = lax.axis_index("seq") // 2
    same_core = [[2 * j + c for j in range(chips)] for c in range(2)]

    def across(value, steps):
        return lax.ppermute(value, "seq", [(i, i ^ (2 * steps)) for i in range(seq_count)])

    def place_in(whole, piece, index, axis):
        return lax.dynamic_update_slice_in_dim(whole, jnp.expand_dims(piece, axis), index, axis)

    def gather_plane(value, token=0, axis=0):
        shape = value.shape[:axis] + (chips,) + value.shape[axis:]
        whole = jnp.zeros(shape, value.dtype)
        for m in range(chips):
            piece = across(value, m) if m else value
            index = chip ^ m if m < chips - 1 else (chip ^ m) + token
            whole = place_in(whole, piece, index, axis)
        return whole

    def with_other_core(mine, axis=1):
        shape = mine.shape[:axis] + (2,) + mine.shape[axis:]
        whole = place_in(jnp.zeros(shape, mine.dtype), mine, core, axis)
        return place_in(whole, flip(mine), 1 - core, axis)

    def gather_seq(value, token=0, axis=0):
        return with_other_core(gather_plane(value, token, axis), axis + 1)

    def scatter_seq(mine, theirs, token=0):
        half = mine.astype(F32) + flip(theirs.astype(BF16)).astype(F32)
        half = half.astype(BF16)
        core_done = done(half)
        total = choose(half, chip, 0).astype(F32)
        for m in range(1, chips):
            total = total + across(choose(half, (chip ^ m) + token, 0), m).astype(F32)
        return total, core_done

    def gather_z(value):
        whole = jnp.zeros((dp_count,) + value.shape, value.dtype)
        for k, piece in enumerate(gather_dp(value, dp_count)):
            whole = lax.dynamic_update_index_in_dim(whole, piece, (place - k) % dp_count, 0)
        return whole

    def scatter_z(blocks, token=0):
        blocks = blocks.astype(BF16)
        total = choose(blocks, place, 0).astype(F32)
        for k in range(1, dp_count):
            block = choose(blocks, (place - k) % dp_count + token, 0)
            total = total + shift(block, "dp", dp_count, -k).astype(F32)
        return total

    def send_home(parts):
        total = parts[0].astype(F32)
        for k in range(1, dp_count):
            total = total + shift(parts[k], "dp", dp_count, -k).astype(F32)
        return total

    def by_core(value, token=0):
        value = value.reshape(chips, 2, tokens, value.shape[1])
        return choose(value, core, 1), choose(value, 1 - core + token, 1)

    padded_width = down_width + 4 + -(down_width + 4) % HEAD_LANES

    def column(gain):
        return jnp.pad(gain, (0, own_rows - gain.shape[0]))[:, None]

    down_own = jnp.concatenate(
        [
            query_down,
            latent_down,
            column(attn_gain),
            column(ffn_gain),
            column(query_gain),
            column(latent_gain),
            jnp.zeros((own_rows, padded_width - down_width - 4), BF16),
        ],
        1,
    )
    down_plane = gather_z(down_own)
    group_of = [s if s % 2 == 0 else (s + 2) % seq_count for s in range(seq_count)]
    to_owner = [
        (z * seq_count + s, group_of[s] * dp_count + z)
        for z in range(dp_count)
        for s in range(seq_count)
    ]
    to_group = [(owner, holder) for holder, owner in to_owner]
    up_rows = max(query_up.shape[1], latent_up.shape[1])
    up_packed = jnp.concatenate(
        [
            jnp.pad(query_up.T, ((0, up_rows - query_up.shape[1]), (0, 0))),
            jnp.pad(latent_up.T, ((0, up_rows - latent_up.shape[1]), (0, 0))),
        ],
        1,
    )
    up_moved = lax.ppermute(up_packed, both, to_group)
    up_group = exchange(repeat(hold(up_moved, done(down_plane)), dp_count), "dp")
    down_full = gather_seq(down_plane, done(up_group), 1).reshape(width, padded_width)
    gains = down_full[:, down_width : down_width + 4].T.astype(F32)
    attn_gain_full = gains[0]
    ffn_gain_full = gains[1]

    def short_gain(row, own):
        return row.reshape(devices, own_rows)[:, : own.shape[0]].reshape(-1)

    query_gain_full = short_gain(gains[2], query_gain)
    latent_gain_full = short_gain(gains[3], latent_gain)

    query_up_padded = jnp.pad(
        up_group[:, : query_up.shape[1], :query_rank].reshape(heads, NOPE + ROPE, query_rank),
        ((0, 0), (0, HEAD_LANES - NOPE - ROPE), (0, 0)),
    ).reshape(heads * HEAD_LANES, query_rank)
    latent_up_group = up_group[:, : latent_up.shape[1], query_rank:].reshape(-1, KV_RANK)

    inputs = layer_input.astype(F32)
    normal_one, inverse_one = norm_parts(inputs)
    normed = (normal_one * attn_gain_full).astype(BF16)
    down_out = jnp.dot(normed, down_full, preferred_element_type=F32)
    normal_query, inverse_query = norm_parts(down_out[:, :query_rank])
    query_normed = (normal_query * query_gain_full).astype(BF16)
    normal_latent, inverse_latent = norm_parts(down_out[:, query_rank : query_rank + KV_RANK])
    latent = (normal_latent * latent_gain_full).astype(BF16)
    cos_table, sin_table = rotary_tables(positions)
    rotary_keys = rotate(
        down_out[:, query_rank + KV_RANK : down_width], cos_table, sin_table
    ).astype(BF16)
    half = ROPE // 2

    def two_parts(table):
        high = table.astype(BF16)
        return [high, (table - high.astype(F32)).astype(BF16)]

    token_message = jnp.concatenate(
        [query_normed, latent]
        + two_parts(cos_table[:, :half])
        + two_parts(sin_table[:, :half])
        + [rotary_keys, jnp.zeros((tokens, HEAD_LANES - NOPE - ROPE), BF16)],
        1,
    )
    tail_start = query_rank + KV_RANK
    token_all = gather_seq(token_message).reshape(length, token_message.shape[1])
    proj_moved = lax.ppermute(output_proj, both, to_group)
    proj_group = exchange(repeat(hold(proj_moved, done(token_message)), dp_count), "dp")
    proj_group = proj_group.reshape(-1, width)
    proj_rows = jnp.pad(
        proj_group, ((0, (heads + 1) // 2 * HEAD_LANES - proj_group.shape[0]), (0, 0))
    )
    grad_out = cotangent.astype(F32)
    grad_two = (RESIDUAL_SCALE * grad_out).astype(BF16)
    grad_all = exchange(repeat(hold(grad_two, done(token_all)), dp_count), "dp")
    grad_rows = jnp.concatenate(
        [choose(grad_all, (place - k) % dp_count, 0) for k in range(dp_count)]
    )
    ffn_own = hold(jnp.stack([ffn_gate.T, ffn_up.T, ffn_down]), done(down_plane))
    ffn_full = lax.all_gather(ffn_own, "seq", axis=1, tiled=True)

    query, pairs, attended, logs = attend(token_all, query_up_padded, latent_up_group)
    head_width = heads * VDIM
    attended_mine, attended_theirs = by_core(attended)
    branch, _ = scatter_seq(
        dot("mtk,kd->mtd", attended_mine, proj_rows),
        dot("mtk,kd->mtd", attended_theirs, proj_rows),
    )
    middle = inputs + RESIDUAL_SCALE * branch
    normal_two, inverse_two = norm_parts(middle)
    normed_two = hold((normal_two * ffn_gain_full).astype(BF16), done(grad_all))

    normed_rows = jnp.concatenate(gather_dp(normed_two, dp_count))
    proj_full = lax.all_gather(hold(proj_group, done(normed_two)), "seq", axis=0, tiled=True)
    own_hidden = ffn_down.shape[0]
    count = dp_count * tokens
    grad_both, activated = ffn_hidden(ffn_full, normed_rows, grad_rows)
    grad_part = dot("gft,gfd->td", grad_both, ffn_full[:2])
    grad_normed_two = send_home(jnp.split(grad_part.astype(BF16), dp_count))
    out_part = dot("ft,fd->td", activated, ffn_full[2]).astype(BF16)
    ffn_sums = lax.psum_scatter(
        ffn_grads(
            grad_both.reshape(2, seq_count, own_hidden, count),
            activated.reshape(seq_count, own_hidden, count),
            normed_rows,
            grad_rows,
        ),
        "seq",
        scatter_dimension=0,
    )
    sum_gate, sum_up, sum_down_rows = ffn_outputs(ffn_sums)

    grad_middle_norm, grad_ffn_gain_part = norm_back(
        grad_normed_two, normal_two, inverse_two, ffn_gain_full
    )
    grad_middle = grad_out + grad_middle_norm
    grad_branch = (RESIDUAL_SCALE * grad_middle).astype(BF16)
    grad_attended = dot("td,kd->tk", grad_branch, proj_full).astype(BF16)
    grad_blocks = grad_attended.reshape(tokens, seq_count, head_width).transpose(1, 0, 2)
    grad_blocks = jnp.pad(
        grad_blocks, ((0, 0), (0, 0), (0, attended.shape[1] - head_width))
    )
    grad_blocks = grad_blocks.reshape(chips, 2, tokens, -1)
    arrived = flip(choose(grad_blocks, 1 - core, 1))
    by_chip = jnp.zeros((chips, 2) + grad_blocks.shape[2:], BF16)
    by_chip = place_in(by_chip, choose(grad_blocks, core, 1), core, 1)
    by_chip = place_in(by_chip, arrived, 1 - core, 1)
    grad_heads = jnp.zeros_like(by_chip)
    for m in range(chips):
        piece = choose(by_chip, chip ^ m, 0)
        grad_heads = place_in(grad_heads, across(piece, m) if m else piece, chip ^ m, 0)
    grad_heads = grad_heads.reshape(length, -1)
    branch_plane = gather_plane(hold(grad_branch, done(grad_heads)))
    grad_projected, grad_pairs, grad_tokens = attend_back(
        token_all,
        query_up_padded,
        latent_up_group,
        query,
        pairs,
        logs,
        grad_heads,
        out_part,
    )
    grad_own, _ = scatter_seq(*by_core(grad_tokens), done(branch_plane))
    out_slots = hold(out_part, done(grad_heads)).reshape(dp_count, tokens, width)
    out_blocks = jnp.stack(
        [choose(out_slots, (place - j) % dp_count, 0) for j in range(dp_count)]
    )
    out_all = exchange(out_blocks, "dp")
    layer_output = (middle + RESIDUAL_SCALE * jnp.sum(out_all.astype(F32), 0)).astype(BF16)
    grad_own = hold(grad_own, done(out_all))

    query_up_grads = dot("tk,tq->kq", grad_projected, token_all[:, :query_rank]).astype(BF16)
    query_up_grads = query_up_grads.reshape(heads, HEAD_LANES, query_rank)[:, : NOPE + ROPE]
    query_up_grads = query_up_grads.reshape(dp_count, -1, query_rank)
    latent_up_grads = dot("tk,tc->kc", grad_pairs, token_all[:, query_rank:tail_start])
    latent_up_grads = latent_up_grads.astype(BF16).reshape(dp_count, -1, KV_RANK)
    up_grads = jnp.concatenate(
        [
            jnp.pad(
                query_up_grads, ((0, 0), (0, up_rows - query_up_grads.shape[1]), (0, 0))
            ),
            jnp.pad(
                latent_up_grads, ((0, 0), (0, up_rows - latent_up_grads.shape[1]), (0, 0))
            ),
        ],
        2,
    )
    branch_all = with_other_core(branch_plane)
    proj_grads = dot("tk,td->kd", attended, branch_all.reshape(length, width)).astype(BF16)
    proj_grads = proj_grads[:head_width]
    group_grads = jnp.concatenate(
        [up_grads, proj_grads.reshape(dp_count, -1, up_grads.shape[2])], 1
    )
    grad_query_latent, grad_query_gain_part = norm_back(
        grad_own[:, :query_rank], normal_query, inverse_query, query_gain_full
    )
    grad_latent_norm, grad_latent_gain_part = norm_back(
        grad_own[:, query_rank : query_rank + KV_RANK],
        normal_latent,
        inverse_latent,
        latent_gain_full,
    )
    grad_down_out = jnp.concatenate(
        [
            grad_query_latent,
            grad_latent_norm,
            rotate_back(
                grad_own[:, tail_start + NOPE : tail_start + NOPE + ROPE], cos_table, sin_table
            ),
            jnp.zeros((tokens, padded_width - down_width), F32),
        ],
        -1,
    ).astype(BF16)
    grad_normed = dot("tc,dc->td", grad_down_out, down_full)
    grad_input_norm, grad_attn_gain_part = norm_back(
        grad_normed, normal_one, inverse_one, attn_gain_full
    )
    input_grad = grad_middle + grad_input_norm

    def short_column(grads, own):
        blocks = grads.reshape(devices, own.shape[0])
        return jnp.pad(blocks, ((0, 0), (0, own_rows - own.shape[0]))).reshape(-1)

    gain_columns = jnp.stack(
        [
            grad_attn_gain_part,
            grad_ffn_gain_part,
            short_column(grad_query_gain_part, query_gain),
            short_column(grad_latent_gain_part, latent_gain),
        ],
        1,
    )
    down_sums = dot("td,tc->dc", normed, grad_down_out) + jnp.pad(
        gain_columns, ((0, 0), (down_width, padded_width - down_width - 4))
    )
    down_sums = down_sums.astype(BF16).reshape(dp_count, chips, 2, own_rows, padded_width)
    down_sums = down_sums.transpose(1, 2, 0, 3, 4)
    sum_down, core_done = scatter_seq(
        choose(down_sums, core, 1),
        choose(down_sums, 1 - core + done(group_grads), 1),
    )
    sum_down = scatter_z(sum_down, done(sum_down_rows))
    group_sums = jnp.sum(exchange(hold(group_grads, core_done), "dp").astype(F32), 0)
    group_sums = lax.ppermute(group_sums.astype(BF16), both, to_owner).astype(F32)
    sum_query_up = group_sums[: query_up.shape[1], :query_rank].T
    sum_latent_up = group_sums[: latent_up.shape[1], query_rank:].T
    sum_out = group_sums[up_rows:].reshape(-1, width)
    sum_gains = sum_down[:, down_width : down_width + 4].T
    return (
        layer_output,
        input_grad,
        sum_gains[0],
        sum_down[:, :query_rank],
        sum_gains[2][: query_gain.shape[0]],
        sum_query_up,
        sum_down[:, query_rank:down_width],
        sum_gains[3][: latent_gain.shape[0]],
        sum_latent_up,
        sum_out,
        sum_gains[1],
        sum_gate,
        sum_up,
        sum_down_rows,
    )


def solution(mesh):
    both = ("dp", "seq")
    dp_count = mesh.shape["dp"]

    seq_count = mesh.shape["seq"]
    by_heads = HEADS % seq_count == 0 and seq_count & (seq_count - 1) == 0

    def run(*arrays):
        if by_heads:
            return per_device_heads(dp_count, seq_count, *arrays)
        return per_device_general(dp_count, *arrays)

    in_specs = (
        P(both, None),
        P(both),
        P(both),
        P(both, None),
        P(both),
        P(None, both),
        P(both, None),
        P(both),
        P(None, both),
        P(both, None),
        P(both),
        P(None, both),
        P(None, both),
        P(both, None),
        P(both, None),
    )
    out_specs = (
        P(both, None),
        P(both, None),
        P(both),
        P(both, None),
        P(both),
        P(None, both),
        P(both, None),
        P(both),
        P(None, both),
        P(both, None),
        P(both),
        P(None, both),
        P(None, both),
        P(both, None),
    )
    return jax.shard_map(run, mesh=mesh, in_specs=in_specs, out_specs=out_specs, check_vma=False)
```
